32 devices in a mesh: dp: 4 (over x, core), mp: 8 (over z, y).
Axes of the slice: x: 2, y: 2, z: 4, core: 2. Of those that a mesh axis runs over, the one named last changes fastest.
Arguments:
- stream_in: bfloat16 [32, 256, 2048], P('dp', 'mp'), may hold values from -6 to 6
- cotangent: float32 [32, 256, 2048], P('dp', 'mp'), may hold values from -6 to 6
- noise_table: float32 [32, 6, 2048], replicated, may hold values from -1.2 to 2.9, as said below
- timesteps: int32 [32], P('dp'), may hold values from 0 to 31
- bins: int32 [32], P('dp'), may hold values from 0 to 7
- counts: int32 [4], P('dp'), may hold values from 4 to 8, as said below
- w_qkv: float32 [2048, 3, 2048], P('dp', None, 'mp'), may hold values from -0.11932427 to 0.11932427
- w_out: float32 [2048, 2048], P('mp', 'dp'), may hold values from -0.5 to 0.5
- w_up: float32 [2048, 8192], P('dp', 'mp'), may hold values from -0.13258252 to 0.13258252
- w_down: float32 [8192, 2048], P('mp', 'dp'), may hold values from -0.0625 to 0.0625
- m_qkv: float32 [2048, 3, 2048], P('dp', None, 'mp'), may hold values from -0.00024414062 to 0.00024414062
- m_out: float32 [2048, 2048], P('mp', 'dp'), may hold values from -0.00024414062 to 0.00024414062
- m_up: float32 [2048, 8192], P('dp', 'mp'), may hold values from -0.00024414062 to 0.00024414062
- m_down: float32 [8192, 2048], P('mp', 'dp'), may hold values from -0.00024414062 to 0.00024414062
- v_qkv: float32 [2048, 3, 2048], P('dp', None, 'mp'), may hold values from 1.0450681e-09 to 4.172325e-09
- v_out: float32 [2048, 2048], P('mp', 'dp'), may hold values from 1.0450681e-09 to 4.172325e-09
- v_up: float32 [2048, 8192], P('dp', 'mp'), may hold values from 1.0450681e-09 to 4.172325e-09
- v_down: float32 [8192, 2048], P('mp', 'dp'), may hold values from 1.0450681e-09 to 4.172325e-09
Outputs:
- output: bfloat16 [32, 256, 2048], P('dp', 'mp')
- input_grad: float32 [32, 256, 2048], P('dp', 'mp')
- grad_norm: float32 [], replicated
- new_m_qkv: float32 [2048, 3, 2048], P('dp', None, 'mp')
- new_m_out: float32 [2048, 2048], P('mp', 'dp')
- new_m_up: float32 [2048, 8192], P('dp', 'mp')
- new_m_down: float32 [8192, 2048], P('mp', 'dp')
- new_v_qkv: float32 [2048, 3, 2048], P('dp', None, 'mp')
- new_v_out: float32 [2048, 2048], P('mp', 'dp')
- new_v_up: float32 [2048, 8192], P('dp', 'mp')
- new_v_down: float32 [8192, 2048], P('mp', 'dp')
- new_w_qkv: float32 [2048, 3, 2048], P('dp', None, 'mp')
- new_w_out: float32 [2048, 2048], P('mp', 'dp')
- new_w_up: float32 [2048, 8192], P('dp', 'mp')
- new_w_down: float32 [8192, 2048], P('mp', 'dp')
The draws below stay inside these ranges and needn't reach their ends.
Inputs may be any that keep to these rules, and one draw needn't show every extreme that they name: `counts`: on every index of dp the live images fill its first slots; at least one index of dp has all 8 slots live in every draw. `noise_table`: rows 1, 2, 4, 5 of every timestep are positive.
All inputs are finite; a program needn't handle non-finite values.
Results may differ from the reference program's by a relative error of at most 0.022.
Values may be sent and summed in bfloat16 or wider, within the bound.
No kernel may reach another device: no remote copies, remote signals or barrier semaphores. Data moves between devices by JAX's collectives and lax.ppermute only.
A program may use at most 192 MiB of HBM per device.

```python
import math
import jax
import jax.numpy as jnp
from jax import lax

D = 2048
HEADS = 16
HD = 128
FF = 8192
L = 256
SLOTS = 8
STEPS = 32
BINS = 8
ADAM_STEP = 10
IMAGES = 32
N_DP = 4


def column_ramp(count, start_value, end_value):
    steps_made = jnp.arange(count, dtype=jnp.float32) / max(count - 1, 1)
    return start_value + (end_value - start_value) * steps_made


def draw_noise_table(key, part):
    key = jax.random.fold_in(key, 13)
    subkeys = jax.random.split(key, 2)
    shape = (STEPS, 6, D)
    factor = jnp.exp(jax.random.uniform(subkeys[0], shape, jnp.float32, -0.35, 0.35))
    shifts = jnp.clip(0.3 * jax.random.normal(subkeys[1], shape, jnp.float32), -1.2, 1.2)
    positive = column_ramp(D, 0.6, 1.8) * factor
    is_shift = (jnp.arange(6) % 3 == 0)[None, :, None]
    return jnp.where(is_shift, shifts, positive)


def draw_w_qkv(key, part):
    key = jax.random.fold_in(key, 11)
    shape = (D, 3, HEADS * HD)
    base = jnp.clip(jax.random.normal(key, shape, jnp.float32), -4.0, 4.0)
    return base * column_ramp(HEADS * HD, 0.75, 1.35) * D ** (-0.5)


def draw_w_up(key, part):
    key = jax.random.fold_in(key, 12)
    shape = (D, FF)
    base = jnp.clip(jax.random.normal(key, shape, jnp.float32), -4.0, 4.0)
    return base * column_ramp(FF, 0.5, 1.5) * D ** (-0.5)


def draw_counts(key, part):
    key = jax.random.fold_in(key, 17)
    subkeys = jax.random.split(key, 2)
    devices = IMAGES // SLOTS
    fewest = (SLOTS + 1) // 2
    drawn = jax.random.randint(subkeys[0], (devices,), fewest, SLOTS + 1)
    filled = jax.random.randint(subkeys[1], (), 0, devices)
    return jnp.where(jnp.arange(devices) == filled, SLOTS, drawn).astype(jnp.int32)


def set_ends(result, rng, smallest, largest):
    shape = result.shape
    spot = [jax.random.randint(jax.random.fold_in(rng, axis), (), 0, shape[axis]) for axis in range(len(shape))]
    result = result.at[tuple(spot)].set(smallest)
    longest = shape.index(max(shape))
    spot[longest] = (spot[longest] + 1) % shape[longest]
    return result.at[tuple(spot)].set(largest)


def shard_levels(stream_key, extent, cuts, least, high):
    def one(position, shards_of):
        draws = jax.random.uniform(jax.random.fold_in(jax.random.fold_in(stream_key, 6), position), (shards_of,), jnp.float32, least / len(cuts), high / len(cuts))
        return jnp.repeat(jnp.exp(draws), extent[position] // shards_of).reshape((-1,) + (1,) * (len(extent) - position - 1))

    loudness = one(*cuts[0])
    for cut in cuts[1:]:
        loudness = loudness * one(*cut)
    return loudness


def scatter_about(rng, dims, width, limit, cuts=(), held_as=jnp.bfloat16):
    loudness = shard_levels(rng, dims, cuts, -0.22, 0.18) if cuts else 1.0
    result = jax.random.normal(rng, dims, jnp.float32) * width * loudness
    return jnp.minimum(jnp.maximum(result, -limit), limit).astype(held_as)


def setup_inputs(seed: int = 0) -> dict:
    streams_of = jax.random.split(jax.random.key(seed), 19)
    return {
        "stream_in": scatter_about(streams_of[0], (IMAGES, L, D), 1.0, 6.0, ((0, 4), (1, 8))),
        "cotangent": scatter_about(streams_of[1], (IMAGES, L, D), 1.0, 6.0, ((0, 4), (1, 8)), jnp.float32),
        "noise_table": draw_noise_table(jax.random.fold_in(streams_of[18], 71), 0),
        "timesteps": set_ends(jax.random.randint(streams_of[3], (IMAGES,), 0, STEPS), jax.random.fold_in(streams_of[3], 1), 0, STEPS - 1).astype(jnp.int32),
        "bins": set_ends(jax.random.randint(streams_of[4], (IMAGES,), 0, BINS), jax.random.fold_in(streams_of[4], 1), 0, BINS - 1).astype(jnp.int32),
        "counts": draw_counts(jax.random.fold_in(streams_of[18], 71), 0),
        "w_qkv": draw_w_qkv(jax.random.fold_in(streams_of[18], 71), 0),
        "w_out": scatter_about(streams_of[7], (HEADS * HD, D), (D // 16) ** -0.5, 0.5, ((0, 8), (1, 4)), jnp.float32),
        "w_up": draw_w_up(jax.random.fold_in(streams_of[18], 71), 0),
        "w_down": scatter_about(streams_of[9], (FF, D), FF ** -0.5, 0.0625, ((0, 8), (1, 4)), jnp.float32),
        "m_qkv": scatter_about(streams_of[10], (D, 3, HEADS * HD), (0.111 * (4 * D * D + 2 * D * FF) ** -0.5), 0.00024414062, ((0, 4), (2, 8)), jnp.float32),
        "m_out": scatter_about(streams_of[11], (HEADS * HD, D), (0.111 * (4 * D * D + 2 * D * FF) ** -0.5), 0.00024414062, ((0, 8), (1, 4)), jnp.float32),
        "m_up": scatter_about(streams_of[12], (D, FF), (0.111 * (4 * D * D + 2 * D * FF) ** -0.5), 0.00024414062, ((0, 4), (1, 8)), jnp.float32),
        "m_down": scatter_about(streams_of[13], (FF, D), (0.111 * (4 * D * D + 2 * D * FF) ** -0.5), 0.00024414062, ((0, 8), (1, 4)), jnp.float32),
        "v_qkv": jnp.clip(jnp.exp(math.log(4.172325152040912e-09) - 1.3843914 * jax.random.uniform(streams_of[14], (D, 3, HEADS * HD), jnp.float32) ** shard_levels(streams_of[14], (D, 3, HEADS * HD), ((0, 4), (2, 8)), -0.2, 0.2)), 1.0450681431350972e-09, 4.172325152040912e-09),
        "v_out": jnp.clip(jnp.exp(math.log(4.172325152040912e-09) - 1.3843914 * jax.random.uniform(streams_of[15], (HEADS * HD, D), jnp.float32) ** shard_levels(streams_of[15], (HEADS * HD, D), ((0, 8), (1, 4)), -0.2, 0.2)), 1.0450681431350972e-09, 4.172325152040912e-09),
        "v_up": jnp.clip(jnp.exp(math.log(4.172325152040912e-09) - 1.3843914 * jax.random.uniform(streams_of[16], (D, FF), jnp.float32) ** shard_levels(streams_of[16], (D, FF), ((0, 4), (1, 8)), -0.2, 0.2)), 1.0450681431350972e-09, 4.172325152040912e-09),
        "v_down": jnp.clip(jnp.exp(math.log(4.172325152040912e-09) - 1.3843914 * jax.random.uniform(streams_of[17], (FF, D), jnp.float32) ** shard_levels(streams_of[17], (FF, D), ((0, 8), (1, 4)), -0.2, 0.2)), 1.0450681431350972e-09, 4.172325152040912e-09),
    }


@jax.custom_vjp
def lower_precision(v):
    return lax.optimization_barrier(v.astype(jnp.bfloat16)).astype(jnp.float32)

@jax.custom_vjp
def lower_precision_backward(v):
    return v

def low_keep(v):
    return (lower_precision(v), None)

def low_pass(kept, grad):
    return (grad,)

def back_keep(v):
    return (v, None)

def back_low(kept, grad):
    return (lower_precision(grad),)
lower_precision.defvjp(low_keep, low_pass)
lower_precision_backward.defvjp(back_keep, back_low)
clip_limit = 1.0
beta_one = 0.9
beta_two = 0.95
learn_rate = 0.02
output_rate = 0.08
adam_epsilon = 1e-08
decay_rate = 0.01

def norm_rows(values):
    center = values - lax.optimization_barrier(jnp.mean(values, axis=-1, keepdims=True))
    spread = lax.optimization_barrier(jnp.mean(center * center, axis=-1, keepdims=True))
    return center * lax.rsqrt(spread + 1e-06)

def gelu_tanh(values):
    return jax.nn.gelu(values, approximate=True)

def block(stream, modulation, query_key_value_weight, output_weight, up_weight, down_weight):
    highest_precision = lax.Precision.HIGHEST
    slot_count, length = (stream.shape[0], stream.shape[1])
    attention_input = lower_precision(norm_rows(stream) * modulation[:, 1:2] + modulation[:, 0:1])
    projection_output = lower_precision_backward(lower_precision(jnp.einsum('ojb,bth->ojth', attention_input, lower_precision(query_key_value_weight), precision=highest_precision)))
    queries = projection_output[:, :, 0].reshape(slot_count, length, HEADS, HD)
    keys_all = projection_output[:, :, 1].reshape(slot_count, length, HEADS, HD)
    values_all = projection_output[:, :, 2].reshape(slot_count, length, HEADS, HD)
    scores = lower_precision_backward(jnp.einsum('sqhe,skhe->shqk', queries, keys_all, precision=highest_precision) * HD ** (-0.5))
    attn_probs = jax.nn.softmax(scores, axis=-1)
    attention_result = lower_precision_backward(lower_precision(jnp.einsum('shqk,skhe->sqhe', lower_precision(attn_probs), values_all, precision=highest_precision)))
    attention_result = attention_result.reshape(slot_count, length, HEADS * HD)
    attention_partial_sum = lower_precision_backward(jnp.einsum('ybo,oh->ybh', attention_result, lower_precision(output_weight), precision=highest_precision))
    residual = stream + modulation[:, 2:3] * attention_partial_sum
    perceptron_input = lower_precision(norm_rows(residual) * modulation[:, 4:5] + modulation[:, 3:4])
    expanded_preactivation = lower_precision_backward(jnp.einsum('bno,oj->bnj', perceptron_input, lower_precision(up_weight), precision=highest_precision))
    hidden_state = lower_precision(gelu_tanh(expanded_preactivation))
    perceptron_partial_sum = lower_precision_backward(jnp.einsum('ybo,oh->ybh', hidden_state, lower_precision(down_weight), precision=highest_precision))
    return residual + modulation[:, 5:6] * perceptron_partial_sum

def adam_update(gradient, moment_one, moment_two, weight, factor, step_rate):
    clipped = gradient * factor
    new_one = beta_one * moment_one + (1.0 - beta_one) * clipped
    new_two = beta_two * moment_two + (1.0 - beta_two) * clipped * clipped
    corrected = new_one / (1.0 - beta_one ** ADAM_STEP)
    root_two = jnp.sqrt(new_two / (1.0 - beta_two ** ADAM_STEP))
    new_weight = weight - step_rate * (corrected / (root_two + adam_epsilon) + decay_rate * weight)
    return (new_one, new_two, new_weight)

def reference(stream_in, cotangent, noise_table, timesteps, bins, counts, w_qkv, w_out, w_up, w_down, m_qkv, m_out, m_up, m_down, v_qkv, v_out, v_up, v_down):
    modulation = noise_table[timesteps]
    image_ids = jnp.arange(IMAGES)
    live = (image_ids % SLOTS < counts[image_ids // SLOTS]).astype(jnp.float32)
    loss_scale = live * (bins.astype(jnp.float32) + 1.0) / BINS
    stream = stream_in.astype(jnp.float32).reshape(N_DP, SLOTS, L, D)
    mods_grouped = modulation.reshape(N_DP, SLOTS, 6, D)
    seeds = (cotangent * loss_scale[:, None, None]).reshape(N_DP, SLOTS, L, D)

    def per_group(carry, items):
        rows, mods_here, seed_here = items

        def local_block(inputs, query_key_value_weight, output_weight, up_weight, down_weight):
            return block(inputs, mods_here, query_key_value_weight, output_weight, up_weight, down_weight)
        outputs, pullback = jax.vjp(local_block, rows, w_qkv, w_out, w_up, w_down)
        grads = pullback(seed_here)
        carry = tuple((summed + addend for summed, addend in zip(carry, grads[1:])))
        return (carry, (outputs.astype(jnp.bfloat16), grads[0]))
    initial = (jnp.zeros_like(w_qkv), jnp.zeros_like(w_out), jnp.zeros_like(w_up), jnp.zeros_like(w_down))
    grads, (outputs, input_grads) = lax.scan(per_group, initial, (stream, mods_grouped, seeds))
    output = outputs.reshape(IMAGES, L, D)
    input_grad = input_grads.reshape(IMAGES, L, D)
    squares = jnp.sum(grads[0] * grads[0]) + jnp.sum(grads[1] * grads[1]) + jnp.sum(grads[2] * grads[2]) + jnp.sum(grads[3] * grads[3])
    grad_norm = jnp.sqrt(squares)
    factor = jnp.minimum(1.0, clip_limit / (grad_norm + 1e-06))
    one_qkv, two_qkv, new_qkv = adam_update(grads[0], m_qkv, v_qkv, w_qkv, factor, learn_rate)
    one_out, two_out, new_out = adam_update(grads[1], m_out, v_out, w_out, factor, output_rate)
    one_up, two_up, new_up = adam_update(grads[2], m_up, v_up, w_up, factor, learn_rate)
    one_down, two_down, new_down = adam_update(grads[3], m_down, v_down, w_down, factor, learn_rate)
    return (output, input_grad, grad_norm, one_qkv, one_out, one_up, one_down, two_qkv, two_out, two_up, two_down, new_qkv, new_out, new_up, new_down)
```

```python
import jax
import jax.numpy as jnp
from jax import lax
from jax.sharding import PartitionSpec as P

HD = 128
BINS = 8
ADAM_STEP = 10

clip_limit = 1.0
beta_one = 0.9
beta_two = 0.95
learn_rate = 0.02
output_rate = 0.08
adam_epsilon = 1e-08
decay_rate = 0.01

BF = jnp.bfloat16
F32 = jnp.float32


def norm_rows(values):
    center = values - jnp.mean(values, axis=-1, keepdims=True)
    spread = jnp.mean(center * center, axis=-1, keepdims=True)
    return center * lax.rsqrt(spread + 1e-06)


def gelu_tanh(values):
    return jax.nn.gelu(values, approximate=True)


def adam_update(gradient, moment_one, moment_two, weight, factor, step_rate):
    clipped = gradient * factor
    new_one = beta_one * moment_one + (1.0 - beta_one) * clipped
    new_two = beta_two * moment_two + (1.0 - beta_two) * clipped * clipped
    corrected = new_one / (1.0 - beta_one**ADAM_STEP)
    root_two = jnp.sqrt(new_two / (1.0 - beta_two**ADAM_STEP))
    new_weight = weight - step_rate * (corrected / (root_two + adam_epsilon) + decay_rate * weight)
    return (new_one, new_two, new_weight)


def after(value, *earlier):
    return lax.optimization_barrier((value, *earlier))[0]


def matmul(a, b, contract):
    return lax.dot_general(a, b, (contract, ((), ())), preferred_element_type=F32)


class Links:
    def __init__(self, n_dp, n_mp):
        self.X, self.H = n_dp // 2, n_mp // 4
        self.n_dp, self.n_mp = n_dp, n_mp

    def from_dp(self, v, jx, jc):
        pairs = []
        for dst in range(self.n_dp):
            x, c = divmod(dst, 2)
            pairs.append((((x + jx) % self.X) * 2 + (c ^ jc), dst))
        return lax.ppermute(v, "dp", pairs)

    def from_mp(self, v, jh, jp, jq):
        pairs = []
        for dst in range(self.n_mp):
            h, p, q = dst // 4, (dst // 2) % 2, dst % 2
            pairs.append((((h + jh) % self.H) * 4 + (p ^ jp) * 2 + (q ^ jq), dst))
        return lax.ppermute(v, "mp", pairs)

    def gather_blocks(self, w, h_dim, d_dim):
        pieces = {(0, 0, 0): w}
        for jh in range(1, self.H):
            pieces[jh, 0, 0] = self.from_mp(w, jh, 0, 0)
        for jh in range(self.H):
            for jx in range(1, self.X):
                pieces[jh, jx, 0] = self.from_dp(pieces[jh, 0, 0], jx, 0)
        for jh in range(self.H):
            for jx in range(self.X):
                pieces[jh, jx, 1] = self.from_dp(pieces[jh, jx, 0], 0, 1)
        return jnp.concatenate(
            [
                jnp.concatenate(
                    [pieces[jh, jx, jc] for jc in range(2) for jx in range(self.X)], axis=d_dim
                )
                for jh in range(self.H)
            ],
            axis=h_dim,
        )

    def reduce_blocks(self, g, h_dim, d_dim):
        half = g.shape[d_dim] // 2
        keep = lax.slice_in_dim(g, 0, half, axis=d_dim)
        sent = self.from_dp(lax.slice_in_dim(g, half, 2 * half, axis=d_dim), 0, 1)
        g = (keep.astype(F32) + sent.astype(F32)).astype(BF)
        width = half // self.X
        total = lax.slice_in_dim(g, 0, width, axis=d_dim).astype(F32)
        for jx in range(1, self.X):
            block = lax.slice_in_dim(g, jx * width, (jx + 1) * width, axis=d_dim)
            total = total + self.from_dp(block, -jx, 0).astype(F32)
        g = total.astype(BF)
        width = g.shape[h_dim] // self.H
        total = lax.slice_in_dim(g, 0, width, axis=h_dim).astype(F32)
        for jh in range(1, self.H):
            block = lax.slice_in_dim(g, jh * width, (jh + 1) * width, axis=h_dim)
            total = total + self.from_mp(block, -jh, 0, 0).astype(F32)
        return total

    def to_group(self, v):
        here = lax.axis_index("mp") // 4
        images = v.shape[0] // self.H
        parts = []
        for jh in range(self.H):
            chosen = lax.dynamic_slice_in_dim(v, ((here - jh) % self.H) * images, images, axis=0)
            parts.append(chosen if jh == 0 else self.from_mp(chosen, jh, 0, 0))
        return jnp.concatenate(parts, axis=1)

    def to_home(self, v):
        here = lax.axis_index("mp") // 4
        images = v.shape[0]
        tokens = v.shape[1] // self.H
        out = jnp.zeros((images * self.H, tokens, v.shape[2]), v.dtype)
        for jh in range(self.H):
            part = v[:, jh * tokens : (jh + 1) * tokens]
            part = part if jh == 0 else self.from_mp(part, -jh, 0, 0)
            out = lax.dynamic_update_slice_in_dim(
                out, part, ((here - jh) % self.H) * images, axis=0
            )
        return out

    def gather_tokens(self, v):
        half = v.shape[0] // 2
        a, b = v[:half], v[half:]
        pa, qb = self.from_mp(a, 0, 1, 0), self.from_mp(b, 0, 0, 1)
        qa, pb = self.from_mp(a, 0, 0, 1), self.from_mp(b, 0, 1, 0)
        da, db = self.from_mp(pa, 0, 0, 1), self.from_mp(qb, 0, 1, 0)
        return jnp.concatenate(
            [
                jnp.concatenate([a, qa, pa, da], axis=1),
                jnp.concatenate([b, qb, pb, db], axis=1),
            ],
            axis=0,
        )

    def reduce_tokens(self, v):
        images, length, width = v.shape
        half, t = images // 2, length // 4
        v = v.reshape(images, 2, 2, t, width)
        a, b = v[:half], v[half:]
        ra = self.from_mp(a[:, :, 1], 0, 0, 1)
        rb = self.from_mp(b[:, 1], 0, 1, 0)
        sa = (a[:, :, 0].astype(F32) + ra.astype(F32)).astype(BF)
        sb = (b[:, 0].astype(F32) + rb.astype(F32)).astype(BF)
        ta = self.from_mp(sa[:, 1], 0, 1, 0)
        tb = self.from_mp(sb[:, 1], 0, 0, 1)
        return jnp.concatenate(
            [
                sa[:, 0].astype(F32) + ta.astype(F32),
                sb[:, 0].astype(F32) + tb.astype(F32),
            ],
            axis=0,
        )

    def features_here(self, v):
        d = lax.axis_index("dp")
        x, c = d // 2, d % 2
        width = v.shape[-1] // self.n_dp
        return jnp.concatenate(
            [
                lax.dynamic_slice_in_dim(
                    v, (((x + jx) % self.X) * 2 + (c ^ jc)) * width, width, axis=v.ndim - 1
                )
                for jc in range(2)
                for jx in range(self.X)
            ],
            axis=-1,
        )

    def features_home(self, v):
        d = lax.axis_index("dp")
        x, c = d // 2, d % 2
        width = v.shape[-1] // self.n_dp
        return jnp.concatenate(
            [
                lax.dynamic_slice_in_dim(
                    v,
                    (((e % 2) ^ c) * self.X + (e // 2 - x) % self.X) * width,
                    width,
                    axis=v.ndim - 1,
                )
                for e in range(self.n_dp)
            ],
            axis=-1,
        )

    def total(self, v):
        step = 1
        while step < self.n_dp:
            v = v + lax.ppermute(v, "dp", [(i ^ step, i) for i in range(self.n_dp)])
            step *= 2
        step = 1
        while step < self.n_mp:
            v = v + lax.ppermute(v, "mp", [(i ^ step, i) for i in range(self.n_mp)])
            step *= 2
        return v


def per_device(
    links,
    stream_in,
    cotangent,
    noise_table,
    timesteps,
    bins,
    counts,
    w_qkv,
    w_out,
    w_up,
    w_down,
    m_qkv,
    m_out,
    m_up,
    m_down,
    v_qkv,
    v_out,
    v_up,
    v_down,
):
    H = links.H
    slots, _, D = stream_in.shape
    images = slots // H
    here = lax.axis_index("mp") // 4

    steps_here = lax.dynamic_slice_in_dim(timesteps, here * images, images)
    table_rows = noise_table.shape[0]
    picks = (steps_here[:, None] == jnp.arange(table_rows)[None, :]).astype(F32)
    modulation = jnp.dot(
        picks, noise_table.reshape(table_rows, -1), precision=lax.Precision.HIGHEST
    ).reshape(images, 6, D)
    modulation = links.features_here(modulation)
    shift_a, scale_a, gate_a, shift_f, scale_f, gate_f = (modulation[:, i : i + 1] for i in range(6))

    stream = links.to_group(links.features_here(stream_in)).astype(F32)

    block = w_qkv.shape[2]
    wq = links.gather_blocks(w_qkv.astype(BF).reshape(w_qkv.shape[0], 3 * block), 1, 0)
    wo = links.gather_blocks(w_out.astype(BF), 0, 1)
    wu = links.gather_blocks(w_up.astype(BF), 1, 0)
    wd = links.gather_blocks(w_down.astype(BF), 0, 1)

    live = jnp.arange(slots) < counts[0]
    loss_scale = live.astype(F32) * (bins.astype(F32) + 1.0) / BINS
    loss_scale = lax.dynamic_slice_in_dim(loss_scale, here * images, images)
    cot = links.to_group(links.features_here(cotangent.astype(BF))).astype(F32)
    dy = cot * loss_scale[:, None, None]

    def first_norm(rows):
        return norm_rows(rows) * scale_a + shift_a

    def second_norm(rows):
        return norm_rows(rows) * scale_f + shift_f

    a_rows = links.gather_tokens(first_norm(stream).astype(BF))
    length = a_rows.shape[1]
    rows = images * length
    a_rows = a_rows.reshape(rows, D)
    heads = H * block // HD
    qkv = matmul(a_rows, wq, ((1,), (0,))).astype(BF)
    qkv = qkv.reshape(images, length, H, 3, block)
    q = qkv[:, :, :, 0].reshape(images, length, heads, HD)
    k = qkv[:, :, :, 1].reshape(images, length, heads, HD)
    v = qkv[:, :, :, 2].reshape(images, length, heads, HD)
    scores = jnp.einsum("sqhe,skhe->shqk", q, k, preferred_element_type=F32) * HD ** (-0.5)
    top = jnp.max(scores, axis=-1, keepdims=True)
    lse = top + jnp.log(jnp.sum(jnp.exp(scores - top), axis=-1, keepdims=True))
    probs = jnp.exp(scores - lse)
    o = jnp.einsum("shqk,skhe->sqhe", probs.astype(BF), v, preferred_element_type=F32).astype(BF)
    o = o.reshape(rows, heads * HD)
    att = links.reduce_tokens(
        matmul(o, wo, ((1,), (0,))).astype(BF).reshape(images, length, D)
    )
    residual = stream + gate_a * att
    b_rows = links.gather_tokens(second_norm(residual).astype(BF)).reshape(rows, D)
    u = matmul(b_rows, wu, ((1,), (0,)))
    hidden = gelu_tanh(u).astype(BF)
    ff = links.reduce_tokens(
        matmul(hidden, wd, ((1,), (0,))).astype(BF).reshape(images, length, D)
    )
    output = links.features_home(links.to_home((residual + gate_f * ff).astype(BF)))

    df_rows = links.gather_tokens((gate_f * dy).astype(BF)).reshape(rows, D)
    g_down = matmul(hidden, df_rows, ((0,), (0,))).astype(BF)
    d_hidden = matmul(df_rows, wd, ((1,), (1,)))
    du = jax.vjp(gelu_tanh, u)[1](d_hidden)[0].astype(BF)
    g_up = matmul(b_rows, du, ((0,), (0,))).astype(BF)
    db = links.reduce_tokens(
        matmul(du, wu, ((1,), (1,))).astype(BF).reshape(images, length, D)
    )
    dr = dy + jax.vjp(second_norm, residual)[1](db)[0]
    datt = links.gather_tokens((gate_a * dr).astype(BF)).reshape(rows, D)
    g_out = matmul(o, datt, ((0,), (0,))).astype(BF)
    do = matmul(datt, wo, ((1,), (1,))).astype(BF).reshape(images, length, heads, HD)
    dv = jnp.einsum("shqk,sqhe->skhe", probs.astype(BF), do, preferred_element_type=F32)
    dp = jnp.einsum("sqhe,skhe->shqk", do, v, preferred_element_type=F32)
    ds = (probs * (dp - jnp.sum(probs * dp, axis=-1, keepdims=True))).astype(BF)
    dq = jnp.einsum("shqk,skhe->sqhe", ds, k, preferred_element_type=F32) * HD ** (-0.5)
    dk = jnp.einsum("shqk,sqhe->skhe", ds, q, preferred_element_type=F32) * HD ** (-0.5)
    dqkv = jnp.stack(
        [t.astype(BF).reshape(images, length, H, block) for t in (dq, dk, dv)], axis=3
    ).reshape(rows, H * 3 * block)
    g_qkv = matmul(a_rows, dqkv, ((0,), (0,))).astype(BF)
    da = links.reduce_tokens(
        matmul(dqkv, wq, ((1,), (1,))).astype(BF).reshape(images, length, D)
    )
    d_stream = dr + jax.vjp(first_norm, stream)[1](da)[0]
    input_grad = links.features_home(links.to_home(d_stream.astype(BF))).astype(F32)

    g_down = links.reduce_blocks(g_down, 0, 1)
    g_up = links.reduce_blocks(g_up, 1, 0)
    g_out = links.reduce_blocks(g_out, 0, 1)
    g_qkv = links.reduce_blocks(g_qkv, 1, 0).reshape(w_qkv.shape)
    squares = (
        jnp.sum(g_qkv * g_qkv)
        + jnp.sum(g_out * g_out)
        + jnp.sum(g_up * g_up)
        + jnp.sum(g_down * g_down)
    )
    grad_norm = jnp.sqrt(links.total(squares))
    factor = jnp.minimum(1.0, clip_limit / (grad_norm + 1e-06))
    one_qkv, two_qkv, new_qkv = adam_update(g_qkv, m_qkv, v_qkv, w_qkv, factor, learn_rate)
    one_out, two_out, new_out = adam_update(g_out, m_out, v_out, w_out, factor, output_rate)
    one_up, two_up, new_up = adam_update(g_up, m_up, v_up, w_up, factor, learn_rate)
    one_down, two_down, new_down = adam_update(g_down, m_down, v_down, w_down, factor, learn_rate)
    return (
        output,
        input_grad,
        grad_norm,
        one_qkv,
        one_out,
        one_up,
        one_down,
        two_qkv,
        two_out,
        two_up,
        two_down,
        new_qkv,
        new_out,
        new_up,
        new_down,
    )


def solution(mesh):
    links = Links(mesh.shape["dp"], mesh.shape["mp"])
    tokens, qkv = P("dp", "mp", None), P("dp", None, "mp")
    rows, columns = P("mp", "dp"), P("dp", "mp")
    weights = (qkv, rows, columns, rows)
    return jax.shard_map(
        lambda *args: per_device(links, *args),
        mesh=mesh,
        in_specs=(tokens, tokens, P(), P("dp"), P("dp"), P("dp")) + 3 * weights,
        out_specs=(tokens, tokens, P()) + 3 * weights,
        check_vma=False,
    )
```

```python
import jax
import jax.numpy as jnp
from jax import lax
from jax.experimental import pallas as pl
from jax.experimental.pallas import tpu as pltpu
from jax.sharding import Mesh
from jax.sharding import PartitionSpec as P

HD = 128
BINS = 8
ADAM_STEP = 10

clip_limit = 1.0
beta_one = 0.9
beta_two = 0.95
learn_rate = 0.02
output_rate = 0.08
adam_epsilon = 1e-08
decay_rate = 0.01

BF = jnp.bfloat16
F32 = jnp.float32


def norm_rows(values):
    center = values - jnp.mean(values, axis=-1, keepdims=True)
    spread = jnp.mean(center * center, axis=-1, keepdims=True)
    return center * lax.rsqrt(spread + 1e-06)


def gelu_tanh(values):
    return jax.nn.gelu(values, approximate=True)


def adam_update(gradient, moment_one, moment_two, weight, factor, step_rate):
    clipped = gradient * factor
    new_one = beta_one * moment_one + (1.0 - beta_one) * clipped
    new_two = beta_two * moment_two + (1.0 - beta_two) * clipped * clipped
    corrected = new_one / (1.0 - beta_one**ADAM_STEP)
    root_two = jnp.sqrt(new_two / (1.0 - beta_two**ADAM_STEP))
    new_weight = weight - step_rate * (corrected / (root_two + adam_epsilon) + decay_rate * weight)
    return (new_one, new_two, new_weight)


def sync(*values):
    return lax.optimization_barrier(values)


def dot(a, b, contract=(1, 0)):
    return lax.dot_general(
        a, b, (((contract[0],), (contract[1],)), ((), ())), preferred_element_type=F32
    )


def rows_of(ref, columns=slice(None)):
    value = ref[0, :, :, columns]
    return value.reshape(value.shape[0] * value.shape[1], value.shape[2])


def join_tokens(pieces, whole):
    for kind, two in enumerate(pieces):
        for r, ref in enumerate(two):
            t = ref.shape[1]
            whole[0, kind, r * t : (r + 1) * t] = ref[0]


def put_parts(value, columns, parts):
    half = value.shape[0] // (2 * len(parts))
    for kind, (keep, send) in enumerate(parts):
        keep[0, :, columns] = value[2 * kind * half : (2 * kind + 1) * half]
        send[0, :, columns] = value[(2 * kind + 1) * half : (2 * kind + 2) * half]


def softmax_rows(q, k):
    scores = dot(q, k, (1, 1)) * HD ** (-0.5)
    weights = jnp.exp(scores - jnp.max(scores, axis=-1, keepdims=True))
    return weights / jnp.sum(weights, axis=-1, keepdims=True)


def head_columns(jh, part, n, block):
    start = (jh * 3 + part) * block + n * HD
    return slice(start, start + HD)


class Pieces:
    def __init__(self, refs):
        self.refs, self.at = refs, 0

    def take(self, count):
        self.at += count
        return self.refs[self.at - count : self.at]

    def tokens(self):
        near_far = self.take(4)
        return near_far[:2], near_far[2:]

    def parts(self):
        a, b, c, d = self.take(4)
        return (a, b), (c, d)


class Separate:
    def __init__(self, refs, nd):
        self.refs, self.depth = refs, refs[0].shape[0]
        self.shape = refs[0].shape[1:]

    def block(self, jh, d, rows=slice(None), columns=slice(None)):
        core, x = divmod(d, self.depth)
        return self.refs[2 * jh + core][x, rows, columns]


def attention_kernel(nh, nd, gates, *refs):
    refs = Pieces(refs)
    tokens, weights = refs.tokens(), Separate(refs.take(2 * nh), nd)
    refs.take(gates)
    (a, qkv, o), parts = refs.take(3), refs.parts()
    join_tokens(tokens, a)
    depth, block = weights.shape[0], weights.shape[1] // 4
    width = 3 * block
    inward = (slice(None), slice(0, width))
    outward = (slice(None), slice(width, width + block))
    kinds, length = a.shape[1], a.shape[2]
    for jh in range(nh):
        total = dot(rows_of(a, slice(0, depth)), weights.block(jh, 0, *inward))
        for d in range(1, nd):
            total += dot(rows_of(a, slice(d * depth, (d + 1) * depth)), weights.block(jh, d, *inward))
        qkv[0, :, :, jh * width : (jh + 1) * width] = total.astype(BF).reshape(kinds, length, width)
    for kind in range(kinds):
        for jh in range(nh):
            for n in range(block // HD):
                q, k, v = (qkv[0, kind, :, head_columns(jh, i, n, block)] for i in range(3))
                out = dot(softmax_rows(q, k).astype(BF), v).astype(BF)
                o[0, kind, :, jh * block + n * HD : jh * block + (n + 1) * HD] = out
    for d in range(nd):
        total = dot(rows_of(o, slice(0, block)), weights.block(0, d, *outward), (1, 1))
        for jh in range(1, nh):
            total += dot(rows_of(o, slice(jh * block, (jh + 1) * block)), weights.block(jh, d, *outward), (1, 1))
        put_parts(total.astype(BF), slice(d * depth, (d + 1) * depth), parts)


def mlp_kernel(nh, nd, gates, *refs):
    refs = Pieces(refs)
    b_tokens, df_tokens = refs.tokens(), refs.tokens()
    wu, wd = (Separate(refs.take(2 * nh), nd) for _ in range(2))
    refs.take(gates)
    (b, df, hidden, du), parts = refs.take(4), refs.parts()
    join_tokens(b_tokens, b)
    join_tokens(df_tokens, df)
    depth, width = wu.shape
    kinds, length = b.shape[1], b.shape[2]
    chunk = min(width, 512)
    curve, cubic = 0.7978845608028654, 0.044715
    for jh in range(nh):
        for c in range(0, width, chunk):
            part = slice(c, c + chunk)
            u = dot(rows_of(b, slice(0, depth)), wu.block(jh, 0, columns=part))
            dh = dot(rows_of(df, slice(0, depth)), wd.block(jh, 0, part), (1, 1))
            for d in range(1, nd):
                cols = slice(d * depth, (d + 1) * depth)
                u += dot(rows_of(b, cols), wu.block(jh, d, columns=part))
                dh += dot(rows_of(df, cols), wd.block(jh, d, part), (1, 1))
            square = u * u
            t = jnp.tanh(curve * u * (1.0 + cubic * square))
            near = 0.5 * (1.0 + t)
            slope = near + 0.5 * u * (1.0 - t * t) * (curve * (1.0 + 3.0 * cubic * square))
            cols = slice(jh * width + c, jh * width + c + chunk)
            hidden[0, :, :, cols] = (u * near).astype(BF).reshape(kinds, length, chunk)
            du[0, :, :, cols] = (dh * slope).astype(BF).reshape(kinds, length, chunk)
    for d in range(nd):
        total = dot(rows_of(du, slice(0, width)), wu.block(0, d), (1, 1))
        for jh in range(1, nh):
            total += dot(rows_of(du, slice(jh * width, (jh + 1) * width)), wu.block(jh, d), (1, 1))
        put_parts(total.astype(BF), slice(d * depth, (d + 1) * depth), parts)


def down_kernel(nh, nd, gates, *refs):
    refs = Pieces(refs)
    (hidden,), wd = refs.take(1), Separate(refs.take(2 * nh), nd)
    refs.take(gates)
    parts = refs.parts()
    width, depth = wd.shape
    for d in range(nd):
        total = dot(rows_of(hidden, slice(0, width)), wd.block(0, d))
        for jh in range(1, nh):
            total += dot(rows_of(hidden, slice(jh * width, (jh + 1) * width)), wd.block(jh, d))
        put_parts(total.astype(BF), slice(d * depth, (d + 1) * depth), parts)


def attention_back_kernel(nh, nd, gates, *refs):
    refs = Pieces(refs)
    tokens, (qkv,) = refs.tokens(), refs.take(1)
    weights = Separate(refs.take(2 * nh), nd)
    refs.take(gates)
    (datt, dqkv), parts = refs.take(2), refs.parts()
    join_tokens(tokens, datt)
    depth, block = weights.shape[0], weights.shape[1] // 4
    width = 3 * block
    inward = (slice(None), slice(0, width))
    outward = (slice(None), slice(width, width + block))
    kinds, length = datt.shape[1], datt.shape[2]
    for jh in range(nh):
        do_all = dot(rows_of(datt, slice(0, depth)), weights.block(jh, 0, *outward))
        for d in range(1, nd):
            do_all += dot(rows_of(datt, slice(d * depth, (d + 1) * depth)), weights.block(jh, d, *outward))
        do_all = do_all.astype(BF)
        for kind in range(kinds):
            for n in range(block // HD):
                q, k, v = (qkv[0, kind, :, head_columns(jh, i, n, block)] for i in range(3))
                do = do_all[kind * length : (kind + 1) * length, n * HD : (n + 1) * HD]
                p = softmax_rows(q, k)
                dv = dot(p.astype(BF), do, (0, 0))
                dp = dot(do, v, (1, 1))
                ds = (p * (dp - jnp.sum(p * dp, axis=-1, keepdims=True))).astype(BF)
                dq = dot(ds, k) * HD ** (-0.5)
                dk = dot(ds, q, (0, 0)) * HD ** (-0.5)
                for i, value in enumerate((dq, dk, dv)):
                    dqkv[0, kind, :, head_columns(jh, i, n, block)] = value.astype(BF)
    for d in range(nd):
        total = dot(rows_of(dqkv, slice(0, width)), weights.block(0, d, *inward), (1, 1))
        for jh in range(1, nh):
            total += dot(rows_of(dqkv, slice(jh * width, (jh + 1) * width)), weights.block(jh, d, *inward), (1, 1))
        put_parts(total.astype(BF), slice(d * depth, (d + 1) * depth), parts)


def group_call(kernel, name, nh, nd, steps, blocked, whole, gates, outs):
    def cut(shape):
        zeros = (0,) * (len(shape) - 1)
        return pl.BlockSpec((1,) + tuple(shape[1:]), lambda i: (i,) + zeros)

    return pl.pallas_call(
        lambda *refs: kernel(nh, nd, len(gates), *refs),
        name=name,
        grid=(steps,),
        in_specs=[cut(v.shape) for v in blocked]
        + [pl.BlockSpec(memory_space=pltpu.VMEM)] * len(whole)
        + [pl.BlockSpec(memory_space=pl.ANY)] * len(gates),
        out_specs=[cut(s) for s in outs],
        out_shape=[jax.ShapeDtypeStruct(s, BF) for s in outs],
        compiler_params=pltpu.CompilerParams(vmem_limit_bytes=60 * 2**20),
        cost_estimate=pl.CostEstimate(flops=0, bytes_accessed=0, transcendentals=0),
    )(*blocked, *whole, *gates)


def pack_attention_weights(w_qkv, w_out):
    depth, _, block = w_qkv.shape

    def kernel(inward, outward, packed):
        for i in range(3):
            packed[:, i * block : (i + 1) * block] = inward[i].astype(BF)
        packed[:, 3 * block :] = outward[...].T.astype(BF)

    return pl.pallas_call(
        kernel,
        name="pack",
        out_shape=jax.ShapeDtypeStruct((depth, 4 * block), BF),
        compiler_params=pltpu.CompilerParams(vmem_limit_bytes=32 * 2**20),
    )(w_qkv.transpose(1, 0, 2), w_out)


def gradient(name, nh, nd, left, right, left_is_hidden, core):
    rows = left.shape[0]
    hidden, features = (left, right) if left_is_hidden else (right, left)
    h_width, d_width, half = hidden.shape[1] // nh, features.shape[1] // nd, nd // 2

    def kernel(left, right, out):
        out[...] = dot(left[...], right[...], (0, 0)).astype(BF)

    h_spec = pl.BlockSpec((rows, h_width), lambda jh, d: (0, jh))
    d_spec = pl.BlockSpec((rows, d_width), lambda jh, d: (0, core * half + d))
    if left_is_hidden:
        in_specs, out_spec = [h_spec, d_spec], pl.BlockSpec((h_width, d_width), lambda jh, d: (jh, d))
        shape = (nh * h_width, half * d_width)
    else:
        in_specs, out_spec = [d_spec, h_spec], pl.BlockSpec((d_width, h_width), lambda jh, d: (d, jh))
        shape = (half * d_width, nh * h_width)
    return pl.pallas_call(
        kernel,
        name=name,
        grid=(nh, half),
        in_specs=in_specs,
        out_specs=out_spec,
        out_shape=jax.ShapeDtypeStruct(shape, BF),
        compiler_params=pltpu.CompilerParams(vmem_limit_bytes=48 * 2**20),
        cost_estimate=pl.CostEstimate(flops=0, bytes_accessed=0, transcendentals=0),
    )(left, right)


class Links:
    everywhere = ("x", "core", "h")

    def __init__(self, n_dp, n_mp):
        self.X, self.H = n_dp // 2, n_mp // 4
        self.n_dp, self.n_mp = n_dp, n_mp

    def shifted(self, v, axis, size, offset, name):
        with jax.named_scope(f"{name}_{axis}"):
            return lax.ppermute(v, axis, [((dst + offset) % size, dst) for dst in range(size)])

    def from_core(self, v, name):
        return self.shifted(v, "core", 2, 1, name)

    def from_x(self, v, jx, name):
        return self.shifted(v, "x", self.X, jx, name)

    def from_h(self, v, jh, name):
        return self.shifted(v, "h", self.H, jh, name)

    def over_h(self, w, name):
        return [self.from_h(w, jh, name) for jh in range(1, self.H)]

    def over_x(self, w, name):
        return [self.from_x(w, jx, name) for jx in range(1, self.X)]

    def part(self, g, d, h, jx, far):
        width = g.shape[d] // self.X
        g = lax.slice_in_dim(g, jx * width, (jx + 1) * width, axis=d)
        width = g.shape[h] // self.H
        return lax.slice_in_dim(g, width if far else 0, g.shape[h] if far else width, axis=h)

    def send_x(self, g, d, h, far, name):
        return [self.from_x(self.part(g, d, h, jx, far), -jx, name) for jx in range(1, self.X)]

    def sum_x(self, g, d, h, far, received):
        return self.part(g, d, h, 0, far).astype(F32) + sum(v.astype(F32) for v in received)

    def send_h(self, g, h, name, rows=None):
        width = g.shape[h] // (self.H - 1)
        received = []
        for jh in range(1, self.H):
            block = lax.slice_in_dim(g, (jh - 1) * width, jh * width, axis=h)
            if rows is not None:
                size = block.shape[0] // 2
                block = block[rows * size : (rows + 1) * size]
            received.append(self.from_h(block, -jh, name))
        return received

    def for_groups(self, v):
        here = lax.axis_index("h")
        images = v.shape[0] // self.H
        return [
            lax.dynamic_slice_in_dim(v, ((here - jh) % self.H) * images, images, axis=0)
            for jh in range(self.H)
        ]

    def to_group(self, parts, name):
        return [self.from_h(parts[jh], jh, name) for jh in range(1, self.H)]

    def leave_group(self, v, name):
        tokens = v.shape[1] // self.H
        return [
            self.from_h(v[:, jh * tokens : (jh + 1) * tokens], -jh, name) for jh in range(1, self.H)
        ]

    def at_home(self, v, received):
        here = lax.axis_index("h")
        images = v.shape[0]
        tokens = v.shape[1] // self.H
        out = jnp.zeros((images * self.H, tokens, v.shape[2]), v.dtype)
        for jh, part in enumerate([v[:, :tokens], *received]):
            out = lax.dynamic_update_slice_in_dim(
                out, part, ((here - jh) % self.H) * images, axis=0
            )
        return self.features_home(out)

    def over(self, v, kind, late, name):
        return self.shifted(v, "p" if (kind == 0) != late else "q", 2, 1, f"{name}{kind}")

    def first_hop(self, v, name):
        half = v.shape[0] // 2
        own = [v[k * half : (k + 1) * half] for k in range(2)]
        return [(own[k], self.over(own[k], k, False, name)) for k in range(2)]

    def near(self, hops):
        return [jnp.concatenate(pair, axis=1) for pair in hops]

    def last_hop(self, near, name):
        return [self.over(near[k], k, True, name) for k in range(2)]

    def send_late(self, parts, name):
        return [self.over(parts[2 * k + 1], k, True, name) for k in range(2)]

    def onward(self, parts, got):
        t = parts[0].shape[1] // 2
        return [
            (parts[2 * k][:, t:].astype(F32) + got[k][:, t:].astype(F32)).astype(BF)
            for k in range(2)
        ]

    def send_on(self, onward, name):
        return [self.over(onward[k], k, False, name) for k in range(2)]

    def total_tokens(self, parts, got, last):
        t = parts[0].shape[1] // 2
        return jnp.concatenate(
            [
                parts[2 * k][:, :t].astype(F32) + got[k][:, :t].astype(F32) + last[k].astype(F32)
                for k in range(2)
            ],
            axis=0,
        )

    def features_here(self, v):
        x, c = lax.axis_index("x"), lax.axis_index("core")
        width = v.shape[-1] // self.n_dp
        return jnp.concatenate(
            [
                lax.dynamic_slice_in_dim(
                    v, (((x + jx) % self.X) * 2 + (c ^ jc)) * width, width, axis=v.ndim - 1
                )
                for jc in range(2)
                for jx in range(self.X)
            ],
            axis=-1,
        )

    def features_home(self, v):
        x, c = lax.axis_index("x"), lax.axis_index("core")
        width = v.shape[-1] // self.n_dp
        return jnp.concatenate(
            [
                lax.dynamic_slice_in_dim(
                    v,
                    (((e % 2) ^ c) * self.X + (e // 2 - x) % self.X) * width,
                    width,
                    axis=v.ndim - 1,
                )
                for e in range(self.n_dp)
            ],
            axis=-1,
        )

    def total(self, v):
        for axis, size in (("core", 2), ("q", 2), ("p", 2), ("x", self.X), ("h", self.H)):
            step = 1
            while step < size:
                with jax.named_scope("norm"):
                    v = v + lax.ppermute(v, axis, [(i ^ step, i) for i in range(size)])
                step *= 2
        return v


def per_device(
    links,
    stream_in,
    cotangent,
    noise_table,
    timesteps,
    bins,
    counts,
    w_qkv,
    w_out,
    w_up,
    w_down,
    m_qkv,
    m_out,
    m_up,
    m_down,
    v_qkv,
    v_out,
    v_up,
    v_down,
):
    H = links.H
    slots, _, D = stream_in.shape
    images = slots // H
    here = lax.axis_index("h")

    steps_here = lax.dynamic_slice_in_dim(timesteps, here * images, images)
    table_rows = noise_table.shape[0]
    picks = (steps_here[:, None] == jnp.arange(table_rows)[None, :]).astype(F32)
    modulation = jnp.dot(
        picks, noise_table.reshape(table_rows, -1), precision=lax.Precision.HIGHEST
    ).reshape(images, 6, D)
    modulation = links.features_here(modulation)
    shift_a, scale_a, gate_a, shift_f, scale_f, gate_f = (modulation[:, i : i + 1] for i in range(6))
    live = jnp.arange(slots) < counts[0]
    loss_scale = live.astype(F32) * (bins.astype(F32) + 1.0) / BINS
    loss_scale = lax.dynamic_slice_in_dim(loss_scale, here * images, images)

    def first_norm(rows):
        return norm_rows(rows) * scale_a + shift_a

    def second_norm(rows):
        return norm_rows(rows) * scale_f + shift_f

    block = w_qkv.shape[2]
    length = stream_in.shape[1] * H * 4
    steps = images // 2
    rows = images * length
    nh, nd = H, 2 * links.X
    heads = H * block
    hidden_width = H * w_up.shape[1]
    whole = lambda width: (steps, 2, length, width)
    parts = [(steps, length // 2, D)] * 4

    def flat(v):
        return v.reshape(rows, v.shape[-1])

    def call(kernel, name, blocked, weights, gates, outs):
        return list(
            group_call(kernel, name, nh, nd, steps, blocked, weights, gates, outs + parts)
        )

    def halves(w):
        size = w.shape[0] // 2
        return w[:size], w[size:]

    def joined(pair):
        return [jnp.concatenate(two, axis=0) for two in zip(*pair)]

    def add_core(keep, sent):
        return (keep.astype(F32) + sent.astype(F32)).astype(BF)

    stream_parts = links.for_groups(links.features_here(stream_in))
    packed = pack_attention_weights(w_qkv, w_out)
    up, down = w_up.astype(BF), w_down.astype(BF)
    stream_got = links.to_group(stream_parts, "stream")
    x_packed = links.over_x(packed, "wqo0")
    stream_parts, stream_got, x_packed, packed, up = sync(
        stream_parts, stream_got, x_packed, packed, up
    )

    stream = jnp.concatenate([stream_parts[0], *stream_got], axis=1).astype(F32)
    a_hops = links.first_hop(first_norm(stream).astype(BF), "a")
    packed_halves = halves(packed)
    far_one = links.over_h(packed_halves[0], "wqoA")
    x_up = links.over_x(up, "wu0")
    wqo = [jnp.stack([packed, *x_packed])]
    a_hops, wqo = sync(a_hops, wqo)
    wqo.append(links.from_core(wqo[0], "wqo0"))
    a_near = links.near(a_hops)
    a_near, far_one, x_up, wqo, packed_two, down = sync(
        a_near, far_one, x_up, wqo, packed_halves[1], down
    )

    a_far = links.last_hop(a_near, "a")
    far_two = links.over_h(packed_two, "wqoB")
    x_down = links.over_x(down, "wd0")
    cot_parts = links.for_groups(links.features_here(cotangent.astype(BF)))
    a_far, far_two, x_down, cot_parts = sync(a_far, far_two, x_down, cot_parts)

    packed_far = joined((far_one, far_two))
    x_far = [links.over_x(w, "wqo1") for w in packed_far]
    cot_got = links.to_group(cot_parts, "cot")
    wu = [jnp.stack([up, *x_up])]
    wu.append(links.from_core(wu[0], "wu0"))
    wd = [jnp.stack([down, *x_down])]
    wd, wu = sync(wd, wu)
    wd.append(links.from_core(wd[0], "wd0"))
    packed_far, x_far, cot_got, wu, wd, up = sync(packed_far, x_far, cot_got, wu, wd, up)

    cot = jnp.concatenate([cot_parts[0], *cot_got], axis=1).astype(F32)
    dy = cot * loss_scale[:, None, None]
    df_hops = links.first_hop((gate_f * dy).astype(BF), "df")
    for w, others in zip(packed_far, x_far):
        wqo.append(jnp.stack([w, *others]))
        wqo.append(links.from_core(wqo[-1], "wqo1"))
    up_halves = halves(up)
    up_one = links.over_h(up_halves[0], "wuA")
    df_near, wqo = sync(links.near(df_hops), wqo)

    df_far = links.last_hop(df_near, "df")
    a_rows, qkv, o, *att = call(
        attention_kernel,
        "attention",
        [a_near[0], a_far[0], a_near[1], a_far[1]],
        wqo,
        [],
        [whole(D), whole(3 * heads), whole(heads)],
    )
    df_far, att, up_one, up_two = sync(df_far, att, up_one, up_halves[1])

    att_got = links.send_late(att, "att")
    up_two = links.over_h(up_two, "wuB")
    att_got, up_two, down = sync(att_got, up_two, down)

    att_last = links.send_on(links.onward(att, att_got), "att")
    down_halves = halves(down)
    down_one = links.over_h(down_halves[0], "wdA")
    up_far = joined((up_one, up_two))
    x_up = [links.over_x(w, "wu1") for w in up_far]
    residual = stream + gate_a * links.total_tokens(att, att_got, att_last)
    b = second_norm(residual).astype(BF)
    b, down_one, up_far, x_up, down_two = sync(b, down_one, up_far, x_up, down_halves[1])

    b_hops = links.first_hop(b, "b")
    down_two = links.over_h(down_two, "wdB")
    for w, others in zip(up_far, x_up):
        wu.append(jnp.stack([w, *others]))
        wu.append(links.from_core(wu[-1], "wu1"))
    b_near, wu, down_one = sync(links.near(b_hops), wu, down_one)
    x_one = [links.over_x(w, "wdA1") for w in down_one]
    down_two, x_one, b_near = sync(down_two, x_one, b_near)

    b_far = links.last_hop(b_near, "b")
    x_two = [links.over_x(w, "wdB1") for w in down_two]
    for w, one, two in zip(joined((down_one, down_two)), x_one, x_two):
        wd.append(jnp.stack([w, *joined((one, two))]))
        wd.append(links.from_core(wd[-1], "wd1"))
    b_far, wd = sync(b_far, wd)

    b_rows, df_rows, hidden, du, *db = call(
        mlp_kernel,
        "mlp",
        [b_near[0], b_far[0], b_near[1], b_far[1], df_near[0], df_far[0], df_near[1], df_far[1]],
        wu + wd,
        [],
        [whole(D), whole(D), whole(hidden_width), whole(hidden_width)],
    )
    b_rows, df_rows, hidden, du, db = sync(b_rows, df_rows, hidden, du, db)

    db_got = links.send_late(db, "db")
    left, right = flat(hidden), flat(df_rows)
    g_send = gradient("g_down_send", nh, nd, left, right, True, 1)
    g_sent = links.from_core(g_send, "g_down")
    g_keep = gradient("g_down_keep", nh, nd, left, right, True, 0)
    db_got, g_sent, g_keep, b_rows, du = sync(db_got, g_sent, g_keep, b_rows, du)

    db_last = links.send_on(links.onward(db, db_got), "db")
    g_down = add_core(g_keep, g_sent)
    down_far = links.send_x(g_down, 1, 0, True, "g_downA")
    left, right = flat(b_rows), flat(du)
    g_send = gradient("g_up_send", nh, nd, left, right, False, 1)
    g_sent = links.from_core(g_send, "g_up")
    g_keep = gradient("g_up_keep", nh, nd, left, right, False, 0)
    dr = dy + jax.vjp(second_norm, residual)[1](links.total_tokens(db, db_got, db_last))[0]
    datt = (gate_a * dr).astype(BF)
    datt, g_down, down_far, g_sent, g_keep, hidden = sync(
        datt, g_down, down_far, g_sent, g_keep, hidden
    )

    datt_hops = links.first_hop(datt, "datt")
    down_far = links.sum_x(g_down, 1, 0, True, down_far).astype(BF)
    down_here = links.send_x(g_down, 1, 0, False, "g_downB")
    down_one = links.send_h(down_far, 0, "g_downA", 0)
    ff = call(down_kernel, "down", [hidden], wd, [], [])
    g_up = add_core(g_keep, g_sent)
    datt_near, down_far, down_here, down_one, ff, g_up = sync(
        links.near(datt_hops), down_far, down_here, down_one, ff, g_up
    )

    datt_far = links.last_hop(datt_near, "datt")
    down_here = links.sum_x(g_down, 1, 0, False, down_here)
    down_two = links.send_h(down_far, 0, "g_downB", 1)
    up_far = links.send_x(g_up, 0, 1, True, "g_upA")
    datt_far, down_two, up_far, g_up, ff = sync(datt_far, down_two, up_far, g_up, ff)

    up_far = links.sum_x(g_up, 0, 1, True, up_far).astype(BF)
    up_one = links.send_h(up_far, 1, "g_upA", 0)
    up_here = links.send_x(g_up, 0, 1, False, "g_upB")
    ff_got = links.send_late(ff, "ff")
    datt, dqkv, *da = call(
        attention_back_kernel,
        "attention_back",
        [datt_near[0], datt_far[0], datt_near[1], datt_far[1], qkv],
        wqo,
        [],
        [whole(D), whole(3 * heads)],
    )
    up_far, up_one, up_here, ff_got, datt, dqkv, da = sync(
        up_far, up_one, up_here, ff_got, datt, dqkv, da
    )

    up_two = links.send_h(up_far, 1, "g_upB", 1)
    da_got = links.send_late(da, "da")
    left, right = flat(a_rows), flat(dqkv)
    g_send = gradient("g_qkv_send", nh, nd, left, right, False, 1)
    g_sent = links.from_core(g_send, "g_qkv")
    g_keep = gradient("g_qkv_keep", nh, nd, left, right, False, 0)
    left, right = sync(flat(datt), flat(o), g_keep)[:2]
    o_send = gradient("g_out_send", nh, nd, left, right, False, 1)
    o_sent = links.from_core(o_send, "g_out")
    o_keep = gradient("g_out_keep", nh, nd, left, right, False, 0)
    up_two, da_got, g_sent, g_keep, o_sent, o_keep = sync(
        up_two, da_got, g_sent, g_keep, o_sent, o_keep
    )

    g_qkv, g_out = add_core(g_keep, g_sent), add_core(o_keep, o_sent)
    qkv_far = links.send_x(g_qkv, 0, 1, True, "g_qkvA")
    da_last = links.send_on(links.onward(da, da_got), "da")
    ff_last = links.send_on(links.onward(ff, ff_got), "ff")
    qkv_far, da_last, ff_last, g_qkv, g_out = sync(qkv_far, da_last, ff_last, g_qkv, g_out)

    qkv_far = links.sum_x(g_qkv, 0, 1, True, qkv_far).astype(BF)
    qkv_there = links.send_h(qkv_far, 1, "g_qkv")
    qkv_here = links.send_x(g_qkv, 0, 1, False, "g_qkvB")
    out_far = links.send_x(g_out, 0, 1, True, "g_outA")
    out_here = links.send_x(g_out, 0, 1, False, "g_outB")
    output = (residual + gate_f * links.total_tokens(ff, ff_got, ff_last)).astype(BF)
    da = links.total_tokens(da, da_got, da_last)
    input_grad = (dr + jax.vjp(first_norm, stream)[1](da)[0]).astype(BF)
    qkv_there, qkv_here, out_far, out_here, g_out, output, input_grad = sync(
        qkv_there, qkv_here, out_far, out_here, g_out, output, input_grad
    )

    out_far = links.sum_x(g_out, 0, 1, True, out_far).astype(BF)
    out_there = links.send_h(out_far, 1, "g_out")
    output = links.at_home(output, links.leave_group(output, "output"))
    input_grad = links.at_home(input_grad, links.leave_group(input_grad, "input_grad")).astype(F32)

    def total(here, there):
        return here + sum(v.astype(F32) for v in there)

    g_down = total(down_here, joined((down_one, down_two)))
    up_here = links.sum_x(g_up, 0, 1, False, up_here)
    g_up = total(up_here, joined((up_one, up_two)))
    g_qkv = total(links.sum_x(g_qkv, 0, 1, False, qkv_here), qkv_there)
    g_qkv = jnp.stack([g_qkv[:, i * block : (i + 1) * block] for i in range(3)])
    g_out = total(links.sum_x(g_out, 0, 1, False, out_here), out_there)
    (g_out,) = sync(g_out)
    g_out = g_out.T
    squares = (
        jnp.sum(g_qkv * g_qkv)
        + jnp.sum(g_out * g_out)
        + jnp.sum(g_up * g_up)
        + jnp.sum(g_down * g_down)
    )
    grad_norm = jnp.sqrt(links.total(squares))
    factor = jnp.minimum(1.0, clip_limit / (grad_norm + 1e-06))
    one_qkv, two_qkv, new_qkv = (
        v.transpose(1, 0, 2)
        for v in adam_update(
            g_qkv, *(v.transpose(1, 0, 2) for v in (m_qkv, v_qkv, w_qkv)), factor, learn_rate
        )
    )
    one_out, two_out, new_out = adam_update(g_out, m_out, v_out, w_out, factor, output_rate)
    one_up, two_up, new_up = adam_update(g_up, m_up, v_up, w_up, factor, learn_rate)
    one_down, two_down, new_down = adam_update(g_down, m_down, v_down, w_down, factor, learn_rate)
    return (
        output,
        input_grad,
        grad_norm,
        one_qkv,
        one_out,
        one_up,
        one_down,
        two_qkv,
        two_out,
        two_up,
        two_down,
        new_qkv,
        new_out,
        new_up,
        new_down,
    )


def solution(mesh):
    n_dp, n_mp = mesh.shape["dp"], mesh.shape["mp"]
    links = Links(n_dp, n_mp)
    fine = Mesh(mesh.devices.reshape(links.X, 2, links.H, 2, 2), ("x", "core", "h", "p", "q"))
    dp, mp = ("x", "core"), ("h", "p", "q")
    tokens, qkv = P(dp, mp, None), P(dp, None, mp)
    rows, columns = P(mp, dp), P(dp, mp)
    weights = (qkv, rows, columns, rows)
    return jax.shard_map(
        lambda *args: per_device(links, *args),
        mesh=fine,
        in_specs=(tokens, tokens, P(), P(dp), P(dp), P(dp)) + 3 * weights,
        out_specs=(tokens, tokens, P()) + 3 * weights,
        check_vma=False,
    )
```

```python
import jax
import jax.numpy as jnp
from jax import lax
from jax.experimental import pallas as pl
from jax.experimental.pallas import tpu as pltpu
from jax.sharding import Mesh
from jax.sharding import PartitionSpec as P

HD = 128
BINS = 8
ADAM_STEP = 10

clip_limit = 1.0
beta_one = 0.9
beta_two = 0.95
learn_rate = 0.02
output_rate = 0.08
adam_epsilon = 1e-08
decay_rate = 0.01

BF = jnp.bfloat16
F32 = jnp.float32


def adam_update(gradient, moment_one, moment_two, weight, factor, step_rate):
    clipped = gradient * factor
    new_one = beta_one * moment_one + (1.0 - beta_one) * clipped
    new_two = beta_two * moment_two + (1.0 - beta_two) * clipped * clipped
    corrected = new_one / (1.0 - beta_one**ADAM_STEP)
    root_two = jnp.sqrt(new_two / (1.0 - beta_two**ADAM_STEP))
    new_weight = weight - step_rate * (corrected / (root_two + adam_epsilon) + decay_rate * weight)
    return (new_one, new_two, new_weight)


def sync(*values):
    return lax.optimization_barrier(values)


def dot(a, b, contract=(1, 0)):
    return lax.dot_general(
        a, b, (((contract[0],), (contract[1],)), ((), ())), preferred_element_type=F32
    )


def rows_of(ref, columns=slice(None)):
    value = ref[0, :, :, columns]
    return value.reshape(value.shape[0] * value.shape[1], value.shape[2])


def join_tokens(pieces, whole):
    for kind, two in enumerate(pieces):
        for r, ref in enumerate(two):
            t = ref.shape[1]
            whole[0, kind, r * t : (r + 1) * t] = ref[0]


def put_parts(value, columns, parts):
    half = value.shape[0] // (2 * len(parts))
    for kind, (keep, send) in enumerate(parts):
        keep[0, :, columns] = value[2 * kind * half : (2 * kind + 1) * half]
        send[0, :, columns] = value[(2 * kind + 1) * half : (2 * kind + 2) * half]


def softmax_rows(q, k):
    scores = dot(q, k, (1, 1)) * HD ** (-0.5)
    weights = jnp.exp(scores - jnp.max(scores, axis=-1, keepdims=True))
    return weights * (1.0 / jnp.sum(weights, axis=-1, keepdims=True))


def head_columns(jh, part, n, block):
    start = (jh * 3 + part) * block + n * HD
    return slice(start, start + HD)


class Pieces:
    def __init__(self, refs):
        self.refs, self.at = refs, 0

    def take(self, count):
        self.at += count
        return self.refs[self.at - count : self.at]

    def tokens(self):
        near_far = self.take(4)
        return near_far[:2], near_far[2:]

    def parts(self):
        a, b, c, d = self.take(4)
        return (a, b), (c, d)


class Separate:
    def __init__(self, refs, nd):
        self.refs, self.depth = refs, refs[0].shape[0]
        self.shape = refs[0].shape[1:]

    def block(self, jh, d, rows=slice(None), columns=slice(None)):
        core, x = divmod(d, self.depth)
        return self.refs[2 * jh + core][x, rows, columns]


def attention_kernel(nh, nd, *refs):
    refs = Pieces(refs)
    tokens, weights = refs.tokens(), Separate(refs.take(2 * nh), nd)
    (a, qkv, o, probs), parts = refs.take(4), refs.parts()
    join_tokens(tokens, a)
    depth, block = weights.shape[0], weights.shape[1] // 4
    width = 3 * block
    inward = (slice(None), slice(0, width))
    outward = (slice(None), slice(width, width + block))
    kinds, length = a.shape[1], a.shape[2]
    for jh in range(nh):
        total = dot(rows_of(a, slice(0, depth)), weights.block(jh, 0, *inward))
        for d in range(1, nd):
            total += dot(rows_of(a, slice(d * depth, (d + 1) * depth)), weights.block(jh, d, *inward))
        qkv[0, :, :, jh * width : (jh + 1) * width] = total.astype(BF).reshape(kinds, length, width)
    for kind in range(kinds):
        for jh in range(nh):
            for n in range(block // HD):
                q, k, v = (qkv[0, kind, :, head_columns(jh, i, n, block)] for i in range(3))
                p = softmax_rows(q, k).astype(BF)
                probs[0, kind, jh * (block // HD) + n] = p
                out = dot(p, v).astype(BF)
                o[0, kind, :, jh * block + n * HD : jh * block + (n + 1) * HD] = out
    for d in range(nd):
        total = dot(rows_of(o, slice(0, block)), weights.block(0, d, *outward), (1, 1))
        for jh in range(1, nh):
            total += dot(rows_of(o, slice(jh * block, (jh + 1) * block)), weights.block(jh, d, *outward), (1, 1))
        put_parts(total.astype(BF), slice(d * depth, (d + 1) * depth), parts)


def up_kernel(nh, nd, *refs):
    refs = Pieces(refs)
    b_tokens, wu = refs.tokens(), Separate(refs.take(2 * nh), nd)
    b, hidden, slope = refs.take(3)
    join_tokens(b_tokens, b)
    depth, width = wu.shape
    kinds, length = b.shape[1], b.shape[2]
    chunk = min(width, 512)
    curve, cubic = 0.7978845608028654, 0.044715
    for jh in range(nh):
        for c in range(0, width, chunk):
            part = slice(c, c + chunk)
            u = dot(rows_of(b, slice(0, depth)), wu.block(jh, 0, columns=part))
            for d in range(1, nd):
                cols = slice(d * depth, (d + 1) * depth)
                u += dot(rows_of(b, cols), wu.block(jh, d, columns=part))
            square = u * u
            t = jnp.tanh(curve * u * (1.0 + cubic * square))
            near = 0.5 * (1.0 + t)
            rise = near + 0.5 * u * (1.0 - t * t) * (curve * (1.0 + 3.0 * cubic * square))
            cols = slice(jh * width + c, jh * width + c + chunk)
            hidden[0, :, :, cols] = (u * near).astype(BF).reshape(kinds, length, chunk)
            slope[0, :, :, cols] = rise.astype(BF).reshape(kinds, length, chunk)


def up_back_kernel(nh, nd, *refs):
    refs = Pieces(refs)
    df_tokens, (slope,) = refs.tokens(), refs.take(1)
    wu, wd = (Separate(refs.take(2 * nh), nd) for _ in range(2))
    (df, du), parts = refs.take(2), refs.parts()
    join_tokens(df_tokens, df)
    depth, width = wu.shape
    kinds, length = df.shape[1], df.shape[2]
    chunk = min(width, 512)
    for jh in range(nh):
        for c in range(0, width, chunk):
            part = slice(c, c + chunk)
            dh = dot(rows_of(df, slice(0, depth)), wd.block(jh, 0, part), (1, 1))
            for d in range(1, nd):
                cols = slice(d * depth, (d + 1) * depth)
                dh += dot(rows_of(df, cols), wd.block(jh, d, part), (1, 1))
            cols = slice(jh * width + c, jh * width + c + chunk)
            value = dh * rows_of(slope, cols).astype(F32)
            du[0, :, :, cols] = value.astype(BF).reshape(kinds, length, chunk)
    for d in range(nd):
        total = dot(rows_of(du, slice(0, width)), wu.block(0, d), (1, 1))
        for jh in range(1, nh):
            total += dot(rows_of(du, slice(jh * width, (jh + 1) * width)), wu.block(jh, d), (1, 1))
        put_parts(total.astype(BF), slice(d * depth, (d + 1) * depth), parts)


def down_kernel(nh, nd, *refs):
    refs = Pieces(refs)
    (hidden,), wd = refs.take(1), Separate(refs.take(2 * nh), nd)
    parts = refs.parts()
    width, depth = wd.shape
    for d in range(nd):
        total = dot(rows_of(hidden, slice(0, width)), wd.block(0, d))
        for jh in range(1, nh):
            total += dot(rows_of(hidden, slice(jh * width, (jh + 1) * width)), wd.block(jh, d))
        put_parts(total.astype(BF), slice(d * depth, (d + 1) * depth), parts)


def attention_back_kernel(nh, nd, *refs):
    refs = Pieces(refs)
    (a, o), tokens, (qkv, probs) = refs.take(2), refs.tokens(), refs.take(2)
    weights = Separate(refs.take(2 * nh), nd)
    parts, (all_datt, all_dqkv, sent) = refs.parts(), refs.take(3)
    step = pl.program_id(0)
    datt, dqkv = (v.at[pl.ds(step, 1)] for v in (all_datt, all_dqkv))
    join_tokens(tokens, datt)
    depth, block = weights.shape[0], weights.shape[1] // 4
    width = 3 * block
    inward = (slice(None), slice(0, width))
    outward = (slice(None), slice(width, width + block))
    kinds, length = datt.shape[1], datt.shape[2]
    for jh in range(nh):
        do_all = dot(rows_of(datt, slice(0, depth)), weights.block(jh, 0, *outward))
        for d in range(1, nd):
            do_all += dot(rows_of(datt, slice(d * depth, (d + 1) * depth)), weights.block(jh, d, *outward))
        do_all = do_all.astype(BF)
        for kind in range(kinds):
            for n in range(block // HD):
                q, k, v = (qkv[0, kind, :, head_columns(jh, i, n, block)] for i in range(3))
                do = do_all[kind * length : (kind + 1) * length, n * HD : (n + 1) * HD]
                rounded = probs[0, kind, jh * (block // HD) + n]
                dv = dot(rounded, do, (0, 0))
                dp = dot(do, v, (1, 1))
                p = rounded.astype(F32)
                ds = (p * (dp - jnp.sum(p * dp, axis=-1, keepdims=True))).astype(BF)
                dq = dot(ds, k) * HD ** (-0.5)
                dk = dot(ds, q, (0, 0)) * HD ** (-0.5)
                for i, value in enumerate((dq, dk, dv)):
                    dqkv[0, kind, :, head_columns(jh, i, n, block)] = value.astype(BF)
    for d in range(nd):
        total = dot(rows_of(dqkv, slice(0, width)), weights.block(0, d, *inward), (1, 1))
        for jh in range(1, nh):
            total += dot(rows_of(dqkv, slice(jh * width, (jh + 1) * width)), weights.block(jh, d, *inward), (1, 1))
        put_parts(total.astype(BF), slice(d * depth, (d + 1) * depth), parts)
    across, both = nd // 2, width + block

    def every_row(ref, columns=slice(None)):
        value = ref[:, :, :, columns]
        return value.reshape(-1, value.shape[-1])

    @pl.when(step == pl.num_programs(0) - 1)
    def _():
        for jx in range(across):
            cols = slice((across + jx) * depth, (across + jx + 1) * depth)
            inward = dot(a[cols], every_row(all_dqkv)).astype(BF)
            outward = dot(every_row(all_datt, cols), every_row(o), (0, 0)).astype(BF)
            rows = slice(jx * depth, (jx + 1) * depth)
            for jh in range(nh):
                at = jh * both
                sent[rows, at : at + width] = inward[:, jh * width : (jh + 1) * width]
                sent[rows, at + width : at + both] = outward[:, jh * block : (jh + 1) * block]


def group_call(kernel, name, nh, nd, steps, blocked, whole, outs, resident=(), whole_outs=()):
    def cut(shape):
        zeros = (0,) * (len(shape) - 1)
        return pl.BlockSpec((1,) + tuple(shape[1:]), lambda i: (i,) + zeros)

    def stay(shape):
        zeros = (0,) * len(shape)
        return pl.BlockSpec(tuple(shape), lambda i: zeros)

    return pl.pallas_call(
        lambda *refs: kernel(nh, nd, *refs),
        name=name,
        grid=(steps,),
        in_specs=[stay(v.shape) for v in resident]
        + [cut(v.shape) for v in blocked]
        + [pl.BlockSpec(memory_space=pltpu.VMEM)] * len(whole),
        out_specs=[cut(s) for s in outs] + [stay(s) for s in whole_outs],
        out_shape=[jax.ShapeDtypeStruct(s, BF) for s in (*outs, *whole_outs)],
        compiler_params=pltpu.CompilerParams(vmem_limit_bytes=62 * 2**20),
        cost_estimate=pl.CostEstimate(flops=0, bytes_accessed=0, transcendentals=0),
    )(*resident, *blocked, *whole)


def image_call(kernel, name, steps, arrays, outs):
    def seen(shape):
        return (2, steps, *shape[1:]) if shape[0] == 2 * steps else tuple(shape)

    def cut(shape):
        zeros = (0,) * (len(shape) - 2)
        if shape[0] == 2 and len(shape) == 4:
            return pl.BlockSpec((2, 1, *shape[2:]), lambda i: (0, i, *zeros))
        return pl.BlockSpec((1, *shape[1:]), lambda i: (i, 0, *zeros))

    made = pl.pallas_call(
        kernel,
        name=name,
        grid=(steps,),
        in_specs=[cut(seen(v.shape)) for v in arrays],
        out_specs=[cut(seen(shape)) for shape, _ in outs],
        out_shape=[jax.ShapeDtypeStruct(seen(shape), dtype) for shape, dtype in outs],
        compiler_params=pltpu.CompilerParams(vmem_limit_bytes=32 * 2**20),
        cost_estimate=pl.CostEstimate(flops=0, bytes_accessed=0, transcendentals=0),
    )(*[v.reshape(seen(v.shape)) for v in arrays])
    return [v.reshape(shape) for v, (shape, _) in zip(made, outs)]


def row_parts(values):
    center = values - jnp.mean(values, axis=-1, keepdims=True)
    factor = lax.rsqrt(jnp.mean(center * center, axis=-1, keepdims=True) + 1e-06)
    return center * factor, factor


def norm_back(values, gradient):
    rows, factor = row_parts(values)
    return factor * (
        gradient
        - jnp.mean(gradient, axis=-1, keepdims=True)
        - rows * jnp.mean(gradient * rows, axis=-1, keepdims=True)
    )


def token_sum(sums, kind):
    keep, got, last = sums[kind], sums[2 + kind], sums[4 + kind]
    t = last.shape[1]
    return keep[0, :t].astype(F32) + got[0, :t].astype(F32) + last[0].astype(F32)


def first_norm_kernel(stream, mod, *a):
    for kind in range(2):
        rows, _ = row_parts(stream[kind, 0].astype(F32))
        a[kind][0] = (rows * mod[kind, 0, 1:2] + mod[kind, 0, 0:1]).astype(BF)


def loss_kernel(cot, weight, mod, *df):
    for kind in range(2):
        seed = cot[kind, 0].astype(F32) * weight[kind, 0]
        df[kind][0] = (mod[kind, 0, 5:6] * seed).astype(BF)


def second_norm_kernel(stream, mod, *refs):
    sums, residual, b = refs[:6], refs[6], refs[7:]
    for kind in range(2):
        r = stream[kind, 0].astype(F32) + mod[kind, 0, 2:3] * token_sum(sums, kind)
        residual[kind, 0] = r
        rows, _ = row_parts(r)
        b[kind][0] = (rows * mod[kind, 0, 4:5] + mod[kind, 0, 3:4]).astype(BF)


def second_norm_back_kernel(cot, weight, residual, mod, *refs):
    sums, dr, datt = refs[:6], refs[6], refs[7:]
    for kind in range(2):
        seed = cot[kind, 0].astype(F32) * weight[kind, 0]
        g = seed + norm_back(residual[kind, 0], token_sum(sums, kind) * mod[kind, 0, 4:5])
        dr[kind, 0] = g
        datt[kind][0] = (mod[kind, 0, 2:3] * g).astype(BF)


def first_norm_back_kernel(stream, dr, mod, *refs):
    sums, out = refs[:6], refs[6]
    for kind in range(2):
        g = norm_back(stream[kind, 0].astype(F32), token_sum(sums, kind) * mod[kind, 0, 1:2])
        out[kind, 0] = (dr[kind, 0] + g).astype(BF)


def output_kernel(residual, mod, *refs):
    sums, out = refs[:6], refs[6]
    for kind in range(2):
        out[kind, 0] = (residual[kind, 0] + mod[kind, 0, 5:6] * token_sum(sums, kind)).astype(BF)


def pack_attention_weights(w_qkv, w_out):
    depth, _, block = w_qkv.shape

    def kernel(inward, outward, packed):
        for i in range(3):
            packed[:, i * block : (i + 1) * block] = inward[i].astype(BF)
        packed[:, 3 * block :] = outward[...].T.astype(BF)

    return pl.pallas_call(
        kernel,
        name="pack",
        out_shape=jax.ShapeDtypeStruct((depth, 4 * block), BF),
        compiler_params=pltpu.CompilerParams(vmem_limit_bytes=32 * 2**20),
    )(w_qkv.transpose(1, 0, 2), w_out)


def gradient(name, nh, nd, left, right, left_is_hidden, core):
    rows = left.shape[0]
    hidden, features = (left, right) if left_is_hidden else (right, left)
    h_width, d_width, half = hidden.shape[1] // nh, features.shape[1] // nd, nd // 2

    def kernel(left, right, out):
        out[...] = dot(left[...], right[...], (0, 0)).astype(BF)

    h_spec = pl.BlockSpec((rows, h_width), lambda jh, d: (0, jh))
    d_spec = pl.BlockSpec((rows, d_width), lambda jh, d: (0, core * half + d))
    if left_is_hidden:
        in_specs, out_spec = [h_spec, d_spec], pl.BlockSpec((h_width, d_width), lambda jh, d: (jh, d))
        shape = (nh * h_width, half * d_width)
    else:
        in_specs, out_spec = [d_spec, h_spec], pl.BlockSpec((d_width, h_width), lambda jh, d: (d, jh))
        shape = (half * d_width, nh * h_width)
    return pl.pallas_call(
        kernel,
        name=name,
        grid=(nh, half),
        in_specs=in_specs,
        out_specs=out_spec,
        out_shape=jax.ShapeDtypeStruct(shape, BF),
        compiler_params=pltpu.CompilerParams(vmem_limit_bytes=48 * 2**20),
        cost_estimate=pl.CostEstimate(flops=0, bytes_accessed=0, transcendentals=0),
    )(left, right)


def one_step(kernel, name, arrays, columns, outs, dtype=BF):
    return pl.pallas_call(
        kernel,
        name=name,
        grid=(1,),
        in_specs=[
            pl.BlockSpec((v.shape[0], c or v.shape[1]), lambda i: (0, 0))
            for v, c in zip(arrays, columns)
        ],
        out_specs=[pl.BlockSpec(shape, lambda i: (0, 0)) for shape in outs],
        out_shape=[jax.ShapeDtypeStruct(shape, dtype) for shape in outs],
        compiler_params=pltpu.CompilerParams(vmem_limit_bytes=60 * 2**20),
        cost_estimate=pl.CostEstimate(flops=0, bytes_accessed=0, transcendentals=0),
    )(*arrays)


def down_kept(nh, nd, hidden, df, sent):
    half = nd // 2
    height, width = hidden.shape[1] // nh, df.shape[1] // nd
    cut = height // 2

    def kernel(hidden, df, sent, *outs):
        for jx in range(half):
            one, two, three = outs[3 * jx : 3 * jx + 3]
            cols = slice(jx * width, (jx + 1) * width)
            for jh in range(nh):
                rows = slice(jh * height, (jh + 1) * height)
                g = dot(hidden[:, rows], df[:, cols], (0, 0)) + sent[rows, cols].astype(F32)
                g = g.astype(BF)
                if jh:
                    one[(jh - 1) * cut : jh * cut] = g[:cut]
                    two[(jh - 1) * cut : jh * cut] = g[cut:]
                else:
                    two[(nh - 1) * cut :] = g[:cut]
                    three[...] = g[cut:]

    shapes = [((nh - 1) * cut, width), (nh * cut, width), (cut, width)] * half
    return one_step(kernel, "g_down_keep", (hidden, df, sent), (None, half * width, None), shapes)


def up_kept(nh, nd, b, du, sent):
    half = nd // 2
    height, width = b.shape[1] // nd, du.shape[1] // nh

    def kernel(b, du, sent, *outs):
        for jx in range(half):
            far, here = outs[2 * jx : 2 * jx + 2]
            rows = slice(jx * height, (jx + 1) * height)
            for jh in range(nh):
                cols = slice(jh * width, (jh + 1) * width)
                g = dot(b[:, rows], du[:, cols], (0, 0)) + sent[rows, cols].astype(F32)
                if jh:
                    far[:, (jh - 1) * width : jh * width] = g.astype(BF)
                else:
                    here[...] = g.astype(BF)

    shapes = [(height, (nh - 1) * width), (height, width)] * half
    return one_step(kernel, "g_up_keep", (b, du, sent), (half * height, None, None), shapes)


def attention_kept(nh, nd, a, dqkv, datt, o, sent):
    half = nd // 2
    height = a.shape[0] // nd
    width, block = dqkv.shape[1] // nh, o.shape[1] // nh
    both = width + block

    def kernel(a, dqkv, datt, o, sent, *outs):
        for jx in range(half):
            far, here = outs[2 * jx : 2 * jx + 2]
            rows = slice(jx * height, (jx + 1) * height)
            inward = dot(a[rows], dqkv[...])
            outward = dot(datt[:, rows], o[...], (0, 0))
            for jh in range(nh):
                out, at = (far, (jh - 1) * both) if jh else (here, 0)
                terms = sent[rows, jh * both : (jh + 1) * both].astype(F32)
                g = inward[:, jh * width : (jh + 1) * width] + terms[:, :width]
                out[:, at : at + width] = g.astype(BF)
                g = outward[:, jh * block : (jh + 1) * block] + terms[:, width:]
                out[:, at + width : at + both] = g.astype(BF)

    shapes = [(height, (nh - 1) * both), (height, both)] * half
    cols = half * height
    return one_step(
        kernel, "g_att_keep", (a, dqkv, datt, o, sent), (None, None, cols, None, None), shapes
    )


def add_terms(name, terms, cuts=1, rows=None):
    rows, width = rows or terms[0].shape[0], terms[0].shape[1]
    size = rows // cuts

    def kernel(*refs):
        terms, outs = refs[: len(refs) - cuts], refs[len(refs) - cuts :]
        for c, out in enumerate(outs):
            out[...] = sum(
                v[c * size : (c + 1) * size].astype(F32) for v in terms
            ).astype(BF)

    return one_step(kernel, name, terms, [None] * len(terms), [(size, width)] * cuts)


def onward_kernel(*refs):
    for kind in range(2):
        keep, got, out = refs[kind], refs[2 + kind], refs[4 + kind]
        t = out.shape[1]
        out[0] = (keep[0, t:].astype(F32) + got[0, t:].astype(F32)).astype(BF)


def unpack_attention_gradient(terms):
    depth, width = terms[0].shape
    block = width // 4

    def kernel(*refs):
        *terms, inward, outward, squares = refs
        total = sum(v[...].astype(F32) for v in terms)
        square = total * total
        squares[...] = sum(
            jnp.sum(square[:, c : c + 128].reshape(depth // 8, 8, 128), axis=0)
            for c in range(0, width, 128)
        )
        for i in range(3):
            inward[i] = total[:, i * block : (i + 1) * block]
        outward[...] = total[:, 3 * block :].T

    return pl.pallas_call(
        kernel,
        name="unpack",
        out_shape=[
            jax.ShapeDtypeStruct((3, depth, block), F32),
            jax.ShapeDtypeStruct((block, depth), F32),
            jax.ShapeDtypeStruct((8, 128), F32),
        ],
        compiler_params=pltpu.CompilerParams(vmem_limit_bytes=32 * 2**20),
        cost_estimate=pl.CostEstimate(flops=0, bytes_accessed=0, transcendentals=0),
    )(*terms)


class Links:
    axes = ("x", "core", "h", "p", "q")

    def __init__(self, n_dp, n_mp):
        self.X, self.H = n_dp // 2, n_mp // 4
        self.n_dp, self.n_mp = n_dp, n_mp

    def shifted(self, v, axis, size, offset, name):
        with jax.named_scope(f"{name}_{axis}"):
            return lax.ppermute(v, axis, [((dst + offset) % size, dst) for dst in range(size)])

    def from_core(self, v, name):
        return self.shifted(v, "core", 2, 1, name)

    def from_x(self, v, jx, name):
        return self.shifted(v, "x", self.X, jx, name)

    def from_h(self, v, jh, name):
        return self.shifted(v, "h", self.H, jh, name)

    def over_h(self, w, name):
        return [self.from_h(w, jh, name) for jh in range(1, self.H)]

    def over_x(self, w, name):
        return [self.from_x(w, jx, name) for jx in range(1, self.X)]

    def send_x(self, parts, name):
        return [self.from_x(parts[jx], -jx, name) for jx in range(1, self.X)]

    def send_h(self, g, h, name):
        width = g.shape[h] // (self.H - 1)
        return [
            self.from_h(lax.slice_in_dim(g, (jh - 1) * width, jh * width, axis=h), -jh, name)
            for jh in range(1, self.H)
        ]

    def for_groups(self, v):
        here = lax.axis_index("h")
        images = v.shape[0] // self.H
        return [
            lax.dynamic_slice_in_dim(v, ((here - jh) % self.H) * images, images, axis=0)
            for jh in range(self.H)
        ]

    def to_group(self, parts, name):
        return [self.from_h(parts[jh], jh, name) for jh in range(1, self.H)]

    def leave_group(self, v, name):
        tokens = v.shape[1] // self.H
        return [
            self.from_h(v[:, jh * tokens : (jh + 1) * tokens], -jh, name) for jh in range(1, self.H)
        ]

    def at_home(self, v, received):
        here = lax.axis_index("h")
        images = v.shape[0]
        tokens = v.shape[1] // self.H
        out = jnp.zeros((images * self.H, tokens, v.shape[2]), v.dtype)
        for jh, part in enumerate([v[:, :tokens], *received]):
            out = lax.dynamic_update_slice_in_dim(
                out, part, ((here - jh) % self.H) * images, axis=0
            )
        return self.features_home(out)

    def over(self, v, kind, late, name):
        return self.shifted(v, "p" if (kind == 0) != late else "q", 2, 1, f"{name}{kind}")

    def first_hop(self, own, name):
        return [(own[k], self.over(own[k], k, False, name)) for k in range(2)]

    def near(self, hops):
        return [jnp.concatenate(pair, axis=1) for pair in hops]

    def last_hop(self, near, name):
        return [self.over(near[k], k, True, name) for k in range(2)]

    def send_late(self, parts, name):
        return [self.over(parts[2 * k + 1], k, True, name) for k in range(2)]

    def send_on(self, onward, name):
        return [self.over(onward[k], k, False, name) for k in range(2)]

    def features_here(self, v):
        x, c = lax.axis_index("x"), lax.axis_index("core")
        width = v.shape[-1] // self.n_dp
        return jnp.concatenate(
            [
                lax.dynamic_slice_in_dim(
                    v, (((x + jx) % self.X) * 2 + (c ^ jc)) * width, width, axis=v.ndim - 1
                )
                for jc in range(2)
                for jx in range(self.X)
            ],
            axis=-1,
        )

    def features_home(self, v):
        x, c = lax.axis_index("x"), lax.axis_index("core")
        width = v.shape[-1] // self.n_dp
        return jnp.concatenate(
            [
                lax.dynamic_slice_in_dim(
                    v,
                    (((e % 2) ^ c) * self.X + (e // 2 - x) % self.X) * width,
                    width,
                    axis=v.ndim - 1,
                )
                for e in range(self.n_dp)
            ],
            axis=-1,
        )

    def total(self, v):
        for axis, size in (("core", 2), ("q", 2), ("x", self.X), ("p", 2), ("h", self.H)):
            step = 1
            while step < size:
                with jax.named_scope("norm"):
                    v = v + lax.ppermute(v, axis, [(i ^ step, i) for i in range(size)])
                step *= 2
        return v


def per_device(
    links,
    stream_in,
    cotangent,
    noise_table,
    timesteps,
    bins,
    counts,
    w_qkv,
    w_out,
    w_up,
    w_down,
    m_qkv,
    m_out,
    m_up,
    m_down,
    v_qkv,
    v_out,
    v_up,
    v_down,
):
    H = links.H
    slots, _, D = stream_in.shape
    images = slots // H
    here = lax.axis_index("h")

    steps_here = lax.dynamic_slice_in_dim(timesteps, here * images, images)
    table_rows = noise_table.shape[0]
    picks = (steps_here[:, None] == jnp.arange(table_rows)[None, :]).astype(F32)
    modulation = jnp.dot(
        picks, noise_table.reshape(table_rows, -1), precision=lax.Precision.HIGHEST
    ).reshape(images, 6, D)
    modulation = links.features_here(modulation)
    live = jnp.arange(slots) < counts[0]
    loss_scale = live.astype(F32) * (bins.astype(F32) + 1.0) / BINS
    loss_scale = lax.dynamic_slice_in_dim(loss_scale, here * images, images)
    loss_scale = jnp.broadcast_to(loss_scale[:, None, None], (images, 1, D))

    block = w_qkv.shape[2]
    length = stream_in.shape[1] * H * 4
    steps = images // 2
    rows = images * length
    nh, nd = H, 2 * links.X
    heads = H * block
    hidden_width = H * w_up.shape[1]
    whole = lambda width: (steps, 2, length, width)
    parts = [(steps, length // 2, D)] * 4

    tokens = length // 4
    every, kinds = (images, tokens, D), [((steps, tokens, D), BF)] * 2

    def over_images(kernel, name, arrays, outs):
        return image_call(kernel, name, steps, arrays, outs)

    def onward(parts, got, name):
        arrays = [parts[0], parts[2], *got]
        return over_images(onward_kernel, name, arrays, kinds)

    def sums(parts, got, last):
        return [parts[0], parts[2], *got, *last]

    def flat(v):
        return v.reshape(rows, v.shape[-1])

    def call(kernel, name, blocked, weights, outs, resident=(), whole_outs=()):
        return list(
            group_call(kernel, name, nh, nd, steps, blocked, weights, outs, resident, whole_outs)
        )

    def halves(w):
        size = w.shape[0] // 2
        return w[:size], w[size:]

    def joined(pair):
        return [jnp.concatenate(two, axis=0) for two in zip(*pair)]

    def total(here, there):
        return here + sum(v.astype(F32) for v in there)

    stream_parts = links.for_groups(links.features_here(stream_in))
    packed = pack_attention_weights(w_qkv, w_out)
    stream_got = links.to_group(stream_parts, "stream")
    x_packed = links.over_x(packed, "wqo0")
    up, down = w_up.astype(BF), w_down.astype(BF)
    stream_parts, stream_got, x_packed, packed, up = sync(
        stream_parts, stream_got, x_packed, packed, up
    )

    stream = jnp.concatenate([stream_parts[0], *stream_got], axis=1)
    a_own = over_images(first_norm_kernel, "first_norm", [stream, modulation], kinds)
    a_hops = links.first_hop(a_own, "a")
    packed_one, packed_two = halves(packed)
    far_one = links.over_h(packed_one, "wqoA")
    x_up = links.over_x(up, "wu0")
    wqo = [jnp.stack([packed, *x_packed])]
    a_near, far_one, x_up, wqo, packed_two = sync(
        links.near(a_hops), far_one, x_up, wqo, packed_two
    )

    a_far = links.last_hop(a_near, "a")
    far_two = links.over_h(packed_two, "wqoB")
    x_one = [links.over_x(w, "wqoA1") for w in far_one]
    cot_parts = links.for_groups(links.features_here(cotangent.astype(BF)))
    cot_one = [v[:steps] for v in cot_parts]
    cot_two = [v[steps:] for v in cot_parts]
    wu = [jnp.stack([up, *x_up])]
    a_far, far_two, x_one, cot_one, cot_two, wqo, wu = sync(
        a_far, far_two, x_one, cot_one, cot_two, wqo, wu
    )

    x_two = [links.over_x(w, "wqoB1") for w in far_two]
    cot_one = [cot_one[0], *links.to_group(cot_one, "cotA")]
    wqo.append(links.from_core(wqo[0], "wqo0"))
    wu.append(links.from_core(wu[0], "wu0"))
    packed_far = joined((far_one, far_two))
    packed_far, x_two, cot_one, cot_two, wqo, wu = sync(
        packed_far, x_two, cot_one, cot_two, wqo, wu
    )

    cot_two = [cot_two[0], *links.to_group(cot_two, "cotB")]
    for w, one, two in zip(packed_far, x_one, x_two):
        wqo.append(jnp.stack([w, *joined((one, two))]))
        wqo.append(links.from_core(wqo[-1], "wqo1"))
    up_one, up_two = halves(up)
    cot_one, cot_two, wqo, up_one, up_two, down = sync(cot_one, cot_two, wqo, up_one, up_two, down)

    cot = jnp.concatenate([jnp.concatenate(v, axis=1) for v in (cot_one, cot_two)], axis=0)
    df_own = over_images(loss_kernel, "loss", [cot, loss_scale, modulation], kinds)
    df_near = links.near(links.first_hop(df_own, "df"))
    up_one = links.over_h(up_one, "wuA")
    x_down = links.over_x(down, "wd0")
    a_rows, qkv, o, probs, *att = call(
        attention_kernel,
        "attention",
        [a_near[0], a_far[0], a_near[1], a_far[1]],
        wqo,
        [whole(D), whole(3 * heads), whole(heads), (steps, 2, heads // HD, length, length), *parts],
    )
    df_near, att, up_one, up_two, x_down = sync(df_near, att, up_one, up_two, x_down)

    att_got = links.send_late(att, "att")
    up_two = links.over_h(up_two, "wuB")
    wd = [jnp.stack([down, *x_down])]
    wd.append(links.from_core(wd[0], "wd0"))
    att_got, up_two, wd, down = sync(att_got, up_two, wd, down)

    att_last = links.send_on(onward(att, att_got, "att_onward"), "att")
    down_one, down_two = halves(down)
    down_one = links.over_h(down_one, "wdA")
    up_far = joined((up_one, up_two))
    x_up = [links.over_x(w, "wu1") for w in up_far]
    residual, *b = over_images(
        second_norm_kernel,
        "second_norm",
        [stream, modulation, *sums(att, att_got, att_last)],
        [(every, F32), *kinds],
    )
    b, down_one, up_far, x_up, down_two = sync(b, down_one, up_far, x_up, down_two)

    b_hops = links.first_hop(b, "b")
    down_two = links.over_h(down_two, "wdB")
    x_one = [links.over_x(w, "wdA1") for w in down_one]
    wu_far = [jnp.stack([w, *others]) for w, others in zip(up_far, x_up)]
    b_near, down_two, x_one, wu_far = sync(links.near(b_hops), down_two, x_one, wu_far)

    b_far = links.last_hop(b_near, "b")
    x_two = [links.over_x(w, "wdB1") for w in down_two]
    for w in wu_far:
        wu += [w, links.from_core(w, "wu1")]
    b_far, x_two, wu, df_near = sync(b_far, x_two, wu, df_near)

    df_far = links.last_hop(df_near, "df")
    for w, one, two in zip(joined((down_one, down_two)), x_one, x_two):
        wd.append(jnp.stack([w, *joined((one, two))]))
        wd.append(links.from_core(wd[-1], "wd1"))
    b_rows, hidden, slope = call(
        up_kernel,
        "up",
        [b_near[0], b_far[0], b_near[1], b_far[1]],
        wu,
        [whole(D), whole(hidden_width), whole(hidden_width)],
    )
    df_far, wd, b_rows, hidden, slope = sync(df_far, wd, b_rows, hidden, slope)

    df_rows, du, *db = call(
        up_back_kernel,
        "up_back",
        [df_near[0], df_far[0], df_near[1], df_far[1], slope],
        wu + wd,
        [whole(D), whole(hidden_width), *parts],
    )
    b_rows, df_rows, hidden, du, db, a_rows = sync(b_rows, df_rows, hidden, du, db, a_rows)

    db_got = links.send_late(db, "db")
    down_send = gradient("g_down_send", nh, nd, flat(hidden), flat(df_rows), True, 1)
    up_send = gradient("g_up_send", nh, nd, flat(b_rows), flat(du), False, 1)
    a_columns = flat(a_rows).T
    db_got, down_send, up_send, b_rows, du, hidden, df_rows, a_columns = sync(
        db_got, down_send, up_send, b_rows, du, hidden, df_rows, a_columns
    )

    db_last = links.send_on(onward(db, db_got, "db_onward"), "db")
    down_sent = links.from_core(down_send, "g_down")
    g_down = down_kept(nh, nd, flat(hidden), flat(df_rows), down_sent)
    db_last, g_down, up_send, b_rows, du, hidden = sync(
        db_last, g_down, up_send, b_rows, du, hidden
    )

    dr, *datt_own = over_images(
        second_norm_back_kernel,
        "second_norm_back",
        [cot, loss_scale, residual, modulation, *sums(db, db_got, db_last)],
        [(every, F32), *kinds],
    )
    datt_hops = links.first_hop(datt_own, "datt")
    down_one = links.send_x(g_down[0::3], "g_downA")
    up_sent = links.from_core(up_send, "g_up")
    (down_one,) = add_terms("g_downA_sum", [g_down[0], *down_one])
    datt_near, g_down, down_one, up_sent, b_rows, du, hidden = sync(
        links.near(datt_hops), g_down, down_one, up_sent, b_rows, du, hidden
    )

    datt_far = links.last_hop(datt_near, "datt")
    down_one = links.send_h(down_one, 0, "g_downA")
    down_mid = links.send_x(g_down[1::3], "g_downB")
    ff = call(down_kernel, "down", [hidden], wd, parts)
    g_up = up_kept(nh, nd, flat(b_rows), flat(du), up_sent)
    far = (nh - 1) * (g_down[1].shape[0] // nh)
    (down_two,) = add_terms("g_downB_sum", [g_down[1], *down_mid], 1, far)
    datt_far, down_one, down_mid, down_two, g_down, g_up, ff = sync(
        datt_far, down_one, down_mid, down_two, g_down, g_up, ff
    )

    down_two = links.send_h(down_two, 0, "g_downB")
    up_far = links.send_x(g_up[0::2], "g_upA")
    ff_got = links.send_late(ff, "ff")
    *da, datt, dqkv, att_send = call(
        attention_back_kernel,
        "attention_back",
        [datt_near[0], datt_far[0], datt_near[1], datt_far[1], qkv, probs],
        wqo,
        parts,
        (a_columns, o),
        (whole(D), whole(3 * heads), (D // 2, 4 * heads)),
    )
    up_one, up_two = add_terms("g_upA_sum", [g_up[0], *up_far], 2)
    down_two, up_one, up_two, ff_got, datt, dqkv, da, att_send, g_up, g_down = sync(
        down_two, up_one, up_two, ff_got, datt, dqkv, da, att_send, g_up, g_down
    )

    da_got = links.send_late(da, "da")
    att_sent = links.from_core(att_send, "g_att")
    up_one = links.send_h(up_one, 1, "g_upA")
    down_last = links.send_x(g_down[2::3], "g_downC")
    g_att = attention_kept(nh, nd, a_columns, flat(dqkv), flat(datt), flat(o), att_sent)
    da_got, g_att, g_up, up_one, up_two, da, ff_got, down_last = sync(
        da_got, g_att, g_up, up_one, up_two, da, ff_got, down_last
    )

    att_far = links.send_x(g_att[0::2], "g_attA")
    up_two = links.send_h(up_two, 1, "g_upB")
    da_last = links.send_on(onward(da, da_got, "da_onward"), "da")
    att_one, att_two = add_terms("g_attA_sum", [g_att[0], *att_far], 2)
    att_one, att_two, up_two, da_last, g_att, g_up, ff_got = sync(
        att_one, att_two, up_two, da_last, g_att, g_up, ff_got
    )

    att_one = links.send_h(att_one, 1, "g_attA")
    up_here = links.send_x(g_up[1::2], "g_upC")
    ff_last = links.send_on(onward(ff, ff_got, "ff_onward"), "ff")
    (input_grad,) = over_images(
        first_norm_back_kernel,
        "first_norm_back",
        [stream, dr, modulation, *sums(da, da_got, da_last)],
        [(every, BF)],
    )
    g_down = jnp.concatenate(
        [
            sum(v[far:].astype(F32) for v in (g_down[1], *down_mid)),
            sum(v.astype(F32) for v in (g_down[2], *down_last)),
        ],
        axis=0,
    )
    g_down = total(g_down, joined((down_one, down_two)))
    att_one, att_two, up_here, ff_last, g_att, g_up, input_grad = sync(
        att_one, att_two, up_here, ff_last, g_att, g_up, input_grad
    )

    att_two = links.send_h(att_two, 1, "g_attB")
    att_here = links.send_x(g_att[1::2], "g_attC")
    (output,) = over_images(
        output_kernel,
        "output",
        [residual, modulation, *sums(ff, ff_got, ff_last)],
        [(every, BF)],
    )
    g_up = total(
        g_up[1].astype(F32) + sum(v.astype(F32) for v in up_here), joined((up_one, up_two))
    )
    att_two, att_here, g_att, output, input_grad = sync(
        att_two, att_here, g_att, output, input_grad
    )

    input_grad_got = links.leave_group(input_grad, "input_grad")
    att_there = joined((att_one, att_two))
    g_qkv, g_out, squares = unpack_attention_gradient(
        [g_att[1], *att_here, *att_there]
    )
    squares = jnp.sum(squares) + jnp.sum(g_up * g_up) + jnp.sum(g_down * g_down)
    grad_norm = jnp.sqrt(links.total(squares))
    grad_norm, output = sync(grad_norm, output)
    output_got = links.leave_group(output, "output")
    input_grad = links.at_home(input_grad, input_grad_got).astype(F32)
    output = links.at_home(output, output_got)
    factor = jnp.minimum(1.0, clip_limit / (grad_norm + 1e-06))
    one_qkv, two_qkv, new_qkv = (
        v.transpose(1, 0, 2)
        for v in adam_update(
            g_qkv, *(v.transpose(1, 0, 2) for v in (m_qkv, v_qkv, w_qkv)), factor, learn_rate
        )
    )
    one_out, two_out, new_out = adam_update(g_out, m_out, v_out, w_out, factor, output_rate)
    one_up, two_up, new_up = adam_update(g_up, m_up, v_up, w_up, factor, learn_rate)
    one_down, two_down, new_down = adam_update(g_down, m_down, v_down, w_down, factor, learn_rate)
    return (
        output,
        input_grad,
        grad_norm,
        one_qkv,
        one_out,
        one_up,
        one_down,
        two_qkv,
        two_out,
        two_up,
        two_down,
        new_qkv,
        new_out,
        new_up,
        new_down,
    )


def solution(mesh):
    n_dp, n_mp = mesh.shape["dp"], mesh.shape["mp"]
    links = Links(n_dp, n_mp)
    fine = Mesh(mesh.devices.reshape(links.X, 2, links.H, 2, 2), links.axes)
    dp, mp = ("x", "core"), ("h", "p", "q")
    tokens, qkv = P(dp, mp, None), P(dp, None, mp)
    rows, columns = P(mp, dp), P(dp, mp)
    weights = (qkv, rows, columns, rows)
    return jax.shard_map(
        lambda *args: per_device(links, *args),
        mesh=fine,
        in_specs=(tokens, tokens, P(), P(dp), P(dp), P(dp)) + 3 * weights,
        out_specs=(tokens, tokens, P()) + 3 * weights,
        check_vma=False,
    )
```

```python
import jax
import jax.numpy as jnp
from jax import lax
from jax.experimental import pallas as pl
from jax.experimental.pallas import tpu as pltpu
from jax.sharding import Mesh
from jax.sharding import PartitionSpec as P

HD = 128
BINS = 8
ADAM_STEP = 10

clip_limit = 1.0
beta_one = 0.9
beta_two = 0.95
learn_rate = 0.02
output_rate = 0.08
adam_epsilon = 1e-08
decay_rate = 0.01

BF = jnp.bfloat16
F32 = jnp.float32


def adam_update(gradient, moment_one, moment_two, weight, factor, step_rate):
    clipped = gradient * factor
    new_one = beta_one * moment_one + (1.0 - beta_one) * clipped
    new_two = beta_two * moment_two + (1.0 - beta_two) * clipped * clipped
    corrected = new_one / (1.0 - beta_one**ADAM_STEP)
    root_two = jnp.sqrt(new_two / (1.0 - beta_two**ADAM_STEP))
    new_weight = weight - step_rate * (corrected / (root_two + adam_epsilon) + decay_rate * weight)
    return (new_one, new_two, new_weight)


def sync(*values):
    return lax.optimization_barrier(values)


def dot(a, b, contract=(1, 0)):
    return lax.dot_general(
        a, b, (((contract[0],), (contract[1],)), ((), ())), preferred_element_type=F32
    )


def rows_of(ref, columns=slice(None)):
    value = ref[0, :, :, columns]
    return value.reshape(value.shape[0] * value.shape[1], value.shape[2])


def join_tokens(pieces, whole):
    for kind, two in enumerate(pieces):
        for r, ref in enumerate(two):
            t = ref.shape[1]
            whole[0, kind, r * t : (r + 1) * t] = ref[0]


def put_parts(value, columns, parts):
    half = value.shape[0] // (2 * len(parts))
    for kind, (keep, send) in enumerate(parts):
        keep[0, :, columns] = value[2 * kind * half : (2 * kind + 1) * half]
        send[0, :, columns] = value[(2 * kind + 1) * half : (2 * kind + 2) * half]


def softmax_rows(q, k):
    scores = dot(q, k, (1, 1)) * HD ** (-0.5)
    weights = jnp.exp(scores - jnp.max(scores, axis=-1, keepdims=True))
    return weights * (1.0 / jnp.sum(weights, axis=-1, keepdims=True))


def head_columns(jh, part, n, block):
    start = (jh * 3 + part) * block + n * HD
    return slice(start, start + HD)


class Pieces:
    def __init__(self, refs):
        self.refs, self.at = refs, 0

    def take(self, count):
        self.at += count
        return self.refs[self.at - count : self.at]

    def tokens(self):
        near_far = self.take(4)
        return near_far[:2], near_far[2:]

    def parts(self):
        a, b, c, d = self.take(4)
        return (a, b), (c, d)


class Separate:
    def __init__(self, refs, nd):
        self.refs, self.depth = refs, refs[0].shape[0]
        self.shape = refs[0].shape[1:]

    def block(self, jh, d, rows=slice(None), columns=slice(None)):
        core, x = divmod(d, self.depth)
        return self.refs[2 * jh + core][x, rows, columns]


class Merged:
    def __init__(self, refs):
        self.refs = refs
        x, rows, columns = refs[0].shape
        self.shape = (x * rows, columns)

    def block(self, jh, core, rows=slice(None), columns=slice(None)):
        value = self.refs[2 * jh + core][:, :, columns]
        return value.reshape(self.shape[0], value.shape[2])


def attention_kernel(nh, nd, *refs):
    refs = Pieces(refs)
    tokens, weights = refs.tokens(), Merged(refs.take(2 * nh))
    (a, qkv, o, probs), parts = refs.take(4), refs.parts()
    join_tokens(tokens, a)
    nd = 2
    depth, block = weights.shape[0], weights.shape[1] // 4
    width = 3 * block
    inward = (slice(None), slice(0, width))
    outward = (slice(None), slice(width, width + block))
    kinds, length = a.shape[1], a.shape[2]
    for jh in range(nh):
        total = dot(rows_of(a, slice(0, depth)), weights.block(jh, 0, *inward))
        for d in range(1, nd):
            total += dot(rows_of(a, slice(d * depth, (d + 1) * depth)), weights.block(jh, d, *inward))
        qkv[0, :, :, jh * width : (jh + 1) * width] = total.astype(BF).reshape(kinds, length, width)
    for kind in range(kinds):
        for jh in range(nh):
            for n in range(block // HD):
                q, k, v = (qkv[0, kind, :, head_columns(jh, i, n, block)] for i in range(3))
                p = softmax_rows(q, k).astype(BF)
                probs[0, kind, jh * (block // HD) + n] = p
                out = dot(p, v).astype(BF)
                o[0, kind, :, jh * block + n * HD : jh * block + (n + 1) * HD] = out
    for d in range(nd):
        total = dot(rows_of(o, slice(0, block)), weights.block(0, d, *outward), (1, 1))
        for jh in range(1, nh):
            total += dot(rows_of(o, slice(jh * block, (jh + 1) * block)), weights.block(jh, d, *outward), (1, 1))
        put_parts(total.astype(BF), slice(d * depth, (d + 1) * depth), parts)


def up_kernel(nh, nd, *refs):
    refs = Pieces(refs)
    b_tokens, wu = refs.tokens(), Merged(refs.take(2 * nh))
    b, hidden, slope = refs.take(3)
    join_tokens(b_tokens, b)
    nd = 2
    depth, width = wu.shape
    kinds, length = b.shape[1], b.shape[2]
    chunk = min(width, 512)
    curve, cubic = 0.7978845608028654, 0.044715
    for jh in range(nh):
        for c in range(0, width, chunk):
            part = slice(c, c + chunk)
            u = dot(rows_of(b, slice(0, depth)), wu.block(jh, 0, columns=part))
            for d in range(1, nd):
                cols = slice(d * depth, (d + 1) * depth)
                u += dot(rows_of(b, cols), wu.block(jh, d, columns=part))
            square = u * u
            t = jnp.tanh(curve * u * (1.0 + cubic * square))
            near = 0.5 * (1.0 + t)
            rise = near + 0.5 * u * (1.0 - t * t) * (curve * (1.0 + 3.0 * cubic * square))
            cols = slice(jh * width + c, jh * width + c + chunk)
            hidden[0, :, :, cols] = (u * near).astype(BF).reshape(kinds, length, chunk)
            slope[0, :, :, cols] = rise.astype(BF).reshape(kinds, length, chunk)


def up_back_kernel(nh, nd, *refs):
    refs = Pieces(refs)
    df_tokens, (slope,) = refs.tokens(), refs.take(1)
    wu, wd = Merged(refs.take(2 * nh)), Separate(refs.take(2 * nh), nd)
    (df, du), parts = refs.take(2), refs.parts()
    join_tokens(df_tokens, df)
    width, depth = wd.shape
    kinds, length = df.shape[1], df.shape[2]
    chunk = min(width, 512)
    for jh in range(nh):
        for c in range(0, width, chunk):
            part = slice(c, c + chunk)
            dh = dot(rows_of(df, slice(0, depth)), wd.block(jh, 0, part), (1, 1))
            for d in range(1, nd):
                cols = slice(d * depth, (d + 1) * depth)
                dh += dot(rows_of(df, cols), wd.block(jh, d, part), (1, 1))
            cols = slice(jh * width + c, jh * width + c + chunk)
            value = dh * rows_of(slope, cols).astype(F32)
            du[0, :, :, cols] = value.astype(BF).reshape(kinds, length, chunk)
    depth = wu.shape[0]
    for d in range(2):
        total = dot(rows_of(du, slice(0, width)), wu.block(0, d), (1, 1))
        for jh in range(1, nh):
            total += dot(rows_of(du, slice(jh * width, (jh + 1) * width)), wu.block(jh, d), (1, 1))
        put_parts(total.astype(BF), slice(d * depth, (d + 1) * depth), parts)


def down_kernel(nh, nd, *refs):
    refs = Pieces(refs)
    (hidden,), wd = refs.take(1), Separate(refs.take(2 * nh), nd)
    parts = refs.parts()
    width, depth = wd.shape
    for d in range(nd):
        total = dot(rows_of(hidden, slice(0, width)), wd.block(0, d))
        for jh in range(1, nh):
            total += dot(rows_of(hidden, slice(jh * width, (jh + 1) * width)), wd.block(jh, d))
        put_parts(total.astype(BF), slice(d * depth, (d + 1) * depth), parts)


def attention_back_kernel(nh, nd, *refs):
    refs = Pieces(refs)
    (a, o), tokens, (qkv, probs) = refs.take(2), refs.tokens(), refs.take(2)
    weights = Merged(refs.take(2 * nh))
    parts, (all_datt, all_dqkv, sent) = refs.parts(), refs.take(3)
    step = pl.program_id(0)
    datt, dqkv = (v.at[pl.ds(step, 1)] for v in (all_datt, all_dqkv))
    join_tokens(tokens, datt)
    nd = 2
    depth, block = weights.shape[0], weights.shape[1] // 4
    width = 3 * block
    inward = (slice(None), slice(0, width))
    outward = (slice(None), slice(width, width + block))
    kinds, length = datt.shape[1], datt.shape[2]
    for jh in range(nh):
        do_all = dot(rows_of(datt, slice(0, depth)), weights.block(jh, 0, *outward))
        for d in range(1, nd):
            do_all += dot(rows_of(datt, slice(d * depth, (d + 1) * depth)), weights.block(jh, d, *outward))
        do_all = do_all.astype(BF)
        for kind in range(kinds):
            for n in range(block // HD):
                q, k, v = (qkv[0, kind, :, head_columns(jh, i, n, block)] for i in range(3))
                do = do_all[kind * length : (kind + 1) * length, n * HD : (n + 1) * HD]
                rounded = probs[0, kind, jh * (block // HD) + n]
                dv = dot(rounded, do, (0, 0))
                dp = dot(do, v, (1, 1))
                p = rounded.astype(F32)
                ds = (p * (dp - jnp.sum(p * dp, axis=-1, keepdims=True))).astype(BF)
                dq = dot(ds, k) * HD ** (-0.5)
                dk = dot(ds, q, (0, 0)) * HD ** (-0.5)
                for i, value in enumerate((dq, dk, dv)):
                    dqkv[0, kind, :, head_columns(jh, i, n, block)] = value.astype(BF)
    for d in range(nd):
        total = dot(rows_of(dqkv, slice(0, width)), weights.block(0, d, *inward), (1, 1))
        for jh in range(1, nh):
            total += dot(rows_of(dqkv, slice(jh * width, (jh + 1) * width)), weights.block(jh, d, *inward), (1, 1))
        put_parts(total.astype(BF), slice(d * depth, (d + 1) * depth), parts)
    across, both = nd // 2, width + block

    def every_row(ref, columns=slice(None)):
        value = ref[:, :, :, columns]
        return value.reshape(-1, value.shape[-1])

    @pl.when(step == pl.num_programs(0) - 1)
    def _():
        for jx in range(across):
            cols = slice((across + jx) * depth, (across + jx + 1) * depth)
            inward = dot(a[cols], every_row(all_dqkv)).astype(BF)
            outward = dot(every_row(all_datt, cols), every_row(o), (0, 0)).astype(BF)
            rows = slice(jx * depth, (jx + 1) * depth)
            for jh in range(nh):
                at = jh * both
                sent[rows, at : at + width] = inward[:, jh * width : (jh + 1) * width]
                sent[rows, at + width : at + both] = outward[:, jh * block : (jh + 1) * block]


def group_call(kernel, name, nh, nd, steps, blocked, whole, outs, resident=(), whole_outs=()):
    def cut(shape):
        zeros = (0,) * (len(shape) - 1)
        return pl.BlockSpec((1,) + tuple(shape[1:]), lambda i: (i,) + zeros)

    def stay(shape):
        zeros = (0,) * len(shape)
        return pl.BlockSpec(tuple(shape), lambda i: zeros)

    return pl.pallas_call(
        lambda *refs: kernel(nh, nd, *refs),
        name=name,
        grid=(steps,),
        in_specs=[stay(v.shape) for v in resident]
        + [cut(v.shape) for v in blocked]
        + [pl.BlockSpec(memory_space=pltpu.VMEM)] * len(whole),
        out_specs=[cut(s) for s in outs] + [stay(s) for s in whole_outs],
        out_shape=[jax.ShapeDtypeStruct(s, BF) for s in (*outs, *whole_outs)],
        compiler_params=pltpu.CompilerParams(vmem_limit_bytes=62 * 2**20),
        cost_estimate=pl.CostEstimate(flops=0, bytes_accessed=0, transcendentals=0),
    )(*resident, *blocked, *whole)


def image_call(kernel, name, steps, arrays, outs):
    def seen(shape):
        return (2, steps, *shape[1:]) if shape[0] == 2 * steps else tuple(shape)

    def cut(shape):
        zeros = (0,) * (len(shape) - 2)
        if shape[0] == 2 and len(shape) == 4:
            return pl.BlockSpec((2, 1, *shape[2:]), lambda i: (0, i, *zeros))
        return pl.BlockSpec((1, *shape[1:]), lambda i: (i, 0, *zeros))

    made = pl.pallas_call(
        kernel,
        name=name,
        grid=(steps,),
        in_specs=[cut(seen(v.shape)) for v in arrays],
        out_specs=[cut(seen(shape)) for shape, _ in outs],
        out_shape=[jax.ShapeDtypeStruct(seen(shape), dtype) for shape, dtype in outs],
        compiler_params=pltpu.CompilerParams(vmem_limit_bytes=32 * 2**20),
        cost_estimate=pl.CostEstimate(flops=0, bytes_accessed=0, transcendentals=0),
    )(*[v.reshape(seen(v.shape)) for v in arrays])
    return [v.reshape(shape) for v, (shape, _) in zip(made, outs)]


def move_call(kernel, name, table, arrays, outs):
    def whole(shape):
        zeros = (0,) * len(shape)
        return pl.BlockSpec(tuple(shape), lambda i, table: zeros)

    return pl.pallas_call(
        kernel,
        name=name,
        grid_spec=pltpu.PrefetchScalarGridSpec(
            num_scalar_prefetch=1,
            grid=(1,),
            in_specs=[whole(v.shape) for v in arrays],
            out_specs=[whole(shape) for shape, _ in outs],
        ),
        out_shape=[jax.ShapeDtypeStruct(shape, dtype) for shape, dtype in outs],
        compiler_params=pltpu.CompilerParams(vmem_limit_bytes=32 * 2**20),
        cost_estimate=pl.CostEstimate(flops=0, bytes_accessed=0, transcendentals=0),
    )(table, *arrays)


def leave_home(name, table, groups, v):
    slots, t, D = v.shape
    blocks, images = table.shape[0] - groups, slots // groups
    width = D // blocks

    def kernel(table, v, *outs):
        for jh in range(groups):
            picked = pl.ds(table[jh] * images, images)
            for e in range(blocks):
                columns = pl.ds(pl.multiple_of(table[groups + e] * width, width), width)
                outs[jh][:, :, e * width : (e + 1) * width] = v[picked, :, columns].astype(BF)

    return move_call(kernel, name, table, [v], [((images, t, D), BF)] * groups)


def come_home(name, table, groups, own, received, dtype):
    images, length, D = own.shape
    blocks, t = table.shape[0] - groups, length // groups
    width = D // blocks

    def kernel(table, own, *refs):
        *received, out = refs
        for jh in range(groups):
            picked = pl.ds(table[jh] * images, images)
            for e in range(blocks):
                columns = pl.ds(pl.multiple_of(table[groups + e] * width, width), width)
                part = received[jh - 1][:, :, columns] if jh else own[:, :t, columns]
                out[picked, :, e * width : (e + 1) * width] = part.astype(dtype)

    shape = (images * groups, t, D)
    return move_call(kernel, name, table, [own, *received], [(shape, dtype)])[0]


def row_parts(values):
    center = values - jnp.mean(values, axis=-1, keepdims=True)
    factor = lax.rsqrt(jnp.mean(center * center, axis=-1, keepdims=True) + 1e-06)
    return center * factor, factor


def norm_back(values, gradient):
    rows, factor = row_parts(values)
    return factor * (
        gradient
        - jnp.mean(gradient, axis=-1, keepdims=True)
        - rows * jnp.mean(gradient * rows, axis=-1, keepdims=True)
    )


def token_sum(sums, kind):
    keep, got, last = sums[kind], sums[2 + kind], sums[4 + kind]
    t = last.shape[1]
    return keep[0, :t].astype(F32) + got[0, :t].astype(F32) + last[0].astype(F32)


def first_norm_kernel(stream, mod, *a):
    for kind in range(2):
        rows, _ = row_parts(stream[kind, 0].astype(F32))
        a[kind][0] = (rows * mod[kind, 0, 1:2] + mod[kind, 0, 0:1]).astype(BF)


def loss_kernel(cot, weight, mod, *df):
    for kind in range(2):
        seed = cot[kind, 0].astype(F32) * weight[kind, 0]
        df[kind][0] = (mod[kind, 0, 5:6] * seed).astype(BF)


def second_norm_kernel(stream, mod, *refs):
    sums, residual, b = refs[:6], refs[6], refs[7:]
    for kind in range(2):
        r = stream[kind, 0].astype(F32) + mod[kind, 0, 2:3] * token_sum(sums, kind)
        residual[kind, 0] = r
        rows, _ = row_parts(r)
        b[kind][0] = (rows * mod[kind, 0, 4:5] + mod[kind, 0, 3:4]).astype(BF)


def second_norm_back_kernel(cot, weight, residual, mod, *refs):
    sums, dr, datt = refs[:6], refs[6], refs[7:]
    for kind in range(2):
        seed = cot[kind, 0].astype(F32) * weight[kind, 0]
        g = seed + norm_back(residual[kind, 0], token_sum(sums, kind) * mod[kind, 0, 4:5])
        dr[kind, 0] = g
        datt[kind][0] = (mod[kind, 0, 2:3] * g).astype(BF)


def first_norm_back_kernel(stream, dr, mod, *refs):
    sums, out = refs[:6], refs[6]
    for kind in range(2):
        g = norm_back(stream[kind, 0].astype(F32), token_sum(sums, kind) * mod[kind, 0, 1:2])
        out[kind, 0] = (dr[kind, 0] + g).astype(BF)


def output_kernel(residual, mod, *refs):
    sums, out = refs[:6], refs[6]
    for kind in range(2):
        out[kind, 0] = (residual[kind, 0] + mod[kind, 0, 5:6] * token_sum(sums, kind)).astype(BF)


def rounded(weights):
    def kernel(*refs):
        for source, copy in zip(refs[: len(weights)], refs[len(weights) :]):
            copy[...] = source[...].astype(BF)

    halves = [pl.BlockSpec((v.shape[0] // 2, v.shape[1]), lambda i: (i, 0)) for v in weights]
    return pl.pallas_call(
        kernel,
        name="rounded",
        grid=(2,),
        in_specs=halves,
        out_specs=halves,
        out_shape=[jax.ShapeDtypeStruct(v.shape, BF) for v in weights],
        compiler_params=pltpu.CompilerParams(vmem_limit_bytes=32 * 2**20),
        cost_estimate=pl.CostEstimate(flops=0, bytes_accessed=0, transcendentals=0),
    )(*weights)


def pack_attention_weights(w_qkv, w_out):
    depth, _, block = w_qkv.shape

    def kernel(inward, outward, packed):
        for i in range(3):
            packed[:, i * block : (i + 1) * block] = inward[i].astype(BF)
        packed[:, 3 * block :] = outward[...].T.astype(BF)

    return pl.pallas_call(
        kernel,
        name="pack",
        out_shape=jax.ShapeDtypeStruct((depth, 4 * block), BF),
        compiler_params=pltpu.CompilerParams(vmem_limit_bytes=32 * 2**20),
        cost_estimate=pl.CostEstimate(flops=0, bytes_accessed=0, transcendentals=0),
    )(w_qkv.transpose(1, 0, 2), w_out)


def gradient(name, nh, nd, left, right, left_is_hidden, core):
    rows = left.shape[0]
    hidden, features = (left, right) if left_is_hidden else (right, left)
    h_width, d_width, half = hidden.shape[1] // nh, features.shape[1] // nd, nd // 2

    def kernel(left, right, out):
        out[...] = dot(left[...], right[...], (0, 0)).astype(BF)

    h_spec = pl.BlockSpec((rows, h_width), lambda jh, d: (0, jh))
    d_spec = pl.BlockSpec((rows, d_width), lambda jh, d: (0, core * half + d))
    if left_is_hidden:
        in_specs, out_spec = [h_spec, d_spec], pl.BlockSpec((h_width, d_width), lambda jh, d: (jh, d))
        shape = (nh * h_width, half * d_width)
    else:
        in_specs, out_spec = [d_spec, h_spec], pl.BlockSpec((d_width, h_width), lambda jh, d: (d, jh))
        shape = (half * d_width, nh * h_width)
    return pl.pallas_call(
        kernel,
        name=name,
        grid=(nh, half),
        in_specs=in_specs,
        out_specs=out_spec,
        out_shape=jax.ShapeDtypeStruct(shape, BF),
        compiler_params=pltpu.CompilerParams(vmem_limit_bytes=48 * 2**20),
        cost_estimate=pl.CostEstimate(flops=0, bytes_accessed=0, transcendentals=0),
    )(left, right)


def one_step(kernel, name, arrays, columns, outs, dtype=BF):
    return pl.pallas_call(
        kernel,
        name=name,
        grid=(1,),
        in_specs=[
            pl.BlockSpec((v.shape[0], c or v.shape[1]), lambda i: (0, 0))
            for v, c in zip(arrays, columns)
        ],
        out_specs=[pl.BlockSpec(shape, lambda i: (0, 0)) for shape in outs],
        out_shape=[jax.ShapeDtypeStruct(shape, dtype) for shape in outs],
        compiler_params=pltpu.CompilerParams(vmem_limit_bytes=60 * 2**20),
        cost_estimate=pl.CostEstimate(flops=0, bytes_accessed=0, transcendentals=0),
    )(*arrays)


def down_kept(nh, nd, hidden, df, sent):
    half = nd // 2
    height, width = hidden.shape[1] // nh, df.shape[1] // nd
    cut = height // 2

    def kernel(hidden, df, sent, *outs):
        for jx in range(half):
            one, two, three = outs[3 * jx : 3 * jx + 3]
            cols = slice(jx * width, (jx + 1) * width)
            for jh in range(nh):
                rows = slice(jh * height, (jh + 1) * height)
                g = dot(hidden[:, rows], df[:, cols], (0, 0)) + sent[rows, cols].astype(F32)
                g = g.astype(BF)
                if jh:
                    one[(jh - 1) * cut : jh * cut] = g[:cut]
                    two[(jh - 1) * cut : jh * cut] = g[cut:]
                else:
                    two[(nh - 1) * cut :] = g[:cut]
                    three[...] = g[cut:]

    shapes = [((nh - 1) * cut, width), (nh * cut, width), (cut, width)] * half
    return one_step(kernel, "g_down_keep", (hidden, df, sent), (None, half * width, None), shapes)


def up_kept(nh, nd, b, du, sent):
    half = nd // 2
    height, width = b.shape[1] // nd, du.shape[1] // nh

    def kernel(b, du, sent, *outs):
        for jx in range(half):
            far, here = outs[2 * jx : 2 * jx + 2]
            rows = slice(jx * height, (jx + 1) * height)
            for jh in range(nh):
                cols = slice(jh * width, (jh + 1) * width)
                g = dot(b[:, rows], du[:, cols], (0, 0)) + sent[rows, cols].astype(F32)
                if jh:
                    far[:, (jh - 1) * width : jh * width] = g.astype(BF)
                else:
                    here[...] = g.astype(BF)

    shapes = [(height, (nh - 1) * width), (height, width)] * half
    return one_step(kernel, "g_up_keep", (b, du, sent), (half * height, None, None), shapes)


def attention_kept(nh, nd, a, dqkv, datt, o, sent):
    half = nd // 2
    height = a.shape[0] // nd
    width, block = dqkv.shape[1] // nh, o.shape[1] // nh
    both = width + block

    def kernel(a, dqkv, datt, o, sent, *outs):
        for jx in range(half):
            far, here = outs[2 * jx : 2 * jx + 2]
            rows = slice(jx * height, (jx + 1) * height)
            inward = dot(a[rows], dqkv[...])
            outward = dot(datt[:, rows], o[...], (0, 0))
            for jh in range(nh):
                out, at = (far, (jh - 1) * both) if jh else (here, 0)
                terms = sent[rows, jh * both : (jh + 1) * both].astype(F32)
                g = inward[:, jh * width : (jh + 1) * width] + terms[:, :width]
                out[:, at : at + width] = g.astype(BF)
                g = outward[:, jh * block : (jh + 1) * block] + terms[:, width:]
                out[:, at + width : at + both] = g.astype(BF)

    shapes = [(height, (nh - 1) * both), (height, both)] * half
    cols = half * height
    return one_step(
        kernel, "g_att_keep", (a, dqkv, datt, o, sent), (None, None, cols, None, None), shapes
    )


def add_terms(name, terms, cuts=1, rows=None):
    rows, width = rows or terms[0].shape[0], terms[0].shape[1]
    size = rows // cuts

    def kernel(*refs):
        terms, outs = refs[: len(refs) - cuts], refs[len(refs) - cuts :]
        for c, out in enumerate(outs):
            out[...] = sum(
                v[c * size : (c + 1) * size].astype(F32) for v in terms
            ).astype(BF)

    return one_step(kernel, name, terms, [None] * len(terms), [(size, width)] * cuts)


def onward_kernel(*refs):
    for kind in range(2):
        keep, got, out = refs[kind], refs[2 + kind], refs[4 + kind]
        t = out.shape[1]
        out[0] = (keep[0, t:].astype(F32) + got[0, t:].astype(F32)).astype(BF)


def unpack_attention_gradient(terms):
    depth, width = terms[0].shape
    block = width // 4

    def kernel(*refs):
        *terms, inward, outward, squares = refs
        total = sum(v[...].astype(F32) for v in terms)
        square = total * total
        squares[...] = sum(
            jnp.sum(square[:, c : c + 128].reshape(depth // 8, 8, 128), axis=0)
            for c in range(0, width, 128)
        )
        for i in range(3):
            inward[i] = total[:, i * block : (i + 1) * block]
        outward[...] = total[:, 3 * block :].T

    return pl.pallas_call(
        kernel,
        name="unpack",
        out_shape=[
            jax.ShapeDtypeStruct((3, depth, block), F32),
            jax.ShapeDtypeStruct((block, depth), F32),
            jax.ShapeDtypeStruct((8, 128), F32),
        ],
        compiler_params=pltpu.CompilerParams(vmem_limit_bytes=32 * 2**20),
        cost_estimate=pl.CostEstimate(flops=0, bytes_accessed=0, transcendentals=0),
    )(*terms)


class Links:
    axes = ("x", "core", "h", "p", "q")

    def __init__(self, n_dp, n_mp):
        self.X, self.H = n_dp // 2, n_mp // 4
        self.n_dp, self.n_mp = n_dp, n_mp

    def shifted(self, v, axis, size, offset, name):
        with jax.named_scope(f"{name}_{axis}"):
            return lax.ppermute(v, axis, [((dst + offset) % size, dst) for dst in range(size)])

    def from_core(self, v, name):
        return self.shifted(v, "core", 2, 1, name)

    def from_x(self, v, jx, name):
        return self.shifted(v, "x", self.X, jx, name)

    def from_h(self, v, jh, name):
        return self.shifted(v, "h", self.H, jh, name)

    def over_h(self, w, name):
        return [self.from_h(w, jh, name) for jh in range(1, self.H)]

    def over_x(self, w, name):
        return [self.from_x(w, jx, name) for jx in range(1, self.X)]

    def send_x(self, parts, name):
        return [self.from_x(parts[jx], -jx, name) for jx in range(1, self.X)]

    def send_h(self, g, h, name):
        width = g.shape[h] // (self.H - 1)
        return [
            self.from_h(lax.slice_in_dim(g, (jh - 1) * width, jh * width, axis=h), -jh, name)
            for jh in range(1, self.H)
        ]

    def tables(self):
        x, core, h = (lax.axis_index(axis) for axis in self.axes[:3])
        groups = [(h - jh) % self.H for jh in range(self.H)]
        here = [
            ((x + jx) % self.X) * 2 + (core ^ jc) for jc in range(2) for jx in range(self.X)
        ]
        home = [((e % 2) ^ core) * self.X + (e // 2 - x) % self.X for e in range(self.n_dp)]
        return [jnp.stack(groups + rest).astype(jnp.int32) for rest in (here, home)]

    def to_group(self, parts, name):
        return [self.from_h(parts[jh], jh, name) for jh in range(1, self.H)]

    def leave_group(self, v, name):
        tokens = v.shape[1] // self.H
        return [
            self.from_h(v[:, jh * tokens : (jh + 1) * tokens], -jh, name) for jh in range(1, self.H)
        ]

    def over(self, v, kind, late, name):
        return self.shifted(v, "p" if (kind == 0) != late else "q", 2, 1, f"{name}{kind}")

    def first_hop(self, own, name):
        return [(own[k], self.over(own[k], k, False, name)) for k in range(2)]

    def near(self, hops):
        return [jnp.concatenate(pair, axis=1) for pair in hops]

    def last_hop(self, near, name):
        return [self.over(near[k], k, True, name) for k in range(2)]

    def send_late(self, parts, name):
        return [self.over(parts[2 * k + 1], k, True, name) for k in range(2)]

    def send_on(self, onward, name):
        return [self.over(onward[k], k, False, name) for k in range(2)]

    def features_here(self, v):
        x, c = lax.axis_index("x"), lax.axis_index("core")
        width = v.shape[-1] // self.n_dp
        return jnp.concatenate(
            [
                lax.dynamic_slice_in_dim(
                    v, (((x + jx) % self.X) * 2 + (c ^ jc)) * width, width, axis=v.ndim - 1
                )
                for jc in range(2)
                for jx in range(self.X)
            ],
            axis=-1,
        )

    def total(self, v):
        for axis, size in (("core", 2), ("q", 2), ("x", self.X), ("p", 2), ("h", self.H)):
            step = 1
            while step < size:
                with jax.named_scope("norm"):
                    v = v + lax.ppermute(v, axis, [(i ^ step, i) for i in range(size)])
                step *= 2
        return v


def per_device(
    links,
    stream_in,
    cotangent,
    noise_table,
    timesteps,
    bins,
    counts,
    w_qkv,
    w_out,
    w_up,
    w_down,
    m_qkv,
    m_out,
    m_up,
    m_down,
    v_qkv,
    v_out,
    v_up,
    v_down,
):
    H = links.H
    slots, _, D = stream_in.shape
    images = slots // H
    here = lax.axis_index("h")

    steps_here = lax.dynamic_slice_in_dim(timesteps, here * images, images)
    table_rows = noise_table.shape[0]
    picks = (steps_here[:, None] == jnp.arange(table_rows)[None, :]).astype(F32)
    modulation = jnp.dot(
        picks, noise_table.reshape(table_rows, -1), precision=lax.Precision.HIGHEST
    ).reshape(images, 6, D)
    modulation = links.features_here(modulation)
    live = jnp.arange(slots) < counts[0]
    loss_scale = live.astype(F32) * (bins.astype(F32) + 1.0) / BINS
    loss_scale = lax.dynamic_slice_in_dim(loss_scale, here * images, images)
    loss_scale = jnp.broadcast_to(loss_scale[:, None, None], (images, 1, D))

    block = w_qkv.shape[2]
    length = stream_in.shape[1] * H * 4
    steps = images // 2
    rows = images * length
    nh, nd = H, 2 * links.X
    heads = H * block
    hidden_width = H * w_up.shape[1]
    whole = lambda width: (steps, 2, length, width)
    parts = [(steps, length // 2, D)] * 4

    tokens = length // 4
    every, kinds = (images, tokens, D), [((steps, tokens, D), BF)] * 2

    def over_images(kernel, name, arrays, outs):
        return image_call(kernel, name, steps, arrays, outs)

    def onward(parts, got, name):
        arrays = [parts[0], parts[2], *got]
        return over_images(onward_kernel, name, arrays, kinds)

    def sums(parts, got, last):
        return [parts[0], parts[2], *got, *last]

    def flat(v):
        return v.reshape(rows, v.shape[-1])

    def call(kernel, name, blocked, weights, outs, resident=(), whole_outs=()):
        return list(
            group_call(kernel, name, nh, nd, steps, blocked, weights, outs, resident, whole_outs)
        )

    def halves(w):
        size = w.shape[0] // 2
        return w[:size], w[size:]

    def joined(pair):
        return [jnp.concatenate(two, axis=0) for two in zip(*pair)]

    def total(here, there):
        return here + sum(v.astype(F32) for v in there)

    leave, come = links.tables()
    stream_parts = leave_home("stream_leaves", leave, H, stream_in)
    packed = pack_attention_weights(w_qkv, w_out)
    stream_got = links.to_group(stream_parts, "stream")
    x_packed = links.over_x(packed, "wqo0")
    up, down = rounded([w_up, w_down])
    stream_parts, stream_got, x_packed, packed, up, down = sync(
        stream_parts, stream_got, x_packed, packed, up, down
    )

    stream = jnp.concatenate([stream_parts[0], *stream_got], axis=1)
    a_own = over_images(first_norm_kernel, "first_norm", [stream, modulation], kinds)
    a_hops = links.first_hop(a_own, "a")
    packed_one, packed_two = halves(packed)
    far_one = links.over_h(packed_one, "wqoA")
    x_up = links.over_x(up, "wu0")
    wqo = [jnp.stack([packed, *x_packed])]
    a_near, far_one, x_up, wqo, packed_two = sync(
        links.near(a_hops), far_one, x_up, wqo, packed_two
    )

    a_far = links.last_hop(a_near, "a")
    far_two = links.over_h(packed_two, "wqoB")
    x_one = [links.over_x(w, "wqoA1") for w in far_one]
    cot_parts = leave_home("cot_leaves", leave, H, cotangent)
    cot_one = [v[:steps] for v in cot_parts]
    cot_two = [v[steps:] for v in cot_parts]
    wu = [jnp.stack([up, *x_up])]
    a_far, far_two, x_one, cot_one, cot_two, wqo, wu = sync(
        a_far, far_two, x_one, cot_one, cot_two, wqo, wu
    )

    x_two = [links.over_x(w, "wqoB1") for w in far_two]
    cot_one = [cot_one[0], *links.to_group(cot_one, "cotA")]
    wqo.append(links.from_core(wqo[0], "wqo0"))
    wu.append(links.from_core(wu[0], "wu0"))
    packed_far = joined((far_one, far_two))
    packed_far, x_two, cot_one, cot_two, wqo, wu = sync(
        packed_far, x_two, cot_one, cot_two, wqo, wu
    )

    cot_two = [cot_two[0], *links.to_group(cot_two, "cotB")]
    for w, one, two in zip(packed_far, x_one, x_two):
        wqo.append(jnp.stack([w, *joined((one, two))]))
        wqo.append(links.from_core(wqo[-1], "wqo1"))
    up_one, up_two = halves(up)
    cot_one, cot_two, wqo, up_one, up_two, down = sync(cot_one, cot_two, wqo, up_one, up_two, down)

    cot = jnp.concatenate([jnp.concatenate(v, axis=1) for v in (cot_one, cot_two)], axis=0)
    df_own = over_images(loss_kernel, "loss", [cot, loss_scale, modulation], kinds)
    df_near = links.near(links.first_hop(df_own, "df"))
    up_one = links.over_h(up_one, "wuA")
    x_down = links.over_x(down, "wd0")
    a_rows, qkv, o, probs, *att = call(
        attention_kernel,
        "attention",
        [a_near[0], a_far[0], a_near[1], a_far[1]],
        wqo,
        [whole(D), whole(3 * heads), whole(heads), (steps, 2, heads // HD, length, length), *parts],
    )
    df_near, att, up_one, up_two, x_down = sync(df_near, att, up_one, up_two, x_down)

    att_got = links.send_late(att, "att")
    up_two = links.over_h(up_two, "wuB")
    wd = [jnp.stack([down, *x_down])]
    wd.append(links.from_core(wd[0], "wd0"))
    att_got, up_two, wd, down = sync(att_got, up_two, wd, down)

    att_last = links.send_on(onward(att, att_got, "att_onward"), "att")
    down_one, down_two = halves(down)
    down_one = links.over_h(down_one, "wdA")
    up_far = joined((up_one, up_two))
    x_up = [links.over_x(w, "wu1") for w in up_far]
    residual, *b = over_images(
        second_norm_kernel,
        "second_norm",
        [stream, modulation, *sums(att, att_got, att_last)],
        [(every, F32), *kinds],
    )
    b, down_one, up_far, x_up, down_two = sync(b, down_one, up_far, x_up, down_two)

    b_hops = links.first_hop(b, "b")
    down_two = links.over_h(down_two, "wdB")
    x_one = [links.over_x(w, "wdA1") for w in down_one]
    wu_far = [jnp.stack([w, *others]) for w, others in zip(up_far, x_up)]
    b_near, down_two, x_one, wu_far = sync(links.near(b_hops), down_two, x_one, wu_far)

    b_far = links.last_hop(b_near, "b")
    x_two = [links.over_x(w, "wdB1") for w in down_two]
    for w in wu_far:
        wu += [w, links.from_core(w, "wu1")]
    b_far, x_two, wu, df_near = sync(b_far, x_two, wu, df_near)

    df_far = links.last_hop(df_near, "df")
    for w, one, two in zip(joined((down_one, down_two)), x_one, x_two):
        wd.append(jnp.stack([w, *joined((one, two))]))
        wd.append(links.from_core(wd[-1], "wd1"))
    b_rows, hidden, slope = call(
        up_kernel,
        "up",
        [b_near[0], b_far[0], b_near[1], b_far[1]],
        wu,
        [whole(D), whole(hidden_width), whole(hidden_width)],
    )
    df_far, wd, b_rows, hidden, slope = sync(df_far, wd, b_rows, hidden, slope)

    df_rows, du, *db = call(
        up_back_kernel,
        "up_back",
        [df_near[0], df_far[0], df_near[1], df_far[1], slope],
        wu + wd,
        [whole(D), whole(hidden_width), *parts],
    )
    b_rows, df_rows, hidden, du, db, a_rows = sync(b_rows, df_rows, hidden, du, db, a_rows)

    db_got = links.send_late(db, "db")
    down_send = gradient("g_down_send", nh, nd, flat(hidden), flat(df_rows), True, 1)
    up_send = gradient("g_up_send", nh, nd, flat(b_rows), flat(du), False, 1)
    a_columns = flat(a_rows).T
    db_got, down_send, up_send, b_rows, du, hidden, df_rows, a_columns = sync(
        db_got, down_send, up_send, b_rows, du, hidden, df_rows, a_columns
    )

    db_last = links.send_on(onward(db, db_got, "db_onward"), "db")
    down_sent = links.from_core(down_send, "g_down")
    g_down = down_kept(nh, nd, flat(hidden), flat(df_rows), down_sent)
    db_last, g_down, up_send, b_rows, du, hidden = sync(
        db_last, g_down, up_send, b_rows, du, hidden
    )

    dr, *datt_own = over_images(
        second_norm_back_kernel,
        "second_norm_back",
        [cot, loss_scale, residual, modulation, *sums(db, db_got, db_last)],
        [(every, F32), *kinds],
    )
    datt_hops = links.first_hop(datt_own, "datt")
    down_one = links.send_x(g_down[0::3], "g_downA")
    up_sent = links.from_core(up_send, "g_up")
    (down_one,) = add_terms("g_downA_sum", [g_down[0], *down_one])
    datt_near, g_down, down_one, up_sent, b_rows, du, hidden = sync(
        links.near(datt_hops), g_down, down_one, up_sent, b_rows, du, hidden
    )

    datt_far = links.last_hop(datt_near, "datt")
    down_one = links.send_h(down_one, 0, "g_downA")
    down_mid = links.send_x(g_down[1::3], "g_downB")
    ff = call(down_kernel, "down", [hidden], wd, parts)
    g_up = up_kept(nh, nd, flat(b_rows), flat(du), up_sent)
    far = (nh - 1) * (g_down[1].shape[0] // nh)
    (down_two,) = add_terms("g_downB_sum", [g_down[1], *down_mid], 1, far)
    datt_far, down_one, down_mid, down_two, g_down, g_up, ff = sync(
        datt_far, down_one, down_mid, down_two, g_down, g_up, ff
    )

    down_two = links.send_h(down_two, 0, "g_downB")
    up_far = links.send_x(g_up[0::2], "g_upA")
    ff_got = links.send_late(ff, "ff")
    *da, datt, dqkv, att_send = call(
        attention_back_kernel,
        "attention_back",
        [datt_near[0], datt_far[0], datt_near[1], datt_far[1], qkv, probs],
        wqo,
        parts,
        (a_columns, o),
        (whole(D), whole(3 * heads), (D // 2, 4 * heads)),
    )
    up_one, up_two = add_terms("g_upA_sum", [g_up[0], *up_far], 2)
    down_two, up_one, up_two, ff_got, datt, dqkv, da, att_send, g_up, g_down = sync(
        down_two, up_one, up_two, ff_got, datt, dqkv, da, att_send, g_up, g_down
    )

    da_got = links.send_late(da, "da")
    att_sent = links.from_core(att_send, "g_att")
    up_one = links.send_h(up_one, 1, "g_upA")
    down_last = links.send_x(g_down[2::3], "g_downC")
    g_att = attention_kept(nh, nd, a_columns, flat(dqkv), flat(datt), flat(o), att_sent)
    da_got, g_att, g_up, up_one, up_two, da, ff_got, down_last = sync(
        da_got, g_att, g_up, up_one, up_two, da, ff_got, down_last
    )

    att_far = links.send_x(g_att[0::2], "g_attA")
    up_two = links.send_h(up_two, 1, "g_upB")
    da_last = links.send_on(onward(da, da_got, "da_onward"), "da")
    att_one, att_two = add_terms("g_attA_sum", [g_att[0], *att_far], 2)
    att_one, att_two, up_two, da_last, g_att, g_up, ff_got = sync(
        att_one, att_two, up_two, da_last, g_att, g_up, ff_got
    )

    att_one = links.send_h(att_one, 1, "g_attA")
    up_here = links.send_x(g_up[1::2], "g_upC")
    ff_last = links.send_on(onward(ff, ff_got, "ff_onward"), "ff")
    (input_grad,) = over_images(
        first_norm_back_kernel,
        "first_norm_back",
        [stream, dr, modulation, *sums(da, da_got, da_last)],
        [(every, BF)],
    )
    g_down = jnp.concatenate(
        [
            sum(v[far:].astype(F32) for v in (g_down[1], *down_mid)),
            sum(v.astype(F32) for v in (g_down[2], *down_last)),
        ],
        axis=0,
    )
    g_down = total(g_down, joined((down_one, down_two)))
    att_one, att_two, up_here, ff_last, g_att, g_up, input_grad = sync(
        att_one, att_two, up_here, ff_last, g_att, g_up, input_grad
    )

    att_two = links.send_h(att_two, 1, "g_attB")
    att_here = links.send_x(g_att[1::2], "g_attC")
    (output,) = over_images(
        output_kernel,
        "output",
        [residual, modulation, *sums(ff, ff_got, ff_last)],
        [(every, BF)],
    )
    g_up = total(
        g_up[1].astype(F32) + sum(v.astype(F32) for v in up_here), joined((up_one, up_two))
    )
    att_two, att_here, g_att, output, input_grad = sync(
        att_two, att_here, g_att, output, input_grad
    )

    input_grad_got = links.leave_group(input_grad, "input_grad")
    att_there = joined((att_one, att_two))
    g_qkv, g_out, squares = unpack_attention_gradient(
        [g_att[1], *att_here, *att_there]
    )
    squares = jnp.sum(squares) + jnp.sum(g_up * g_up) + jnp.sum(g_down * g_down)
    grad_norm = jnp.sqrt(links.total(squares))
    grad_norm, output = sync(grad_norm, output)
    output_got = links.leave_group(output, "output")
    input_grad = come_home("input_grad_home", come, H, input_grad, input_grad_got, F32)
    output = come_home("output_home", come, H, output, output_got, BF)
    factor = jnp.minimum(1.0, clip_limit / (grad_norm + 1e-06))
    one_qkv, two_qkv, new_qkv = (
        v.transpose(1, 0, 2)
        for v in adam_update(
            g_qkv, *(v.transpose(1, 0, 2) for v in (m_qkv, v_qkv, w_qkv)), factor, learn_rate
        )
    )
    one_out, two_out, new_out = adam_update(g_out, m_out, v_out, w_out, factor, output_rate)
    one_up, two_up, new_up = adam_update(g_up, m_up, v_up, w_up, factor, learn_rate)
    one_down, two_down, new_down = adam_update(g_down, m_down, v_down, w_down, factor, learn_rate)
    return (
        output,
        input_grad,
        grad_norm,
        one_qkv,
        one_out,
        one_up,
        one_down,
        two_qkv,
        two_out,
        two_up,
        two_down,
        new_qkv,
        new_out,
        new_up,
        new_down,
    )


def solution(mesh):
    n_dp, n_mp = mesh.shape["dp"], mesh.shape["mp"]
    links = Links(n_dp, n_mp)
    fine = Mesh(mesh.devices.reshape(links.X, 2, links.H, 2, 2), links.axes)
    dp, mp = ("x", "core"), ("h", "p", "q")
    tokens, qkv = P(dp, mp, None), P(dp, None, mp)
    rows, columns = P(mp, dp), P(dp, mp)
    weights = (qkv, rows, columns, rows)
    return jax.shard_map(
        lambda *args: per_device(links, *args),
        mesh=fine,
        in_specs=(tokens, tokens, P(), P(dp), P(dp), P(dp)) + 3 * weights,
        out_specs=(tokens, tokens, P()) + 3 * weights,
        check_vma=False,
    )
```

```python
import jax
import jax.numpy as jnp
from jax import lax
from jax.experimental import pallas as pl
from jax.experimental.pallas import tpu as pltpu
from jax.sharding import Mesh
from jax.sharding import PartitionSpec as P

HD = 128
BINS = 8
ADAM_STEP = 10

clip_limit = 1.0
beta_one = 0.9
beta_two = 0.95
learn_rate = 0.02
output_rate = 0.08
adam_epsilon = 1e-08
decay_rate = 0.01

BF = jnp.bfloat16
F32 = jnp.float32


def adam_update(gradient, moment_one, moment_two, weight, factor, step_rate):
    clipped = gradient * factor
    new_one = beta_one * moment_one + (1.0 - beta_one) * clipped
    new_two = beta_two * moment_two + (1.0 - beta_two) * clipped * clipped
    corrected = new_one / (1.0 - beta_one**ADAM_STEP)
    root_two = jnp.sqrt(new_two / (1.0 - beta_two**ADAM_STEP))
    new_weight = weight - step_rate * (corrected / (root_two + adam_epsilon) + decay_rate * weight)
    return (new_one, new_two, new_weight)


def sync(*values):
    return lax.optimization_barrier(values)


def dot(a, b, contract=(1, 0)):
    return lax.dot_general(
        a, b, (((contract[0],), (contract[1],)), ((), ())), preferred_element_type=F32
    )


def rows_of(ref, columns=slice(None)):
    value = ref[0, :, :, columns]
    return value.reshape(value.shape[0] * value.shape[1], value.shape[2])


def join_tokens(pieces, whole):
    for kind, two in enumerate(pieces):
        for r, ref in enumerate(two):
            t = ref.shape[1]
            whole[0, kind, r * t : (r + 1) * t] = ref[0]


def put_parts(value, columns, parts):
    half = value.shape[0] // (2 * len(parts))
    for kind, (keep, send) in enumerate(parts):
        keep[0, :, columns] = value[2 * kind * half : (2 * kind + 1) * half]
        send[0, :, columns] = value[(2 * kind + 1) * half : (2 * kind + 2) * half]


def softmax_columns(q, k):
    scores = dot(k, q, (1, 1)) * HD ** (-0.5)
    weights = jnp.exp(scores - jnp.max(scores, axis=0, keepdims=True))
    return weights * (1.0 / jnp.sum(weights, axis=0, keepdims=True))


def head_columns(jh, part, n, block):
    start = (jh * 3 + part) * block + n * HD
    return slice(start, start + HD)


class Pieces:
    def __init__(self, refs):
        self.refs, self.at = refs, 0

    def take(self, count):
        self.at += count
        return self.refs[self.at - count : self.at]

    def tokens(self):
        near_far = self.take(4)
        return near_far[:2], near_far[2:]

    def parts(self):
        a, b, c, d = self.take(4)
        return (a, b), (c, d)


class Separate:
    def __init__(self, refs, nd):
        self.refs, self.depth = refs, refs[0].shape[0]
        self.shape = refs[0].shape[1:]

    def block(self, jh, d, rows=slice(None), columns=slice(None)):
        core, x = divmod(d, self.depth)
        return self.refs[2 * jh + core][x, rows, columns]


class Merged:
    def __init__(self, refs):
        self.refs = refs
        x, rows, columns = refs[0].shape
        self.shape = (x * rows, columns)

    def block(self, jh, core, rows=slice(None), columns=slice(None)):
        value = self.refs[2 * jh + core][:, :, columns]
        return value.reshape(self.shape[0], value.shape[2])


def attention_kernel(nh, nd, *refs):
    refs = Pieces(refs)
    tokens, weights = refs.tokens(), Merged(refs.take(2 * nh))
    (a, qkv, o, probs), parts = refs.take(4), refs.parts()
    join_tokens(tokens, a)
    nd = 2
    depth, block = weights.shape[0], weights.shape[1] // 4
    width = 3 * block
    inward = (slice(None), slice(0, width))
    outward = (slice(None), slice(width, width + block))
    kinds, length = a.shape[1], a.shape[2]
    for jh in range(nh):
        total = dot(rows_of(a, slice(0, depth)), weights.block(jh, 0, *inward))
        for d in range(1, nd):
            total += dot(rows_of(a, slice(d * depth, (d + 1) * depth)), weights.block(jh, d, *inward))
        qkv[0, :, :, jh * width : (jh + 1) * width] = total.astype(BF).reshape(kinds, length, width)
    for kind in range(kinds):
        for jh in range(nh):
            for n in range(block // HD):
                q, k, v = (qkv[0, kind, :, head_columns(jh, i, n, block)] for i in range(3))
                p = softmax_columns(q, k).astype(BF)
                probs[0, kind, jh * (block // HD) + n] = p
                out = dot(p, v, (0, 0)).astype(BF)
                o[0, kind, :, jh * block + n * HD : jh * block + (n + 1) * HD] = out
    for d in range(nd):
        total = dot(rows_of(o, slice(0, block)), weights.block(0, d, *outward), (1, 1))
        for jh in range(1, nh):
            total += dot(rows_of(o, slice(jh * block, (jh + 1) * block)), weights.block(jh, d, *outward), (1, 1))
        put_parts(total.astype(BF), slice(d * depth, (d + 1) * depth), parts)


def up_kernel(nh, nd, *refs):
    refs = Pieces(refs)
    b_tokens, wu = refs.tokens(), Merged(refs.take(2 * nh))
    b, hidden, slope = refs.take(3)
    join_tokens(b_tokens, b)
    nd = 2
    depth, width = wu.shape
    kinds, length = b.shape[1], b.shape[2]
    chunk = min(width, 512)
    curve, cubic = 0.7978845608028654, 0.044715
    for jh in range(nh):
        for c in range(0, width, chunk):
            part = slice(c, c + chunk)
            u = dot(rows_of(b, slice(0, depth)), wu.block(jh, 0, columns=part))
            for d in range(1, nd):
                cols = slice(d * depth, (d + 1) * depth)
                u += dot(rows_of(b, cols), wu.block(jh, d, columns=part))
            square = u * u
            t = jnp.tanh(curve * u * (1.0 + cubic * square))
            near = 0.5 * (1.0 + t)
            rise = near + 0.5 * u * (1.0 - t * t) * (curve * (1.0 + 3.0 * cubic * square))
            cols = slice(jh * width + c, jh * width + c + chunk)
            hidden[0, :, :, cols] = (u * near).astype(BF).reshape(kinds, length, chunk)
            slope[0, :, :, cols] = rise.astype(BF).reshape(kinds, length, chunk)


def up_back_kernel(nh, nd, *refs):
    refs = Pieces(refs)
    df_tokens, (slope,) = refs.tokens(), refs.take(1)
    wu, wd = Merged(refs.take(2 * nh)), Separate(refs.take(2 * nh), nd)
    (df, du), parts = refs.take(2), refs.parts()
    join_tokens(df_tokens, df)
    width, depth = wd.shape
    kinds, length = df.shape[1], df.shape[2]
    chunk = min(width, 512)
    for jh in range(nh):
        for c in range(0, width, chunk):
            part = slice(c, c + chunk)
            dh = dot(rows_of(df, slice(0, depth)), wd.block(jh, 0, part), (1, 1))
            for d in range(1, nd):
                cols = slice(d * depth, (d + 1) * depth)
                dh += dot(rows_of(df, cols), wd.block(jh, d, part), (1, 1))
            cols = slice(jh * width + c, jh * width + c + chunk)
            value = dh * rows_of(slope, cols).astype(F32)
            du[0, :, :, cols] = value.astype(BF).reshape(kinds, length, chunk)
    depth = wu.shape[0]
    for d in range(2):
        total = dot(rows_of(du, slice(0, width)), wu.block(0, d), (1, 1))
        for jh in range(1, nh):
            total += dot(rows_of(du, slice(jh * width, (jh + 1) * width)), wu.block(jh, d), (1, 1))
        put_parts(total.astype(BF), slice(d * depth, (d + 1) * depth), parts)


def down_kernel(nh, nd, *refs):
    refs = Pieces(refs)
    (hidden,), wd = refs.take(1), Separate(refs.take(2 * nh), nd)
    parts = refs.parts()
    width, depth = wd.shape
    for d in range(nd):
        total = dot(rows_of(hidden, slice(0, width)), wd.block(0, d))
        for jh in range(1, nh):
            total += dot(rows_of(hidden, slice(jh * width, (jh + 1) * width)), wd.block(jh, d))
        put_parts(total.astype(BF), slice(d * depth, (d + 1) * depth), parts)


def attention_back_kernel(nh, nd, *refs):
    refs = Pieces(refs)
    (a, o), tokens, (qkv, probs) = refs.take(2), refs.tokens(), refs.take(2)
    weights = Merged(refs.take(2 * nh))
    parts, (all_datt, all_dqkv, sent) = refs.parts(), refs.take(3)
    step = pl.program_id(0)
    datt, dqkv = (v.at[pl.ds(step, 1)] for v in (all_datt, all_dqkv))
    join_tokens(tokens, datt)
    nd = 2
    depth, block = weights.shape[0], weights.shape[1] // 4
    width = 3 * block
    inward = (slice(None), slice(0, width))
    outward = (slice(None), slice(width, width + block))
    kinds, length = datt.shape[1], datt.shape[2]
    for jh in range(nh):
        do_all = dot(rows_of(datt, slice(0, depth)), weights.block(jh, 0, *outward))
        for d in range(1, nd):
            do_all += dot(rows_of(datt, slice(d * depth, (d + 1) * depth)), weights.block(jh, d, *outward))
        do_all = do_all.astype(BF)
        for kind in range(kinds):
            for n in range(block // HD):
                q, k, v = (qkv[0, kind, :, head_columns(jh, i, n, block)] for i in range(3))
                do = do_all[kind * length : (kind + 1) * length, n * HD : (n + 1) * HD]
                rounded = probs[0, kind, jh * (block // HD) + n]
                dv = dot(rounded, do)
                dp = dot(v, do, (1, 1))
                p = rounded.astype(F32)
                ds = (p * (dp - jnp.sum(p * dp, axis=0, keepdims=True))).astype(BF)
                dq = dot(ds, k, (0, 0)) * HD ** (-0.5)
                dk = dot(ds, q) * HD ** (-0.5)
                for i, value in enumerate((dq, dk, dv)):
                    dqkv[0, kind, :, head_columns(jh, i, n, block)] = value.astype(BF)
    for d in range(nd):
        total = dot(rows_of(dqkv, slice(0, width)), weights.block(0, d, *inward), (1, 1))
        for jh in range(1, nh):
            total += dot(rows_of(dqkv, slice(jh * width, (jh + 1) * width)), weights.block(jh, d, *inward), (1, 1))
        put_parts(total.astype(BF), slice(d * depth, (d + 1) * depth), parts)
    across, both = nd // 2, width + block

    def every_row(ref, columns=slice(None)):
        value = ref[:, :, :, columns]
        return value.reshape(-1, value.shape[-1])

    @pl.when(step == pl.num_programs(0) - 1)
    def _():
        for jx in range(across):
            cols = slice((across + jx) * depth, (across + jx + 1) * depth)
            inward = dot(a[cols], every_row(all_dqkv)).astype(BF)
            outward = dot(every_row(all_datt, cols), every_row(o), (0, 0)).astype(BF)
            rows = slice(jx * depth, (jx + 1) * depth)
            for jh in range(nh):
                at = jh * both
                sent[rows, at : at + width] = inward[:, jh * width : (jh + 1) * width]
                sent[rows, at + width : at + both] = outward[:, jh * block : (jh + 1) * block]


def group_call(kernel, name, nh, nd, steps, blocked, whole, outs, resident=(), whole_outs=()):
    def cut(shape):
        zeros = (0,) * (len(shape) - 1)
        return pl.BlockSpec((1,) + tuple(shape[1:]), lambda i: (i,) + zeros)

    def stay(shape):
        zeros = (0,) * len(shape)
        return pl.BlockSpec(tuple(shape), lambda i: zeros)

    return pl.pallas_call(
        lambda *refs: kernel(nh, nd, *refs),
        name=name,
        grid=(steps,),
        in_specs=[stay(v.shape) for v in resident]
        + [cut(v.shape) for v in blocked]
        + [pl.BlockSpec(memory_space=pltpu.VMEM)] * len(whole),
        out_specs=[cut(s) for s in outs] + [stay(s) for s in whole_outs],
        out_shape=[jax.ShapeDtypeStruct(s, BF) for s in (*outs, *whole_outs)],
        compiler_params=pltpu.CompilerParams(vmem_limit_bytes=62 * 2**20),
        cost_estimate=pl.CostEstimate(flops=0, bytes_accessed=0, transcendentals=0),
    )(*resident, *blocked, *whole)


def image_call(kernel, name, steps, arrays, outs):
    def seen(shape):
        return (2, steps, *shape[1:]) if shape[0] == 2 * steps else tuple(shape)

    def cut(shape):
        zeros = (0,) * (len(shape) - 2)
        if shape[0] == 2 and len(shape) == 4:
            return pl.BlockSpec((2, 1, *shape[2:]), lambda i: (0, i, *zeros))
        return pl.BlockSpec((1, *shape[1:]), lambda i: (i, 0, *zeros))

    made = pl.pallas_call(
        kernel,
        name=name,
        grid=(steps,),
        in_specs=[cut(seen(v.shape)) for v in arrays],
        out_specs=[cut(seen(shape)) for shape, _ in outs],
        out_shape=[jax.ShapeDtypeStruct(seen(shape), dtype) for shape, dtype in outs],
        compiler_params=pltpu.CompilerParams(vmem_limit_bytes=32 * 2**20),
        cost_estimate=pl.CostEstimate(flops=0, bytes_accessed=0, transcendentals=0),
    )(*[v.reshape(seen(v.shape)) for v in arrays])
    return [v.reshape(shape) for v, (shape, _) in zip(made, outs)]


def move_call(kernel, name, table, arrays, outs):
    def whole(shape):
        zeros = (0,) * len(shape)
        return pl.BlockSpec(tuple(shape), lambda i, table: zeros)

    return pl.pallas_call(
        kernel,
        name=name,
        grid_spec=pltpu.PrefetchScalarGridSpec(
            num_scalar_prefetch=1,
            grid=(1,),
            in_specs=[whole(v.shape) for v in arrays],
            out_specs=[whole(shape) for shape, _ in outs],
        ),
        out_shape=[jax.ShapeDtypeStruct(shape, dtype) for shape, dtype in outs],
        compiler_params=pltpu.CompilerParams(vmem_limit_bytes=32 * 2**20),
        cost_estimate=pl.CostEstimate(flops=0, bytes_accessed=0, transcendentals=0),
    )(table, *arrays)


def leave_home(name, table, groups, v):
    slots, t, D = v.shape
    blocks, images = table.shape[0] - groups, slots // groups
    width = D // blocks

    def kernel(table, v, *outs):
        for jh in range(groups):
            picked = pl.ds(table[jh] * images, images)
            for e in range(blocks):
                columns = pl.ds(pl.multiple_of(table[groups + e] * width, width), width)
                outs[jh][:, :, e * width : (e + 1) * width] = v[picked, :, columns].astype(BF)

    return move_call(kernel, name, table, [v], [((images, t, D), BF)] * groups)


def come_home(name, table, groups, own, received, dtype):
    images, length, D = own.shape
    blocks, t = table.shape[0] - groups, length // groups
    width = D // blocks

    def kernel(table, own, *refs):
        *received, out = refs
        for jh in range(groups):
            picked = pl.ds(table[jh] * images, images)
            for e in range(blocks):
                columns = pl.ds(pl.multiple_of(table[groups + e] * width, width), width)
                part = received[jh - 1][:, :, columns] if jh else own[:, :t, columns]
                out[picked, :, e * width : (e + 1) * width] = part.astype(dtype)

    shape = (images * groups, t, D)
    return move_call(kernel, name, table, [own, *received], [(shape, dtype)])[0]


def row_parts(values):
    center = values - jnp.mean(values, axis=-1, keepdims=True)
    factor = lax.rsqrt(jnp.mean(center * center, axis=-1, keepdims=True) + 1e-06)
    return center * factor, factor


def norm_back(values, gradient):
    rows, factor = row_parts(values)
    return factor * (
        gradient
        - jnp.mean(gradient, axis=-1, keepdims=True)
        - rows * jnp.mean(gradient * rows, axis=-1, keepdims=True)
    )


def token_sum(sums, kind):
    keep, got, last = sums[kind], sums[2 + kind], sums[4 + kind]
    t = last.shape[1]
    return keep[0, :t].astype(F32) + got[0, :t].astype(F32) + last[0].astype(F32)


def first_norm_kernel(stream, mod, *a):
    for kind in range(2):
        rows, _ = row_parts(stream[kind, 0].astype(F32))
        a[kind][0] = (rows * mod[kind, 0, 1:2] + mod[kind, 0, 0:1]).astype(BF)


def loss_kernel(cot, weight, mod, *df):
    for kind in range(2):
        seed = cot[kind, 0].astype(F32) * weight[kind, 0]
        df[kind][0] = (mod[kind, 0, 5:6] * seed).astype(BF)


def second_norm_kernel(stream, mod, *refs):
    sums, residual, b = refs[:6], refs[6], refs[7:]
    for kind in range(2):
        r = stream[kind, 0].astype(F32) + mod[kind, 0, 2:3] * token_sum(sums, kind)
        residual[kind, 0] = r
        rows, _ = row_parts(r)
        b[kind][0] = (rows * mod[kind, 0, 4:5] + mod[kind, 0, 3:4]).astype(BF)


def second_norm_back_kernel(cot, weight, residual, mod, *refs):
    sums, dr, datt = refs[:6], refs[6], refs[7:]
    for kind in range(2):
        seed = cot[kind, 0].astype(F32) * weight[kind, 0]
        g = seed + norm_back(residual[kind, 0], token_sum(sums, kind) * mod[kind, 0, 4:5])
        dr[kind, 0] = g
        datt[kind][0] = (mod[kind, 0, 2:3] * g).astype(BF)


def first_norm_back_kernel(stream, dr, mod, *refs):
    sums, out = refs[:6], refs[6]
    for kind in range(2):
        g = norm_back(stream[kind, 0].astype(F32), token_sum(sums, kind) * mod[kind, 0, 1:2])
        out[kind, 0] = (dr[kind, 0] + g).astype(BF)


def output_kernel(residual, mod, *refs):
    sums, out = refs[:6], refs[6]
    for kind in range(2):
        out[kind, 0] = (residual[kind, 0] + mod[kind, 0, 5:6] * token_sum(sums, kind)).astype(BF)


def rounded(weights):
    def kernel(*refs):
        for source, copy in zip(refs[: len(weights)], refs[len(weights) :]):
            copy[...] = source[...].astype(BF)

    halves = [pl.BlockSpec((v.shape[0] // 2, v.shape[1]), lambda i: (i, 0)) for v in weights]
    return pl.pallas_call(
        kernel,
        name="rounded",
        grid=(2,),
        in_specs=halves,
        out_specs=halves,
        out_shape=[jax.ShapeDtypeStruct(v.shape, BF) for v in weights],
        compiler_params=pltpu.CompilerParams(vmem_limit_bytes=32 * 2**20),
        cost_estimate=pl.CostEstimate(flops=0, bytes_accessed=0, transcendentals=0),
    )(*weights)


def pack_attention_weights(w_qkv, w_out):
    depth, _, block = w_qkv.shape

    def kernel(inward, outward, packed):
        for i in range(3):
            packed[:, i * block : (i + 1) * block] = inward[i].astype(BF)
        packed[:, 3 * block :] = outward[...].T.astype(BF)

    return pl.pallas_call(
        kernel,
        name="pack",
        out_shape=jax.ShapeDtypeStruct((depth, 4 * block), BF),
        compiler_params=pltpu.CompilerParams(vmem_limit_bytes=32 * 2**20),
        cost_estimate=pl.CostEstimate(flops=0, bytes_accessed=0, transcendentals=0),
    )(w_qkv.transpose(1, 0, 2), w_out)


def gradient(name, nh, nd, left, right, left_is_hidden, core):
    rows = left.shape[0]
    hidden, features = (left, right) if left_is_hidden else (right, left)
    h_width, d_width, half = hidden.shape[1] // nh, features.shape[1] // nd, nd // 2

    def kernel(left, right, out):
        out[...] = dot(left[...], right[...], (0, 0)).astype(BF)

    h_spec = pl.BlockSpec((rows, h_width), lambda jh, d: (0, jh))
    d_spec = pl.BlockSpec((rows, d_width), lambda jh, d: (0, core * half + d))
    if left_is_hidden:
        in_specs, out_spec = [h_spec, d_spec], pl.BlockSpec((h_width, d_width), lambda jh, d: (jh, d))
        shape = (nh * h_width, half * d_width)
    else:
        in_specs, out_spec = [d_spec, h_spec], pl.BlockSpec((d_width, h_width), lambda jh, d: (d, jh))
        shape = (half * d_width, nh * h_width)
    return pl.pallas_call(
        kernel,
        name=name,
        grid=(nh, half),
        in_specs=in_specs,
        out_specs=out_spec,
        out_shape=jax.ShapeDtypeStruct(shape, BF),
        compiler_params=pltpu.CompilerParams(vmem_limit_bytes=48 * 2**20),
        cost_estimate=pl.CostEstimate(flops=0, bytes_accessed=0, transcendentals=0),
    )(left, right)


def one_step(kernel, name, arrays, columns, outs, dtype=BF):
    return pl.pallas_call(
        kernel,
        name=name,
        grid=(1,),
        in_specs=[
            pl.BlockSpec((v.shape[0], c or v.shape[1]), lambda i: (0, 0))
            for v, c in zip(arrays, columns)
        ],
        out_specs=[pl.BlockSpec(shape, lambda i: (0, 0)) for shape in outs],
        out_shape=[jax.ShapeDtypeStruct(shape, dtype) for shape in outs],
        compiler_params=pltpu.CompilerParams(vmem_limit_bytes=60 * 2**20),
        cost_estimate=pl.CostEstimate(flops=0, bytes_accessed=0, transcendentals=0),
    )(*arrays)


def down_kept(nh, nd, hidden, df, sent):
    half = nd // 2
    height, width = hidden.shape[1] // nh, df.shape[1] // nd
    cut = height // 2

    def kernel(hidden, df, sent, *outs):
        for jx in range(half):
            one, two, three = outs[3 * jx : 3 * jx + 3]
            cols = slice(jx * width, (jx + 1) * width)
            for jh in range(nh):
                rows = slice(jh * height, (jh + 1) * height)
                g = dot(hidden[:, rows], df[:, cols], (0, 0)) + sent[rows, cols].astype(F32)
                g = g.astype(BF)
                if jh:
                    one[(jh - 1) * cut : jh * cut] = g[:cut]
                    two[(jh - 1) * cut : jh * cut] = g[cut:]
                else:
                    two[(nh - 1) * cut :] = g[:cut]
                    three[...] = g[cut:]

    shapes = [((nh - 1) * cut, width), (nh * cut, width), (cut, width)] * half
    return one_step(kernel, "g_down_keep", (hidden, df, sent), (None, half * width, None), shapes)


def up_kept(nh, nd, b, du, sent):
    half = nd // 2
    height, width = b.shape[1] // nd, du.shape[1] // nh

    def kernel(b, du, sent, *outs):
        for jx in range(half):
            far, here = outs[2 * jx : 2 * jx + 2]
            rows = slice(jx * height, (jx + 1) * height)
            for jh in range(nh):
                cols = slice(jh * width, (jh + 1) * width)
                g = dot(b[:, rows], du[:, cols], (0, 0)) + sent[rows, cols].astype(F32)
                if jh:
                    far[:, (jh - 1) * width : jh * width] = g.astype(BF)
                else:
                    here[...] = g.astype(BF)

    shapes = [(height, (nh - 1) * width), (height, width)] * half
    return one_step(kernel, "g_up_keep", (b, du, sent), (half * height, None, None), shapes)


def attention_kept(nh, nd, a, dqkv, datt, o, sent):
    half = nd // 2
    height = a.shape[0] // nd
    width, block = dqkv.shape[1] // nh, o.shape[1] // nh
    both = width + block

    def kernel(a, dqkv, datt, o, sent, *outs):
        for jx in range(half):
            far, here = outs[2 * jx : 2 * jx + 2]
            rows = slice(jx * height, (jx + 1) * height)
            inward = dot(a[rows], dqkv[...])
            outward = dot(datt[:, rows], o[...], (0, 0))
            for jh in range(nh):
                out, at = (far, (jh - 1) * both) if jh else (here, 0)
                terms = sent[rows, jh * both : (jh + 1) * both].astype(F32)
                g = inward[:, jh * width : (jh + 1) * width] + terms[:, :width]
                out[:, at : at + width] = g.astype(BF)
                g = outward[:, jh * block : (jh + 1) * block] + terms[:, width:]
                out[:, at + width : at + both] = g.astype(BF)

    shapes = [(height, (nh - 1) * both), (height, both)] * half
    cols = half * height
    return one_step(
        kernel, "g_att_keep", (a, dqkv, datt, o, sent), (None, None, cols, None, None), shapes
    )


def add_terms(name, terms, cuts=1, rows=None):
    rows, width = rows or terms[0].shape[0], terms[0].shape[1]
    size = rows // cuts

    def kernel(*refs):
        terms, outs = refs[: len(refs) - cuts], refs[len(refs) - cuts :]
        for c, out in enumerate(outs):
            out[...] = sum(
                v[c * size : (c + 1) * size].astype(F32) for v in terms
            ).astype(BF)

    return one_step(kernel, name, terms, [None] * len(terms), [(size, width)] * cuts)


def onward_kernel(*refs):
    for kind in range(2):
        keep, got, out = refs[kind], refs[2 + kind], refs[4 + kind]
        t = out.shape[1]
        out[0] = (keep[0, t:].astype(F32) + got[0, t:].astype(F32)).astype(BF)


def unpack_attention_gradient(terms):
    depth, width = terms[0].shape
    block = width // 4

    def kernel(*refs):
        *terms, inward, outward, squares = refs
        total = sum(v[...].astype(F32) for v in terms)
        square = total * total
        squares[...] = sum(
            jnp.sum(square[:, c : c + 128].reshape(depth // 8, 8, 128), axis=0)
            for c in range(0, width, 128)
        )
        for i in range(3):
            inward[i] = total[:, i * block : (i + 1) * block]
        outward[...] = total[:, 3 * block :].T

    return pl.pallas_call(
        kernel,
        name="unpack",
        out_shape=[
            jax.ShapeDtypeStruct((3, depth, block), F32),
            jax.ShapeDtypeStruct((block, depth), F32),
            jax.ShapeDtypeStruct((8, 128), F32),
        ],
        compiler_params=pltpu.CompilerParams(vmem_limit_bytes=32 * 2**20),
        cost_estimate=pl.CostEstimate(flops=0, bytes_accessed=0, transcendentals=0),
    )(*terms)


class Links:
    axes = ("x", "core", "h", "p", "q")

    def __init__(self, n_dp, n_mp):
        self.X, self.H = n_dp // 2, n_mp // 4
        self.n_dp, self.n_mp = n_dp, n_mp

    def shifted(self, v, axis, size, offset, name):
        with jax.named_scope(f"{name}_{axis}"):
            return lax.ppermute(v, axis, [((dst + offset) % size, dst) for dst in range(size)])

    def from_core(self, v, name):
        return self.shifted(v, "core", 2, 1, name)

    def from_x(self, v, jx, name):
        return self.shifted(v, "x", self.X, jx, name)

    def from_h(self, v, jh, name):
        return self.shifted(v, "h", self.H, jh, name)

    def over_h(self, w, name):
        return [self.from_h(w, jh, name) for jh in range(1, self.H)]

    def over_x(self, w, name):
        return [self.from_x(w, jx, name) for jx in range(1, self.X)]

    def send_x(self, parts, name):
        return [self.from_x(parts[jx], -jx, name) for jx in range(1, self.X)]

    def send_h(self, g, h, name):
        width = g.shape[h] // (self.H - 1)
        return [
            self.from_h(lax.slice_in_dim(g, (jh - 1) * width, jh * width, axis=h), -jh, name)
            for jh in range(1, self.H)
        ]

    def tables(self):
        x, core, h = (lax.axis_index(axis) for axis in self.axes[:3])
        groups = [(h - jh) % self.H for jh in range(self.H)]
        here = [
            ((x + jx) % self.X) * 2 + (core ^ jc) for jc in range(2) for jx in range(self.X)
        ]
        home = [((e % 2) ^ core) * self.X + (e // 2 - x) % self.X for e in range(self.n_dp)]
        return [jnp.stack(groups + rest).astype(jnp.int32) for rest in (here, home)]

    def to_group(self, parts, name):
        return [self.from_h(parts[jh], jh, name) for jh in range(1, self.H)]

    def leave_group(self, v, name):
        tokens = v.shape[1] // self.H
        return [
            self.from_h(v[:, jh * tokens : (jh + 1) * tokens], -jh, name) for jh in range(1, self.H)
        ]

    def over(self, v, kind, late, name):
        return self.shifted(v, "p" if (kind == 0) != late else "q", 2, 1, f"{name}{kind}")

    def first_hop(self, own, name):
        return [(own[k], self.over(own[k], k, False, name)) for k in range(2)]

    def near(self, hops):
        return [jnp.concatenate(pair, axis=1) for pair in hops]

    def last_hop(self, near, name):
        return [self.over(near[k], k, True, name) for k in (1, 0)][::-1]

    def send_late(self, parts, name):
        return [self.over(parts[2 * k + 1], k, True, name) for k in (1, 0)][::-1]

    def send_on(self, onward, name):
        return [self.over(onward[k], k, False, name) for k in range(2)]

    def features_here(self, v):
        x, c = lax.axis_index("x"), lax.axis_index("core")
        width = v.shape[-1] // self.n_dp
        return jnp.concatenate(
            [
                lax.dynamic_slice_in_dim(
                    v, (((x + jx) % self.X) * 2 + (c ^ jc)) * width, width, axis=v.ndim - 1
                )
                for jc in range(2)
                for jx in range(self.X)
            ],
            axis=-1,
        )

    def total(self, v):
        for axis, size in (("core", 2), ("q", 2), ("x", self.X), ("p", 2), ("h", self.H)):
            step = 1
            while step < size:
                with jax.named_scope("norm"):
                    v = v + lax.ppermute(v, axis, [(i ^ step, i) for i in range(size)])
                step *= 2
        return v


def per_device(
    links,
    stream_in,
    cotangent,
    noise_table,
    timesteps,
    bins,
    counts,
    w_qkv,
    w_out,
    w_up,
    w_down,
    m_qkv,
    m_out,
    m_up,
    m_down,
    v_qkv,
    v_out,
    v_up,
    v_down,
):
    H = links.H
    slots, _, D = stream_in.shape
    images = slots // H
    here = lax.axis_index("h")

    steps_here = lax.dynamic_slice_in_dim(timesteps, here * images, images)
    table_rows = noise_table.shape[0]
    picks = (steps_here[:, None] == jnp.arange(table_rows)[None, :]).astype(F32)
    modulation = jnp.dot(
        picks, noise_table.reshape(table_rows, -1), precision=lax.Precision.HIGHEST
    ).reshape(images, 6, D)
    modulation = links.features_here(modulation)
    live = jnp.arange(slots) < counts[0]
    loss_scale = live.astype(F32) * (bins.astype(F32) + 1.0) / BINS
    loss_scale = lax.dynamic_slice_in_dim(loss_scale, here * images, images)
    loss_scale = jnp.broadcast_to(loss_scale[:, None, None], (images, 1, D))

    block = w_qkv.shape[2]
    length = stream_in.shape[1] * H * 4
    steps = images // 2
    rows = images * length
    nh, nd = H, 2 * links.X
    heads = H * block
    hidden_width = H * w_up.shape[1]
    whole = lambda width: (steps, 2, length, width)
    parts = [(steps, length // 2, D)] * 4

    tokens = length // 4
    every, kinds = (images, tokens, D), [((steps, tokens, D), BF)] * 2

    def over_images(kernel, name, arrays, outs):
        return image_call(kernel, name, steps, arrays, outs)

    def onward(parts, got, name):
        arrays = [parts[0], parts[2], *got]
        return over_images(onward_kernel, name, arrays, kinds)

    def sums(parts, got, last):
        return [parts[0], parts[2], *got, *last]

    def flat(v):
        return v.reshape(rows, v.shape[-1])

    def call(kernel, name, blocked, weights, outs, resident=(), whole_outs=()):
        return list(
            group_call(kernel, name, nh, nd, steps, blocked, weights, outs, resident, whole_outs)
        )

    def halves(w):
        size = w.shape[0] // 2
        return w[:size], w[size:]

    def joined(pair):
        return [jnp.concatenate(two, axis=0) for two in zip(*pair)]

    def total(here, there):
        return here + sum(v.astype(F32) for v in there)

    leave, come = links.tables()
    stream_parts = leave_home("stream_leaves", leave, H, stream_in)
    packed = pack_attention_weights(w_qkv, w_out)
    stream_got = links.to_group(stream_parts, "stream")
    x_packed = links.over_x(packed, "wqo0")
    up, down = rounded([w_up, w_down])
    stream_parts, stream_got, x_packed, packed, up, down = sync(
        stream_parts, stream_got, x_packed, packed, up, down
    )

    stream = jnp.concatenate([stream_parts[0], *stream_got], axis=1)
    a_own = over_images(first_norm_kernel, "first_norm", [stream, modulation], kinds)
    a_hops = links.first_hop(a_own, "a")
    packed_one, packed_two = halves(packed)
    far_one = links.over_h(packed_one, "wqoA")
    x_up = links.over_x(up, "wu0")
    wqo = [jnp.stack([packed, *x_packed])]
    a_hops, far_one, x_up, wqo, packed_two = sync(a_hops, far_one, x_up, wqo, packed_two)
    a_near = links.near(a_hops)

    far_two = links.over_h(packed_two, "wqoB")
    a_far = links.last_hop(a_near, "a")
    x_one = [links.over_x(w, "wqoA1") for w in far_one]
    cot_parts = leave_home("cot_leaves", leave, H, cotangent)
    cot_one = [v[:steps] for v in cot_parts]
    cot_two = [v[steps:] for v in cot_parts]
    wu = [jnp.stack([up, *x_up])]
    a_far, far_two, x_one, cot_one, cot_two, wqo, wu = sync(
        a_far, far_two, x_one, cot_one, cot_two, wqo, wu
    )

    x_two = [links.over_x(w, "wqoB1") for w in far_two]
    cot_one = [cot_one[0], *links.to_group(cot_one, "cotA")]
    wqo.append(links.from_core(wqo[0], "wqo0"))
    wu.append(links.from_core(wu[0], "wu0"))
    packed_far = joined((far_one, far_two))
    packed_far, x_two, cot_one, cot_two, wqo, wu = sync(
        packed_far, x_two, cot_one, cot_two, wqo, wu
    )

    cot_two = [cot_two[0], *links.to_group(cot_two, "cotB")]
    for w, one, two in zip(packed_far, x_one, x_two):
        wqo.append(jnp.stack([w, *joined((one, two))]))
        wqo.append(links.from_core(wqo[-1], "wqo1"))
    up_one, up_two = halves(up)
    cot_one, cot_two, wqo, up_one, up_two, down = sync(cot_one, cot_two, wqo, up_one, up_two, down)

    cot = jnp.concatenate([jnp.concatenate(v, axis=1) for v in (cot_one, cot_two)], axis=0)
    df_own = over_images(loss_kernel, "loss", [cot, loss_scale, modulation], kinds)
    up_one = links.over_h(up_one, "wuA")
    df_hops = links.first_hop(df_own, "df")
    x_down = links.over_x(down, "wd0")
    a_rows, qkv, o, probs, *att = call(
        attention_kernel,
        "attention",
        [a_near[0], a_far[0], a_near[1], a_far[1]],
        wqo,
        [whole(D), whole(3 * heads), whole(heads), (steps, 2, heads // HD, length, length), *parts],
    )
    df_hops, att, up_one, up_two, x_down = sync(df_hops, att, up_one, up_two, x_down)

    up_two = links.over_h(up_two, "wuB")
    att_got = links.send_late(att, "att")
    wd = [jnp.stack([down, *x_down])]
    wd.append(links.from_core(wd[0], "wd0"))
    att_got, up_two, wd, down = sync(att_got, up_two, wd, down)

    down_one, down_two = halves(down)
    down_one = links.over_h(down_one, "wdA")
    att_last = links.send_on(onward(att, att_got, "att_onward"), "att")
    up_far = joined((up_one, up_two))
    x_up = [links.over_x(w, "wu1") for w in up_far]
    residual, *b = over_images(
        second_norm_kernel,
        "second_norm",
        [stream, modulation, *sums(att, att_got, att_last)],
        [(every, F32), *kinds],
    )
    b, down_one, up_far, x_up, down_two = sync(b, down_one, up_far, x_up, down_two)

    down_two = links.over_h(down_two, "wdB")
    b_hops = links.first_hop(b, "b")
    x_one = [links.over_x(w, "wdA1") for w in down_one]
    wu_far = [jnp.stack([w, *others]) for w, others in zip(up_far, x_up)]
    b_near, down_two, x_one, wu_far, df_hops = sync(
        links.near(b_hops), down_two, x_one, wu_far, df_hops
    )

    b_far = links.last_hop(b_near, "b")
    df_near = links.near(df_hops)
    x_two = [links.over_x(w, "wdB1") for w in down_two]
    for w in wu_far:
        wu += [w, links.from_core(w, "wu1")]
    b_far, x_two, wu, df_near = sync(b_far, x_two, wu, df_near)

    df_far = links.last_hop(df_near, "df")
    for w, one, two in zip(joined((down_one, down_two)), x_one, x_two):
        wd.append(jnp.stack([w, *joined((one, two))]))
        wd.append(links.from_core(wd[-1], "wd1"))
    b_rows, hidden, slope = call(
        up_kernel,
        "up",
        [b_near[0], b_far[0], b_near[1], b_far[1]],
        wu,
        [whole(D), whole(hidden_width), whole(hidden_width)],
    )
    df_far, wd, b_rows, hidden, slope = sync(df_far, wd, b_rows, hidden, slope)

    df_rows, du, *db = call(
        up_back_kernel,
        "up_back",
        [df_near[0], df_far[0], df_near[1], df_far[1], slope],
        wu + wd,
        [whole(D), whole(hidden_width), *parts],
    )
    b_rows, df_rows, hidden, du, db, a_rows = sync(b_rows, df_rows, hidden, du, db, a_rows)

    db_got = links.send_late(db, "db")
    down_send = gradient("g_down_send", nh, nd, flat(hidden), flat(df_rows), True, 1)
    up_send = gradient("g_up_send", nh, nd, flat(b_rows), flat(du), False, 1)
    a_columns = flat(a_rows).T
    db_got, down_send, up_send, b_rows, du, hidden, df_rows, a_columns = sync(
        db_got, down_send, up_send, b_rows, du, hidden, df_rows, a_columns
    )

    db_last = links.send_on(onward(db, db_got, "db_onward"), "db")
    down_sent = links.from_core(down_send, "g_down")
    g_down = down_kept(nh, nd, flat(hidden), flat(df_rows), down_sent)
    db_last, g_down, up_send, b_rows, du, hidden = sync(
        db_last, g_down, up_send, b_rows, du, hidden
    )

    dr, *datt_own = over_images(
        second_norm_back_kernel,
        "second_norm_back",
        [cot, loss_scale, residual, modulation, *sums(db, db_got, db_last)],
        [(every, F32), *kinds],
    )
    datt_hops = links.first_hop(datt_own, "datt")
    down_one = links.send_x(g_down[0::3], "g_downA")
    up_sent = links.from_core(up_send, "g_up")
    (down_one,) = add_terms("g_downA_sum", [g_down[0], *down_one])
    datt_hops, g_down, down_one, up_sent, b_rows, du, hidden = sync(
        datt_hops, g_down, down_one, up_sent, b_rows, du, hidden
    )
    datt_near = links.near(datt_hops)

    down_one = links.send_h(down_one, 0, "g_downA")
    datt_far = links.last_hop(datt_near, "datt")
    down_mid = links.send_x(g_down[1::3], "g_downB")
    ff = call(down_kernel, "down", [hidden], wd, parts)
    g_up = up_kept(nh, nd, flat(b_rows), flat(du), up_sent)
    far = (nh - 1) * (g_down[1].shape[0] // nh)
    (down_two,) = add_terms("g_downB_sum", [g_down[1], *down_mid], 1, far)
    datt_far, down_one, down_mid, down_two, g_down, g_up, ff = sync(
        datt_far, down_one, down_mid, down_two, g_down, g_up, ff
    )

    down_two = links.send_h(down_two, 0, "g_downB")
    up_far = links.send_x(g_up[0::2], "g_upA")
    ff_got = links.send_late(ff, "ff")
    *da, datt, dqkv, att_send = call(
        attention_back_kernel,
        "attention_back",
        [datt_near[0], datt_far[0], datt_near[1], datt_far[1], qkv, probs],
        wqo,
        parts,
        (a_columns, o),
        (whole(D), whole(3 * heads), (D // 2, 4 * heads)),
    )
    up_one, up_two = add_terms("g_upA_sum", [g_up[0], *up_far], 2)
    down_two, up_one, up_two, ff_got, datt, dqkv, da, att_send, g_up, g_down = sync(
        down_two, up_one, up_two, ff_got, datt, dqkv, da, att_send, g_up, g_down
    )

    up_one = links.send_h(up_one, 1, "g_upA")
    da_got = links.send_late(da, "da")
    att_sent = links.from_core(att_send, "g_att")
    down_last = links.send_x(g_down[2::3], "g_downC")
    g_att = attention_kept(nh, nd, a_columns, flat(dqkv), flat(datt), flat(o), att_sent)
    da_got, g_att, g_up, up_one, up_two, da, ff_got, down_last = sync(
        da_got, g_att, g_up, up_one, up_two, da, ff_got, down_last
    )

    up_two = links.send_h(up_two, 1, "g_upB")
    att_far = links.send_x(g_att[0::2], "g_attA")
    da_last = links.send_on(onward(da, da_got, "da_onward"), "da")
    att_one, att_two = add_terms("g_attA_sum", [g_att[0], *att_far], 2)
    att_one, att_two, up_two, da_last, g_att, g_up, ff_got = sync(
        att_one, att_two, up_two, da_last, g_att, g_up, ff_got
    )

    att_one = links.send_h(att_one, 1, "g_attA")
    up_here = links.send_x(g_up[1::2], "g_upC")
    ff_last = links.send_on(onward(ff, ff_got, "ff_onward"), "ff")
    (input_grad,) = over_images(
        first_norm_back_kernel,
        "first_norm_back",
        [stream, dr, modulation, *sums(da, da_got, da_last)],
        [(every, BF)],
    )
    g_down = jnp.concatenate(
        [
            sum(v[far:].astype(F32) for v in (g_down[1], *down_mid)),
            sum(v.astype(F32) for v in (g_down[2], *down_last)),
        ],
        axis=0,
    )
    g_down = total(g_down, joined((down_one, down_two)))
    att_one, att_two, up_here, ff_last, g_att, g_up, input_grad = sync(
        att_one, att_two, up_here, ff_last, g_att, g_up, input_grad
    )

    att_two = links.send_h(att_two, 1, "g_attB")
    att_here = links.send_x(g_att[1::2], "g_attC")
    (output,) = over_images(
        output_kernel,
        "output",
        [residual, modulation, *sums(ff, ff_got, ff_last)],
        [(every, BF)],
    )
    g_up = total(
        g_up[1].astype(F32) + sum(v.astype(F32) for v in up_here), joined((up_one, up_two))
    )
    att_two, att_here, g_att, output, input_grad = sync(
        att_two, att_here, g_att, output, input_grad
    )

    input_grad_got = links.leave_group(input_grad, "input_grad")
    att_there = joined((att_one, att_two))
    g_qkv, g_out, squares = unpack_attention_gradient(
        [g_att[1], *att_here, *att_there]
    )
    squares = jnp.sum(squares) + jnp.sum(g_up * g_up) + jnp.sum(g_down * g_down)
    grad_norm = jnp.sqrt(links.total(squares))
    grad_norm, output = sync(grad_norm, output)
    output_got = links.leave_group(output, "output")
    input_grad = come_home("input_grad_home", come, H, input_grad, input_grad_got, F32)
    output = come_home("output_home", come, H, output, output_got, BF)
    factor = jnp.minimum(1.0, clip_limit / (grad_norm + 1e-06))
    one_qkv, two_qkv, new_qkv = (
        v.transpose(1, 0, 2)
        for v in adam_update(
            g_qkv, *(v.transpose(1, 0, 2) for v in (m_qkv, v_qkv, w_qkv)), factor, learn_rate
        )
    )
    one_out, two_out, new_out = adam_update(g_out, m_out, v_out, w_out, factor, output_rate)
    one_up, two_up, new_up = adam_update(g_up, m_up, v_up, w_up, factor, learn_rate)
    one_down, two_down, new_down = adam_update(g_down, m_down, v_down, w_down, factor, learn_rate)
    return (
        output,
        input_grad,
        grad_norm,
        one_qkv,
        one_out,
        one_up,
        one_down,
        two_qkv,
        two_out,
        two_up,
        two_down,
        new_qkv,
        new_out,
        new_up,
        new_down,
    )


def solution(mesh):
    n_dp, n_mp = mesh.shape["dp"], mesh.shape["mp"]
    links = Links(n_dp, n_mp)
    fine = Mesh(mesh.devices.reshape(links.X, 2, links.H, 2, 2), links.axes)
    dp, mp = ("x", "core"), ("h", "p", "q")
    tokens, qkv = P(dp, mp, None), P(dp, None, mp)
    rows, columns = P(mp, dp), P(dp, mp)
    weights = (qkv, rows, columns, rows)
    return jax.shard_map(
        lambda *args: per_device(links, *args),
        mesh=fine,
        in_specs=(tokens, tokens, P(), P(dp), P(dp), P(dp)) + 3 * weights,
        out_specs=(tokens, tokens, P()) + 3 * weights,
        check_vma=False,
    )
```

```python
import jax
import jax.numpy as jnp
from jax import lax
from jax.experimental import pallas as pl
from jax.experimental.pallas import tpu as pltpu
from jax.sharding import Mesh
from jax.sharding import PartitionSpec as P

HD = 128
BINS = 8
ADAM_STEP = 10

clip_limit = 1.0
beta_one = 0.9
beta_two = 0.95
learn_rate = 0.02
output_rate = 0.08
adam_epsilon = 1e-08
decay_rate = 0.01

BF = jnp.bfloat16
F32 = jnp.float32


def adam_update(gradient, moment_one, moment_two, weight, factor, step_rate):
    clipped = gradient * factor
    new_one = beta_one * moment_one + (1.0 - beta_one) * clipped
    new_two = beta_two * moment_two + (1.0 - beta_two) * clipped * clipped
    corrected = new_one / (1.0 - beta_one**ADAM_STEP)
    root_two = jnp.sqrt(new_two / (1.0 - beta_two**ADAM_STEP))
    new_weight = weight - step_rate * (corrected / (root_two + adam_epsilon) + decay_rate * weight)
    return (new_one, new_two, new_weight)


def sync(*values):
    return lax.optimization_barrier(values)


def dot(a, b, contract=(1, 0)):
    return lax.dot_general(
        a, b, (((contract[0],), (contract[1],)), ((), ())), preferred_element_type=F32
    )


def rows_of(ref, columns=slice(None)):
    value = ref[0, :, :, columns]
    return value.reshape(value.shape[0] * value.shape[1], value.shape[2])


def join_tokens(pieces, whole):
    for kind, two in enumerate(pieces):
        for r, ref in enumerate(two):
            t = ref.shape[1]
            whole[0, kind, r * t : (r + 1) * t] = ref[0]


def put_parts(value, columns, parts):
    half = value.shape[0] // (2 * len(parts))
    for kind, (keep, send) in enumerate(parts):
        keep[0, :, columns] = value[2 * kind * half : (2 * kind + 1) * half]
        send[0, :, columns] = value[(2 * kind + 1) * half : (2 * kind + 2) * half]


def softmax_columns(q, k):
    scores = dot(k, q, (1, 1)) * HD ** (-0.5)
    weights = jnp.exp(scores - jnp.max(scores, axis=0, keepdims=True))
    return weights * (1.0 / jnp.sum(weights, axis=0, keepdims=True))


def head_columns(jh, part, n, block):
    start = (jh * 3 + part) * block + n * HD
    return slice(start, start + HD)


class Pieces:
    def __init__(self, refs):
        self.refs, self.at = refs, 0

    def take(self, count):
        self.at += count
        return self.refs[self.at - count : self.at]

    def tokens(self):
        near_far = self.take(4)
        return near_far[:2], near_far[2:]

    def parts(self):
        a, b, c, d = self.take(4)
        return (a, b), (c, d)


class Separate:
    def __init__(self, refs, nd):
        self.refs, self.depth = refs, refs[0].shape[0]
        self.shape = refs[0].shape[1:]

    def block(self, jh, d, rows=slice(None), columns=slice(None)):
        core, x = divmod(d, self.depth)
        return self.refs[2 * jh + core][x, rows, columns]


class Merged:
    def __init__(self, refs):
        self.refs = refs
        x, rows, columns = refs[0].shape
        self.shape = (x * rows, columns)

    def block(self, jh, core, rows=slice(None), columns=slice(None)):
        value = self.refs[2 * jh + core][:, :, columns]
        return value.reshape(self.shape[0], value.shape[2])


def attention_kernel(nh, nd, *refs):
    refs = Pieces(refs)
    tokens, weights = refs.tokens(), Merged(refs.take(2 * nh))
    (a, qkv, o, probs), parts = refs.take(4), refs.parts()
    join_tokens(tokens, a)
    nd = 2
    depth, block = weights.shape[0], weights.shape[1] // 4
    width = 3 * block
    inward = (slice(None), slice(0, width))
    outward = (slice(None), slice(width, width + block))
    kinds, length = a.shape[1], a.shape[2]
    for jh in range(nh):
        total = dot(rows_of(a, slice(0, depth)), weights.block(jh, 0, *inward))
        for d in range(1, nd):
            total += dot(rows_of(a, slice(d * depth, (d + 1) * depth)), weights.block(jh, d, *inward))
        qkv[0, :, :, jh * width : (jh + 1) * width] = total.astype(BF).reshape(kinds, length, width)
    for kind in range(kinds):
        for jh in range(nh):
            for n in range(block // HD):
                q, k, v = (qkv[0, kind, :, head_columns(jh, i, n, block)] for i in range(3))
                p = softmax_columns(q, k).astype(BF)
                probs[0, kind, jh * (block // HD) + n] = p
                out = dot(p, v, (0, 0)).astype(BF)
                o[0, kind, :, jh * block + n * HD : jh * block + (n + 1) * HD] = out
    for d in range(nd):
        total = dot(rows_of(o, slice(0, block)), weights.block(0, d, *outward), (1, 1))
        for jh in range(1, nh):
            total += dot(rows_of(o, slice(jh * block, (jh + 1) * block)), weights.block(jh, d, *outward), (1, 1))
        put_parts(total.astype(BF), slice(d * depth, (d + 1) * depth), parts)


def up_kernel(nh, nd, *refs):
    refs = Pieces(refs)
    b_tokens, wu = refs.tokens(), Merged(refs.take(2 * nh))
    b, hidden, slope = refs.take(3)
    join_tokens(b_tokens, b)
    nd = 2
    depth, width = wu.shape
    kinds, length = b.shape[1], b.shape[2]
    chunk = min(width, 512)
    curve, cubic = 0.7978845608028654, 0.044715
    for jh in range(nh):
        for c in range(0, width, chunk):
            part = slice(c, c + chunk)
            u = dot(rows_of(b, slice(0, depth)), wu.block(jh, 0, columns=part))
            for d in range(1, nd):
                cols = slice(d * depth, (d + 1) * depth)
                u += dot(rows_of(b, cols), wu.block(jh, d, columns=part))
            square = u * u
            t = jnp.tanh(curve * u * (1.0 + cubic * square))
            near = 0.5 * (1.0 + t)
            rise = near + 0.5 * u * (1.0 - t * t) * (curve * (1.0 + 3.0 * cubic * square))
            cols = slice(jh * width + c, jh * width + c + chunk)
            hidden[0, :, :, cols] = (u * near).astype(BF).reshape(kinds, length, chunk)
            slope[0, :, :, cols] = rise.astype(BF).reshape(kinds, length, chunk)


def up_back_kernel(nh, nd, *refs):
    refs = Pieces(refs)
    df_tokens, (slope,) = refs.tokens(), refs.take(1)
    wu, wd = Merged(refs.take(2 * nh)), Separate(refs.take(2 * nh), nd)
    (df, du), parts = refs.take(2), refs.parts()
    join_tokens(df_tokens, df)
    width, depth = wd.shape
    kinds, length = df.shape[1], df.shape[2]
    chunk = min(width, 512)
    for jh in range(nh):
        for c in range(0, width, chunk):
            part = slice(c, c + chunk)
            dh = dot(rows_of(df, slice(0, depth)), wd.block(jh, 0, part), (1, 1))
            for d in range(1, nd):
                cols = slice(d * depth, (d + 1) * depth)
                dh += dot(rows_of(df, cols), wd.block(jh, d, part), (1, 1))
            cols = slice(jh * width + c, jh * width + c + chunk)
            value = dh * rows_of(slope, cols).astype(F32)
            du[0, :, :, cols] = value.astype(BF).reshape(kinds, length, chunk)
    depth = wu.shape[0]
    for d in range(2):
        total = dot(rows_of(du, slice(0, width)), wu.block(0, d), (1, 1))
        for jh in range(1, nh):
            total += dot(rows_of(du, slice(jh * width, (jh + 1) * width)), wu.block(jh, d), (1, 1))
        put_parts(total.astype(BF), slice(d * depth, (d + 1) * depth), parts)


def down_kernel(nh, nd, *refs):
    refs = Pieces(refs)
    (hidden,), wd = refs.take(1), Separate(refs.take(2 * nh), nd)
    parts = refs.parts()
    width, depth = wd.shape
    for d in range(nd):
        total = dot(rows_of(hidden, slice(0, width)), wd.block(0, d))
        for jh in range(1, nh):
            total += dot(rows_of(hidden, slice(jh * width, (jh + 1) * width)), wd.block(jh, d))
        put_parts(total.astype(BF), slice(d * depth, (d + 1) * depth), parts)


def attention_back_kernel(nh, nd, *refs):
    refs = Pieces(refs)
    (a, o), tokens, (qkv, probs) = refs.take(2), refs.tokens(), refs.take(2)
    weights = Merged(refs.take(2 * nh))
    parts, (datt_out, dqkv_out, sent, all_datt, all_dqkv) = refs.parts(), refs.take(5)
    step = pl.program_id(0)
    datt, dqkv = (v.at[pl.ds(step, 1)] for v in (all_datt, all_dqkv))
    join_tokens(tokens, datt)
    nd = 2
    depth, block = weights.shape[0], weights.shape[1] // 4
    width = 3 * block
    inward = (slice(None), slice(0, width))
    outward = (slice(None), slice(width, width + block))
    kinds, length = datt.shape[1], datt.shape[2]
    for jh in range(nh):
        do_all = dot(rows_of(datt, slice(0, depth)), weights.block(jh, 0, *outward))
        for d in range(1, nd):
            do_all += dot(rows_of(datt, slice(d * depth, (d + 1) * depth)), weights.block(jh, d, *outward))
        do_all = do_all.astype(BF)
        for kind in range(kinds):
            for n in range(block // HD):
                q, k, v = (qkv[0, kind, :, head_columns(jh, i, n, block)] for i in range(3))
                do = do_all[kind * length : (kind + 1) * length, n * HD : (n + 1) * HD]
                rounded = probs[0, kind, jh * (block // HD) + n]
                dv = dot(rounded, do)
                dp = dot(v, do, (1, 1))
                p = rounded.astype(F32)
                ds = (p * (dp - jnp.sum(p * dp, axis=0, keepdims=True))).astype(BF)
                dq = dot(ds, k, (0, 0)) * HD ** (-0.5)
                dk = dot(ds, q) * HD ** (-0.5)
                for i, value in enumerate((dq, dk, dv)):
                    dqkv[0, kind, :, head_columns(jh, i, n, block)] = value.astype(BF)
    for d in range(nd):
        total = dot(rows_of(dqkv, slice(0, width)), weights.block(0, d, *inward), (1, 1))
        for jh in range(1, nh):
            total += dot(rows_of(dqkv, slice(jh * width, (jh + 1) * width)), weights.block(jh, d, *inward), (1, 1))
        put_parts(total.astype(BF), slice(d * depth, (d + 1) * depth), parts)
    datt_out[...] = datt[...]
    dqkv_out[...] = dqkv[...]
    across, both = nd // 2, width + block

    def every_row(ref, columns=slice(None)):
        value = ref[:, :, :, columns]
        return value.reshape(-1, value.shape[-1])

    @pl.when(step == pl.num_programs(0) - 1)
    def _():
        for jx in range(across):
            cols = slice((across + jx) * depth, (across + jx + 1) * depth)
            inward = dot(a[cols], every_row(all_dqkv)).astype(BF)
            outward = dot(every_row(all_datt, cols), every_row(o), (0, 0)).astype(BF)
            rows = slice(jx * depth, (jx + 1) * depth)
            for jh in range(nh):
                at = jh * both
                sent[rows, at : at + width] = inward[:, jh * width : (jh + 1) * width]
                sent[rows, at + width : at + both] = outward[:, jh * block : (jh + 1) * block]


def group_call(
    kernel, name, nh, nd, steps, blocked, whole, outs, resident=(), whole_outs=(), scratch=()
):
    def cut(shape):
        zeros = (0,) * (len(shape) - 1)
        return pl.BlockSpec((1,) + tuple(shape[1:]), lambda i: (i,) + zeros)

    def stay(shape):
        zeros = (0,) * len(shape)
        return pl.BlockSpec(tuple(shape), lambda i: zeros)

    return pl.pallas_call(
        lambda *refs: kernel(nh, nd, *refs),
        name=name,
        grid=(steps,),
        in_specs=[stay(v.shape) for v in resident]
        + [cut(v.shape) for v in blocked]
        + [pl.BlockSpec(memory_space=pltpu.VMEM)] * len(whole),
        out_specs=[cut(s) for s in outs] + [stay(s) for s in whole_outs],
        out_shape=[jax.ShapeDtypeStruct(s, BF) for s in (*outs, *whole_outs)],
        scratch_shapes=[pltpu.VMEM(shape, BF) for shape in scratch],
        compiler_params=pltpu.CompilerParams(vmem_limit_bytes=62 * 2**20),
        cost_estimate=pl.CostEstimate(flops=0, bytes_accessed=0, transcendentals=0),
    )(*resident, *blocked, *whole)


def image_call(kernel, name, steps, arrays, outs):
    def seen(shape):
        return (2, steps, *shape[1:]) if shape[0] == 2 * steps else tuple(shape)

    def cut(shape):
        zeros = (0,) * (len(shape) - 2)
        if shape[0] == 2 and len(shape) == 4:
            return pl.BlockSpec((2, 1, *shape[2:]), lambda i: (0, i, *zeros))
        return pl.BlockSpec((1, *shape[1:]), lambda i: (i, 0, *zeros))

    made = pl.pallas_call(
        kernel,
        name=name,
        grid=(steps,),
        in_specs=[cut(seen(v.shape)) for v in arrays],
        out_specs=[cut(seen(shape)) for shape, _ in outs],
        out_shape=[jax.ShapeDtypeStruct(seen(shape), dtype) for shape, dtype in outs],
        compiler_params=pltpu.CompilerParams(vmem_limit_bytes=32 * 2**20),
        cost_estimate=pl.CostEstimate(flops=0, bytes_accessed=0, transcendentals=0),
    )(*[v.reshape(seen(v.shape)) for v in arrays])
    return [v.reshape(shape) for v, (shape, _) in zip(made, outs)]


def move_call(kernel, name, table, arrays, outs):
    def whole(shape):
        zeros = (0,) * len(shape)
        return pl.BlockSpec(tuple(shape), lambda i, table: zeros)

    return pl.pallas_call(
        kernel,
        name=name,
        grid_spec=pltpu.PrefetchScalarGridSpec(
            num_scalar_prefetch=1,
            grid=(1,),
            in_specs=[whole(v.shape) for v in arrays],
            out_specs=[whole(shape) for shape, _ in outs],
        ),
        out_shape=[jax.ShapeDtypeStruct(shape, dtype) for shape, dtype in outs],
        compiler_params=pltpu.CompilerParams(vmem_limit_bytes=32 * 2**20),
        cost_estimate=pl.CostEstimate(flops=0, bytes_accessed=0, transcendentals=0),
    )(table, *arrays)


def leave_home(name, table, groups, v):
    slots, t, D = v.shape
    blocks, images = table.shape[0] - groups, slots // groups
    width = D // blocks

    def kernel(table, v, *outs):
        for jh in range(groups):
            picked = pl.ds(table[jh] * images, images)
            for e in range(blocks):
                columns = pl.ds(pl.multiple_of(table[groups + e] * width, width), width)
                outs[jh][:, :, e * width : (e + 1) * width] = v[picked, :, columns].astype(BF)

    return move_call(kernel, name, table, [v], [((images, t, D), BF)] * groups)


def come_home(name, table, groups, own, received, dtype):
    images, length, D = own.shape
    blocks, t = table.shape[0] - groups, length // groups
    width = D // blocks

    def kernel(table, own, *refs):
        *received, out = refs
        for jh in range(groups):
            picked = pl.ds(table[jh] * images, images)
            for e in range(blocks):
                columns = pl.ds(pl.multiple_of(table[groups + e] * width, width), width)
                part = received[jh - 1][:, :, columns] if jh else own[:, :t, columns]
                out[picked, :, e * width : (e + 1) * width] = part.astype(dtype)

    shape = (images * groups, t, D)
    return move_call(kernel, name, table, [own, *received], [(shape, dtype)])[0]


def row_parts(values):
    center = values - jnp.mean(values, axis=-1, keepdims=True)
    factor = lax.rsqrt(jnp.mean(center * center, axis=-1, keepdims=True) + 1e-06)
    return center * factor, factor


def norm_back(values, gradient):
    rows, factor = row_parts(values)
    return factor * (
        gradient
        - jnp.mean(gradient, axis=-1, keepdims=True)
        - rows * jnp.mean(gradient * rows, axis=-1, keepdims=True)
    )


def token_sum(sums, kind):
    keep, got, last = sums[kind], sums[2 + kind], sums[4 + kind]
    t = last.shape[1]
    return keep[0, :t].astype(F32) + got[0, :t].astype(F32) + last[0].astype(F32)


def first_norm_kernel(stream, mod, *a):
    for kind in range(2):
        rows, _ = row_parts(stream[kind, 0].astype(F32))
        a[kind][0] = (rows * mod[kind, 0, 1:2] + mod[kind, 0, 0:1]).astype(BF)


def loss_kernel(cot, weight, mod, *df):
    for kind in range(2):
        seed = cot[kind, 0].astype(F32) * weight[kind, 0]
        df[kind][0] = (mod[kind, 0, 5:6] * seed).astype(BF)


def second_norm_kernel(stream, mod, *refs):
    sums, residual, b = refs[:6], refs[6], refs[7:]
    for kind in range(2):
        r = stream[kind, 0].astype(F32) + mod[kind, 0, 2:3] * token_sum(sums, kind)
        residual[kind, 0] = r
        rows, _ = row_parts(r)
        b[kind][0] = (rows * mod[kind, 0, 4:5] + mod[kind, 0, 3:4]).astype(BF)


def second_norm_back_kernel(cot, weight, residual, mod, *refs):
    sums, dr, datt = refs[:6], refs[6], refs[7:]
    for kind in range(2):
        seed = cot[kind, 0].astype(F32) * weight[kind, 0]
        g = seed + norm_back(residual[kind, 0], token_sum(sums, kind) * mod[kind, 0, 4:5])
        dr[kind, 0] = g
        datt[kind][0] = (mod[kind, 0, 2:3] * g).astype(BF)


def first_norm_back_kernel(stream, dr, mod, *refs):
    sums, out = refs[:6], refs[6]
    for kind in range(2):
        g = norm_back(stream[kind, 0].astype(F32), token_sum(sums, kind) * mod[kind, 0, 1:2])
        out[kind, 0] = (dr[kind, 0] + g).astype(BF)


def output_kernel(residual, mod, *refs):
    sums, out = refs[:6], refs[6]
    for kind in range(2):
        out[kind, 0] = (residual[kind, 0] + mod[kind, 0, 5:6] * token_sum(sums, kind)).astype(BF)


def rounded(weights):
    def kernel(*refs):
        for source, copy in zip(refs[: len(weights)], refs[len(weights) :]):
            copy[...] = source[...].astype(BF)

    halves = [pl.BlockSpec((v.shape[0] // 2, v.shape[1]), lambda i: (i, 0)) for v in weights]
    return pl.pallas_call(
        kernel,
        name="rounded",
        grid=(2,),
        in_specs=halves,
        out_specs=halves,
        out_shape=[jax.ShapeDtypeStruct(v.shape, BF) for v in weights],
        compiler_params=pltpu.CompilerParams(vmem_limit_bytes=32 * 2**20),
        cost_estimate=pl.CostEstimate(flops=0, bytes_accessed=0, transcendentals=0),
    )(*weights)


def pack_attention_weights(w_qkv, w_out):
    depth, _, block = w_qkv.shape

    def kernel(inward, outward, packed):
        for i in range(3):
            packed[:, i * block : (i + 1) * block] = inward[i].astype(BF)
        packed[:, 3 * block :] = outward[...].T.astype(BF)

    return pl.pallas_call(
        kernel,
        name="pack",
        out_shape=jax.ShapeDtypeStruct((depth, 4 * block), BF),
        compiler_params=pltpu.CompilerParams(vmem_limit_bytes=32 * 2**20),
        cost_estimate=pl.CostEstimate(flops=0, bytes_accessed=0, transcendentals=0),
    )(w_qkv.transpose(1, 0, 2), w_out)


def gradient(name, nh, nd, left, right, left_is_hidden, core):
    rows = left.shape[0]
    hidden, features = (left, right) if left_is_hidden else (right, left)
    h_width, d_width, half = hidden.shape[1] // nh, features.shape[1] // nd, nd // 2

    def kernel(left, right, out):
        out[...] = dot(left[...], right[...], (0, 0)).astype(BF)

    h_spec = pl.BlockSpec((rows, h_width), lambda jh, d: (0, jh))
    d_spec = pl.BlockSpec((rows, d_width), lambda jh, d: (0, core * half + d))
    if left_is_hidden:
        in_specs, out_spec = [h_spec, d_spec], pl.BlockSpec((h_width, d_width), lambda jh, d: (jh, d))
        shape = (nh * h_width, half * d_width)
    else:
        in_specs, out_spec = [d_spec, h_spec], pl.BlockSpec((d_width, h_width), lambda jh, d: (d, jh))
        shape = (half * d_width, nh * h_width)
    return pl.pallas_call(
        kernel,
        name=name,
        grid=(nh, half),
        in_specs=in_specs,
        out_specs=out_spec,
        out_shape=jax.ShapeDtypeStruct(shape, BF),
        compiler_params=pltpu.CompilerParams(vmem_limit_bytes=48 * 2**20),
        cost_estimate=pl.CostEstimate(flops=0, bytes_accessed=0, transcendentals=0),
    )(left, right)


def one_step(kernel, name, arrays, columns, outs, dtype=BF):
    return pl.pallas_call(
        kernel,
        name=name,
        grid=(1,),
        in_specs=[
            pl.BlockSpec((v.shape[0], c or v.shape[1]), lambda i: (0, 0))
            for v, c in zip(arrays, columns)
        ],
        out_specs=[pl.BlockSpec(shape, lambda i: (0, 0)) for shape in outs],
        out_shape=[jax.ShapeDtypeStruct(shape, dtype) for shape in outs],
        compiler_params=pltpu.CompilerParams(vmem_limit_bytes=60 * 2**20),
        cost_estimate=pl.CostEstimate(flops=0, bytes_accessed=0, transcendentals=0),
    )(*arrays)


def down_kept(nh, nd, hidden, df, sent):
    half = nd // 2
    height, width = hidden.shape[1] // nh, df.shape[1] // nd
    cut = height // 2

    def kernel(hidden, df, sent, *outs):
        for jx in range(half):
            one, two, three = outs[3 * jx : 3 * jx + 3]
            cols = slice(jx * width, (jx + 1) * width)
            for jh in range(nh):
                rows = slice(jh * height, (jh + 1) * height)
                g = dot(hidden[:, rows], df[:, cols], (0, 0)) + sent[rows, cols].astype(F32)
                g = g.astype(BF)
                if jh:
                    one[(jh - 1) * cut : jh * cut] = g[:cut]
                    two[(jh - 1) * cut : jh * cut] = g[cut:]
                else:
                    two[(nh - 1) * cut :] = g[:cut]
                    three[...] = g[cut:]

    shapes = [((nh - 1) * cut, width), (nh * cut, width), (cut, width)] * half
    return one_step(kernel, "g_down_keep", (hidden, df, sent), (None, half * width, None), shapes)


def up_kept(nh, nd, b, du, sent):
    half = nd // 2
    height, width = b.shape[1] // nd, du.shape[1] // nh

    def kernel(b, du, sent, *outs):
        for jx in range(half):
            far, here = outs[2 * jx : 2 * jx + 2]
            rows = slice(jx * height, (jx + 1) * height)
            for jh in range(nh):
                cols = slice(jh * width, (jh + 1) * width)
                g = dot(b[:, rows], du[:, cols], (0, 0)) + sent[rows, cols].astype(F32)
                if jh:
                    far[:, (jh - 1) * width : jh * width] = g.astype(BF)
                else:
                    here[...] = g.astype(BF)

    shapes = [(height, (nh - 1) * width), (height, width)] * half
    return one_step(kernel, "g_up_keep", (b, du, sent), (half * height, None, None), shapes)


def attention_kept(nh, nd, a, dqkv, datt, o, sent):
    half = nd // 2
    height = a.shape[0] // nd
    width, block = dqkv.shape[1] // nh, o.shape[1] // nh
    both = width + block

    def kernel(a, dqkv, datt, o, sent, *outs):
        for jx in range(half):
            far, here = outs[2 * jx : 2 * jx + 2]
            rows = slice(jx * height, (jx + 1) * height)
            inward = dot(a[rows], dqkv[...])
            outward = dot(datt[:, rows], o[...], (0, 0))
            for jh in range(nh):
                out, at = (far, (jh - 1) * both) if jh else (here, 0)
                terms = sent[rows, jh * both : (jh + 1) * both].astype(F32)
                g = inward[:, jh * width : (jh + 1) * width] + terms[:, :width]
                out[:, at : at + width] = g.astype(BF)
                g = outward[:, jh * block : (jh + 1) * block] + terms[:, width:]
                out[:, at + width : at + both] = g.astype(BF)

    shapes = [(height, (nh - 1) * both), (height, both)] * half
    cols = half * height
    return one_step(
        kernel, "g_att_keep", (a, dqkv, datt, o, sent), (None, None, cols, None, None), shapes
    )


def add_terms(name, terms, cuts=1, rows=None):
    rows, width = rows or terms[0].shape[0], terms[0].shape[1]
    size = rows // cuts

    def kernel(*refs):
        terms, outs = refs[: len(refs) - cuts], refs[len(refs) - cuts :]
        for c, out in enumerate(outs):
            out[...] = sum(
                v[c * size : (c + 1) * size].astype(F32) for v in terms
            ).astype(BF)

    return one_step(kernel, name, terms, [None] * len(terms), [(size, width)] * cuts)


def onward_kernel(*refs):
    for kind in range(2):
        keep, got, out = refs[kind], refs[2 + kind], refs[4 + kind]
        t = out.shape[1]
        out[0] = (keep[0, t:].astype(F32) + got[0, t:].astype(F32)).astype(BF)


def unpack_attention_gradient(terms):
    depth, width = terms[0].shape
    block = width // 4

    def kernel(*refs):
        *terms, inward, outward, squares = refs
        total = sum(v[...].astype(F32) for v in terms)
        square = total * total
        squares[...] = sum(
            jnp.sum(square[:, c : c + 128].reshape(depth // 8, 8, 128), axis=0)
            for c in range(0, width, 128)
        )
        for i in range(3):
            inward[i] = total[:, i * block : (i + 1) * block]
        outward[...] = total[:, 3 * block :].T

    return pl.pallas_call(
        kernel,
        name="unpack",
        out_shape=[
            jax.ShapeDtypeStruct((3, depth, block), F32),
            jax.ShapeDtypeStruct((block, depth), F32),
            jax.ShapeDtypeStruct((8, 128), F32),
        ],
        compiler_params=pltpu.CompilerParams(vmem_limit_bytes=32 * 2**20),
        cost_estimate=pl.CostEstimate(flops=0, bytes_accessed=0, transcendentals=0),
    )(*terms)


class Links:
    axes = ("x", "core", "h", "p", "q")

    def __init__(self, n_dp, n_mp):
        self.X, self.H = n_dp // 2, n_mp // 4
        self.n_dp, self.n_mp = n_dp, n_mp

    def shifted(self, v, axis, size, offset, name):
        with jax.named_scope(f"{name}_{axis}"):
            return lax.ppermute(v, axis, [((dst + offset) % size, dst) for dst in range(size)])

    def from_core(self, v, name):
        return self.shifted(v, "core", 2, 1, name)

    def from_x(self, v, jx, name):
        return self.shifted(v, "x", self.X, jx, name)

    def from_h(self, v, jh, name):
        return self.shifted(v, "h", self.H, jh, name)

    def over_h(self, w, name):
        return [self.from_h(w, jh, name) for jh in range(1, self.H)]

    def over_x(self, w, name):
        return [self.from_x(w, jx, name) for jx in range(1, self.X)]

    def send_x(self, parts, name):
        return [self.from_x(parts[jx], -jx, name) for jx in range(1, self.X)]

    def send_h(self, g, h, name):
        width = g.shape[h] // (self.H - 1)
        return [
            self.from_h(lax.slice_in_dim(g, (jh - 1) * width, jh * width, axis=h), -jh, name)
            for jh in range(1, self.H)
        ]

    def tables(self):
        x, core, h = (lax.axis_index(axis) for axis in self.axes[:3])
        groups = [(h - jh) % self.H for jh in range(self.H)]
        here = [
            ((x + jx) % self.X) * 2 + (core ^ jc) for jc in range(2) for jx in range(self.X)
        ]
        home = [((e % 2) ^ core) * self.X + (e // 2 - x) % self.X for e in range(self.n_dp)]
        return [jnp.stack(groups + rest).astype(jnp.int32) for rest in (here, home)]

    def to_group(self, parts, name):
        return [self.from_h(parts[jh], jh, name) for jh in range(1, self.H)]

    def leave_group(self, v, name):
        tokens = v.shape[1] // self.H
        return [
            self.from_h(v[:, jh * tokens : (jh + 1) * tokens], -jh, name) for jh in range(1, self.H)
        ]

    def over(self, v, kind, late, name):
        return self.shifted(v, "p" if (kind == 0) != late else "q", 2, 1, f"{name}{kind}")

    def first_hop(self, own, name):
        return [(own[k], self.over(own[k], k, False, name)) for k in range(2)]

    def near(self, hops):
        return [jnp.concatenate(pair, axis=1) for pair in hops]

    def last_hop(self, near, name):
        return [self.over(near[k], k, True, name) for k in (1, 0)][::-1]

    def send_late(self, parts, name):
        return [self.over(parts[2 * k + 1], k, True, name) for k in (1, 0)][::-1]

    def send_on(self, onward, name):
        return [self.over(onward[k], k, False, name) for k in range(2)]

    def features_here(self, v):
        x, c = lax.axis_index("x"), lax.axis_index("core")
        width = v.shape[-1] // self.n_dp
        return jnp.concatenate(
            [
                lax.dynamic_slice_in_dim(
                    v, (((x + jx) % self.X) * 2 + (c ^ jc)) * width, width, axis=v.ndim - 1
                )
                for jc in range(2)
                for jx in range(self.X)
            ],
            axis=-1,
        )

    def total(self, v):
        for axis, size in (("core", 2), ("q", 2), ("x", self.X), ("p", 2), ("h", self.H)):
            step = 1
            while step < size:
                with jax.named_scope("norm"):
                    v = v + lax.ppermute(v, axis, [(i ^ step, i) for i in range(size)])
                step *= 2
        return v


def per_device(
    links,
    stream_in,
    cotangent,
    noise_table,
    timesteps,
    bins,
    counts,
    w_qkv,
    w_out,
    w_up,
    w_down,
    m_qkv,
    m_out,
    m_up,
    m_down,
    v_qkv,
    v_out,
    v_up,
    v_down,
):
    H = links.H
    slots, _, D = stream_in.shape
    images = slots // H
    here = lax.axis_index("h")

    steps_here = lax.dynamic_slice_in_dim(timesteps, here * images, images)
    table_rows = noise_table.shape[0]
    picks = (steps_here[:, None] == jnp.arange(table_rows)[None, :]).astype(F32)
    modulation = jnp.dot(
        picks, noise_table.reshape(table_rows, -1), precision=lax.Precision.HIGHEST
    ).reshape(images, 6, D)
    modulation = links.features_here(modulation)
    live = jnp.arange(slots) < counts[0]
    loss_scale = live.astype(F32) * (bins.astype(F32) + 1.0) / BINS
    loss_scale = lax.dynamic_slice_in_dim(loss_scale, here * images, images)
    loss_scale = jnp.broadcast_to(loss_scale[:, None, None], (images, 1, D))

    block = w_qkv.shape[2]
    length = stream_in.shape[1] * H * 4
    steps = images // 2
    rows = images * length
    nh, nd = H, 2 * links.X
    heads = H * block
    hidden_width = H * w_up.shape[1]
    whole = lambda width: (steps, 2, length, width)
    parts = [(steps, length // 2, D)] * 4

    tokens = length // 4
    every, kinds = (images, tokens, D), [((steps, tokens, D), BF)] * 2

    def over_images(kernel, name, arrays, outs):
        return image_call(kernel, name, steps, arrays, outs)

    def onward(parts, got, name):
        arrays = [parts[0], parts[2], *got]
        return over_images(onward_kernel, name, arrays, kinds)

    def sums(parts, got, last):
        return [parts[0], parts[2], *got, *last]

    def flat(v):
        return v.reshape(rows, v.shape[-1])

    def call(kernel, name, blocked, weights, outs, *staying):
        return list(group_call(kernel, name, nh, nd, steps, blocked, weights, outs, *staying))

    def halves(w):
        size = w.shape[0] // 2
        return w[:size], w[size:]

    def joined(pair):
        return [jnp.concatenate(two, axis=0) for two in zip(*pair)]

    def total(here, there):
        return here + sum(v.astype(F32) for v in there)

    leave, come = links.tables()
    stream_parts = leave_home("stream_leaves", leave, H, stream_in)
    packed = pack_attention_weights(w_qkv, w_out)
    stream_got = links.to_group(stream_parts, "stream")
    x_packed = links.over_x(packed, "wqo0")
    up, down = rounded([w_up, w_down])
    stream_parts, stream_got, x_packed, packed, up, down = sync(
        stream_parts, stream_got, x_packed, packed, up, down
    )

    stream = jnp.concatenate([stream_parts[0], *stream_got], axis=1)
    a_own = over_images(first_norm_kernel, "first_norm", [stream, modulation], kinds)
    a_hops = links.first_hop(a_own, "a")
    packed_one, packed_two = halves(packed)
    far_one = links.over_h(packed_one, "wqoA")
    x_up = links.over_x(up, "wu0")
    wqo = [jnp.stack([packed, *x_packed])]
    a_hops, far_one, x_up, wqo, packed_two = sync(a_hops, far_one, x_up, wqo, packed_two)
    a_near = links.near(a_hops)

    far_two = links.over_h(packed_two, "wqoB")
    a_far = links.last_hop(a_near, "a")
    x_one = [links.over_x(w, "wqoA1") for w in far_one]
    cot_parts = leave_home("cot_leaves", leave, H, cotangent)
    cot_one = [v[:steps] for v in cot_parts]
    cot_two = [v[steps:] for v in cot_parts]
    wu = [jnp.stack([up, *x_up])]
    a_far, far_two, x_one, cot_one, cot_two, wqo, wu = sync(
        a_far, far_two, x_one, cot_one, cot_two, wqo, wu
    )

    x_two = [links.over_x(w, "wqoB1") for w in far_two]
    cot_one = [cot_one[0], *links.to_group(cot_one, "cotA")]
    wqo.append(links.from_core(wqo[0], "wqo0"))
    wu.append(links.from_core(wu[0], "wu0"))
    packed_far = joined((far_one, far_two))
    packed_far, x_two, cot_one, cot_two, wqo, wu = sync(
        packed_far, x_two, cot_one, cot_two, wqo, wu
    )

    cot_two = [cot_two[0], *links.to_group(cot_two, "cotB")]
    for w, one, two in zip(packed_far, x_one, x_two):
        wqo.append(jnp.stack([w, *joined((one, two))]))
        wqo.append(links.from_core(wqo[-1], "wqo1"))
    up_one, up_two = halves(up)
    cot_one, cot_two, wqo, up_one, up_two, down = sync(cot_one, cot_two, wqo, up_one, up_two, down)

    cot = jnp.concatenate([jnp.concatenate(v, axis=1) for v in (cot_one, cot_two)], axis=0)
    df_own = over_images(loss_kernel, "loss", [cot, loss_scale, modulation], kinds)
    up_one = links.over_h(up_one, "wuA")
    df_hops = links.first_hop(df_own, "df")
    x_down = links.over_x(down, "wd0")
    a_rows, qkv, o, probs, *att = call(
        attention_kernel,
        "attention",
        [a_near[0], a_far[0], a_near[1], a_far[1]],
        wqo,
        [whole(D), whole(3 * heads), whole(heads), (steps, 2, heads // HD, length, length), *parts],
    )
    df_hops, att, up_one, up_two, x_down = sync(df_hops, att, up_one, up_two, x_down)

    up_two = links.over_h(up_two, "wuB")
    att_got = links.send_late(att, "att")
    wd = [jnp.stack([down, *x_down])]
    wd.append(links.from_core(wd[0], "wd0"))
    att_got, up_two, wd, down = sync(att_got, up_two, wd, down)

    down_one, down_two = halves(down)
    down_one = links.over_h(down_one, "wdA")
    att_last = links.send_on(onward(att, att_got, "att_onward"), "att")
    up_far = joined((up_one, up_two))
    x_up = [links.over_x(w, "wu1") for w in up_far]
    residual, *b = over_images(
        second_norm_kernel,
        "second_norm",
        [stream, modulation, *sums(att, att_got, att_last)],
        [(every, F32), *kinds],
    )
    b, down_one, up_far, x_up, down_two = sync(b, down_one, up_far, x_up, down_two)

    down_two = links.over_h(down_two, "wdB")
    b_hops = links.first_hop(b, "b")
    x_one = [links.over_x(w, "wdA1") for w in down_one]
    wu_far = [jnp.stack([w, *others]) for w, others in zip(up_far, x_up)]
    b_near, down_two, x_one, wu_far, df_hops = sync(
        links.near(b_hops), down_two, x_one, wu_far, df_hops
    )

    b_far = links.last_hop(b_near, "b")
    df_near = links.near(df_hops)
    x_two = [links.over_x(w, "wdB1") for w in down_two]
    for w in wu_far:
        wu += [w, links.from_core(w, "wu1")]
    b_far, x_two, wu, df_near = sync(b_far, x_two, wu, df_near)

    df_far = links.last_hop(df_near, "df")
    for w, one, two in zip(joined((down_one, down_two)), x_one, x_two):
        wd.append(jnp.stack([w, *joined((one, two))]))
        wd.append(links.from_core(wd[-1], "wd1"))
    b_rows, hidden, slope = call(
        up_kernel,
        "up",
        [b_near[0], b_far[0], b_near[1], b_far[1]],
        wu,
        [whole(D), whole(hidden_width), whole(hidden_width)],
    )
    df_far, wd, b_rows, hidden, slope = sync(df_far, wd, b_rows, hidden, slope)

    df_rows, du, *db = call(
        up_back_kernel,
        "up_back",
        [df_near[0], df_far[0], df_near[1], df_far[1], slope],
        wu + wd,
        [whole(D), whole(hidden_width), *parts],
    )
    b_rows, df_rows, hidden, du, db, a_rows = sync(b_rows, df_rows, hidden, du, db, a_rows)

    db_got = links.send_late(db, "db")
    down_send = gradient("g_down_send", nh, nd, flat(hidden), flat(df_rows), True, 1)
    up_send = gradient("g_up_send", nh, nd, flat(b_rows), flat(du), False, 1)
    a_columns = flat(a_rows).T
    db_got, down_send, up_send, b_rows, du, hidden, df_rows, a_columns = sync(
        db_got, down_send, up_send, b_rows, du, hidden, df_rows, a_columns
    )

    db_last = links.send_on(onward(db, db_got, "db_onward"), "db")
    down_sent = links.from_core(down_send, "g_down")
    g_down = down_kept(nh, nd, flat(hidden), flat(df_rows), down_sent)
    db_last, g_down, up_send, b_rows, du, hidden = sync(
        db_last, g_down, up_send, b_rows, du, hidden
    )

    dr, *datt_own = over_images(
        second_norm_back_kernel,
        "second_norm_back",
        [cot, loss_scale, residual, modulation, *sums(db, db_got, db_last)],
        [(every, F32), *kinds],
    )
    datt_hops = links.first_hop(datt_own, "datt")
    down_one = links.send_x(g_down[0::3], "g_downA")
    up_sent = links.from_core(up_send, "g_up")
    (down_one,) = add_terms("g_downA_sum", [g_down[0], *down_one])
    datt_hops, g_down, down_one, up_sent, b_rows, du, hidden = sync(
        datt_hops, g_down, down_one, up_sent, b_rows, du, hidden
    )
    datt_near = links.near(datt_hops)

    down_one = links.send_h(down_one, 0, "g_downA")
    datt_far = links.last_hop(datt_near, "datt")
    down_mid = links.send_x(g_down[1::3], "g_downB")
    ff = call(down_kernel, "down", [hidden], wd, parts)
    g_up = up_kept(nh, nd, flat(b_rows), flat(du), up_sent)
    far = (nh - 1) * (g_down[1].shape[0] // nh)
    (down_two,) = add_terms("g_downB_sum", [g_down[1], *down_mid], 1, far)
    datt_far, down_one, down_mid, down_two, g_down, g_up, ff = sync(
        datt_far, down_one, down_mid, down_two, g_down, g_up, ff
    )

    down_two = links.send_h(down_two, 0, "g_downB")
    up_far = links.send_x(g_up[0::2], "g_upA")
    ff_got = links.send_late(ff, "ff")
    *da, datt, dqkv, att_send = call(
        attention_back_kernel,
        "attention_back",
        [datt_near[0], datt_far[0], datt_near[1], datt_far[1], qkv, probs],
        wqo,
        [*parts, whole(D), whole(3 * heads)],
        (a_columns, o),
        [(D // 2, 4 * heads)],
        (whole(D), whole(3 * heads)),
    )
    down_two, up_far, ff_got, datt, dqkv, da, att_send, g_up, g_down = sync(
        down_two, up_far, ff_got, datt, dqkv, da, att_send, g_up, g_down
    )

    up_one, up_two = add_terms("g_upA_sum", [g_up[0], *up_far], 2)
    up_one = links.send_h(up_one, 1, "g_upA")
    da_got = links.send_late(da, "da")
    att_sent = links.from_core(att_send, "g_att")
    down_last = links.send_x(g_down[2::3], "g_downC")
    g_att = attention_kept(nh, nd, a_columns, flat(dqkv), flat(datt), flat(o), att_sent)
    da_got, g_att, g_up, up_one, up_two, da, ff_got, down_last = sync(
        da_got, g_att, g_up, up_one, up_two, da, ff_got, down_last
    )

    up_two = links.send_h(up_two, 1, "g_upB")
    att_far = links.send_x(g_att[0::2], "g_attA")
    da_last = links.send_on(onward(da, da_got, "da_onward"), "da")
    att_one, att_two = add_terms("g_attA_sum", [g_att[0], *att_far], 2)
    att_one, att_two, up_two, da_last, g_att, g_up, ff_got = sync(
        att_one, att_two, up_two, da_last, g_att, g_up, ff_got
    )

    att_one = links.send_h(att_one, 1, "g_attA")
    up_here = links.send_x(g_up[1::2], "g_upC")
    ff_last = links.send_on(onward(ff, ff_got, "ff_onward"), "ff")
    (input_grad,) = over_images(
        first_norm_back_kernel,
        "first_norm_back",
        [stream, dr, modulation, *sums(da, da_got, da_last)],
        [(every, BF)],
    )
    g_down = jnp.concatenate(
        [
            sum(v[far:].astype(F32) for v in (g_down[1], *down_mid)),
            sum(v.astype(F32) for v in (g_down[2], *down_last)),
        ],
        axis=0,
    )
    g_down = total(g_down, joined((down_one, down_two)))
    att_one, att_two, up_here, ff_last, g_att, g_up, input_grad = sync(
        att_one, att_two, up_here, ff_last, g_att, g_up, input_grad
    )

    att_two = links.send_h(att_two, 1, "g_attB")
    att_here = links.send_x(g_att[1::2], "g_attC")
    (output,) = over_images(
        output_kernel,
        "output",
        [residual, modulation, *sums(ff, ff_got, ff_last)],
        [(every, BF)],
    )
    g_up = total(
        g_up[1].astype(F32) + sum(v.astype(F32) for v in up_here), joined((up_one, up_two))
    )
    att_two, att_here, g_att, output, input_grad = sync(
        att_two, att_here, g_att, output, input_grad
    )

    input_grad_got = links.leave_group(input_grad, "input_grad")
    att_there = joined((att_one, att_two))
    g_qkv, g_out, squares = unpack_attention_gradient(
        [g_att[1], *att_here, *att_there]
    )
    squares = jnp.sum(squares) + jnp.sum(g_up * g_up) + jnp.sum(g_down * g_down)
    grad_norm = jnp.sqrt(links.total(squares))
    grad_norm, output = sync(grad_norm, output)
    output_got = links.leave_group(output, "output")
    input_grad = come_home("input_grad_home", come, H, input_grad, input_grad_got, F32)
    output = come_home("output_home", come, H, output, output_got, BF)
    factor = jnp.minimum(1.0, clip_limit / (grad_norm + 1e-06))
    one_qkv, two_qkv, new_qkv = (
        v.transpose(1, 0, 2)
        for v in adam_update(
            g_qkv, *(v.transpose(1, 0, 2) for v in (m_qkv, v_qkv, w_qkv)), factor, learn_rate
        )
    )
    one_out, two_out, new_out = adam_update(g_out, m_out, v_out, w_out, factor, output_rate)
    one_up, two_up, new_up = adam_update(g_up, m_up, v_up, w_up, factor, learn_rate)
    one_down, two_down, new_down = adam_update(g_down, m_down, v_down, w_down, factor, learn_rate)
    return (
        output,
        input_grad,
        grad_norm,
        one_qkv,
        one_out,
        one_up,
        one_down,
        two_qkv,
        two_out,
        two_up,
        two_down,
        new_qkv,
        new_out,
        new_up,
        new_down,
    )


def solution(mesh):
    n_dp, n_mp = mesh.shape["dp"], mesh.shape["mp"]
    links = Links(n_dp, n_mp)
    fine = Mesh(mesh.devices.reshape(links.X, 2, links.H, 2, 2), links.axes)
    dp, mp = ("x", "core"), ("h", "p", "q")
    tokens, qkv = P(dp, mp, None), P(dp, None, mp)
    rows, columns = P(mp, dp), P(dp, mp)
    weights = (qkv, rows, columns, rows)
    return jax.shard_map(
        lambda *args: per_device(links, *args),
        mesh=fine,
        in_specs=(tokens, tokens, P(), P(dp), P(dp), P(dp)) + 3 * weights,
        out_specs=(tokens, tokens, P()) + 3 * weights,
        check_vma=False,
    )
```

```python
import jax
import jax.numpy as jnp
from jax import lax
from jax.experimental import pallas as pl
from jax.experimental.pallas import tpu as pltpu
from jax.sharding import Mesh
from jax.sharding import PartitionSpec as P

HD = 128
BINS = 8
ADAM_STEP = 10

clip_limit = 1.0
beta_one = 0.9
beta_two = 0.95
learn_rate = 0.02
output_rate = 0.08
adam_epsilon = 1e-08
decay_rate = 0.01

BF = jnp.bfloat16
F32 = jnp.float32


def adam_update(gradient, moment_one, moment_two, weight, factor, step_rate):
    clipped = gradient * factor
    new_one = beta_one * moment_one + (1.0 - beta_one) * clipped
    new_two = beta_two * moment_two + (1.0 - beta_two) * clipped * clipped
    corrected = new_one / (1.0 - beta_one**ADAM_STEP)
    root_two = jnp.sqrt(new_two / (1.0 - beta_two**ADAM_STEP))
    new_weight = weight - step_rate * (corrected / (root_two + adam_epsilon) + decay_rate * weight)
    return (new_one, new_two, new_weight)


def sync(*values):
    return lax.optimization_barrier(values)


def dot(a, b, contract=(1, 0)):
    return lax.dot_general(
        a, b, (((contract[0],), (contract[1],)), ((), ())), preferred_element_type=F32
    )


def rows_of(ref, columns=slice(None)):
    value = ref[0, :, :, columns]
    return value.reshape(value.shape[0] * value.shape[1], value.shape[2])


def join_tokens(pieces, whole):
    for kind, two in enumerate(pieces):
        for r, ref in enumerate(two):
            t = ref.shape[1]
            whole[0, kind, r * t : (r + 1) * t] = ref[0]


def put_parts(value, columns, parts):
    half = value.shape[0] // (2 * len(parts))
    for kind, (keep, send) in enumerate(parts):
        keep[0, :, columns] = value[2 * kind * half : (2 * kind + 1) * half]
        send[0, :, columns] = value[(2 * kind + 1) * half : (2 * kind + 2) * half]


def softmax_columns(q, k):
    scores = dot(k, q, (1, 1)) * HD ** (-0.5)
    weights = jnp.exp(scores - jnp.max(scores, axis=0, keepdims=True))
    return weights * (1.0 / jnp.sum(weights, axis=0, keepdims=True))


def head_columns(jh, part, n, block):
    start = (jh * 3 + part) * block + n * HD
    return slice(start, start + HD)


class Pieces:
    def __init__(self, refs):
        self.refs, self.at = refs, 0

    def take(self, count):
        self.at += count
        return self.refs[self.at - count : self.at]

    def tokens(self):
        near_far = self.take(4)
        return near_far[:2], near_far[2:]

    def parts(self):
        a, b, c, d = self.take(4)
        return (a, b), (c, d)


class Separate:
    def __init__(self, refs, nd):
        self.refs, self.depth = refs, refs[0].shape[0]
        self.shape = refs[0].shape[1:]

    def block(self, jh, d, rows=slice(None), columns=slice(None)):
        core, x = divmod(d, self.depth)
        return self.refs[2 * jh + core][x, rows, columns]


class Merged:
    def __init__(self, refs):
        self.refs = refs
        x, rows, columns = refs[0].shape
        self.shape = (x * rows, columns)

    def block(self, jh, core, rows=slice(None), columns=slice(None)):
        value = self.refs[2 * jh + core][:, :, columns]
        return value.reshape(self.shape[0], value.shape[2])


def attention_kernel(nh, nd, *refs):
    refs = Pieces(refs)
    tokens, weights = refs.tokens(), Merged(refs.take(2 * nh))
    (a, qkv, o, probs), parts = refs.take(4), refs.parts()
    join_tokens(tokens, a)
    nd = 2
    depth, block = weights.shape[0], weights.shape[1] // 4
    width = 3 * block
    inward = (slice(None), slice(0, width))
    outward = (slice(None), slice(width, width + block))
    kinds, length = a.shape[1], a.shape[2]
    for jh in range(nh):
        total = dot(rows_of(a, slice(0, depth)), weights.block(jh, 0, *inward))
        for d in range(1, nd):
            total += dot(rows_of(a, slice(d * depth, (d + 1) * depth)), weights.block(jh, d, *inward))
        qkv[0, :, :, jh * width : (jh + 1) * width] = total.astype(BF).reshape(kinds, length, width)
    for kind in range(kinds):
        for jh in range(nh):
            for n in range(block // HD):
                q, k, v = (qkv[0, kind, :, head_columns(jh, i, n, block)] for i in range(3))
                p = softmax_columns(q, k).astype(BF)
                probs[0, kind, jh * (block // HD) + n] = p
                out = dot(p, v, (0, 0)).astype(BF)
                o[0, kind, :, jh * block + n * HD : jh * block + (n + 1) * HD] = out
    for d in range(nd):
        total = dot(rows_of(o, slice(0, block)), weights.block(0, d, *outward), (1, 1))
        for jh in range(1, nh):
            total += dot(rows_of(o, slice(jh * block, (jh + 1) * block)), weights.block(jh, d, *outward), (1, 1))
        put_parts(total.astype(BF), slice(d * depth, (d + 1) * depth), parts)


def up_kernel(nh, nd, *refs):
    refs = Pieces(refs)
    b_tokens, wu = refs.tokens(), Merged(refs.take(2 * nh))
    b, hidden, slope = refs.take(3)
    join_tokens(b_tokens, b)
    nd = 2
    depth, width = wu.shape
    kinds, length = b.shape[1], b.shape[2]
    chunk = min(width, 512)
    curve, cubic = 0.7978845608028654, 0.044715
    for jh in range(nh):
        for c in range(0, width, chunk):
            part = slice(c, c + chunk)
            u = dot(rows_of(b, slice(0, depth)), wu.block(jh, 0, columns=part))
            for d in range(1, nd):
                cols = slice(d * depth, (d + 1) * depth)
                u += dot(rows_of(b, cols), wu.block(jh, d, columns=part))
            square = u * u
            t = jnp.tanh(curve * u * (1.0 + cubic * square))
            near = 0.5 * (1.0 + t)
            rise = near + 0.5 * u * (1.0 - t * t) * (curve * (1.0 + 3.0 * cubic * square))
            cols = slice(jh * width + c, jh * width + c + chunk)
            hidden[0, :, :, cols] = (u * near).astype(BF).reshape(kinds, length, chunk)
            slope[0, :, :, cols] = rise.astype(BF).reshape(kinds, length, chunk)


def up_back_kernel(nh, nd, *refs):
    refs = Pieces(refs)
    df_tokens, (slope,) = refs.tokens(), refs.take(1)
    wu, wd = Merged(refs.take(2 * nh)), Separate(refs.take(2 * nh), nd)
    (df, du), parts = refs.take(2), refs.parts()
    join_tokens(df_tokens, df)
    width, depth = wd.shape
    kinds, length = df.shape[1], df.shape[2]
    chunk = min(width, 512)
    for jh in range(nh):
        for c in range(0, width, chunk):
            part = slice(c, c + chunk)
            dh = dot(rows_of(df, slice(0, depth)), wd.block(jh, 0, part), (1, 1))
            for d in range(1, nd):
                cols = slice(d * depth, (d + 1) * depth)
                dh += dot(rows_of(df, cols), wd.block(jh, d, part), (1, 1))
            cols = slice(jh * width + c, jh * width + c + chunk)
            value = dh * rows_of(slope, cols).astype(F32)
            du[0, :, :, cols] = value.astype(BF).reshape(kinds, length, chunk)
    depth = wu.shape[0]
    for d in range(2):
        total = dot(rows_of(du, slice(0, width)), wu.block(0, d), (1, 1))
        for jh in range(1, nh):
            total += dot(rows_of(du, slice(jh * width, (jh + 1) * width)), wu.block(jh, d), (1, 1))
        put_parts(total.astype(BF), slice(d * depth, (d + 1) * depth), parts)


def down_kernel(nh, nd, *refs):
    refs = Pieces(refs)
    (hidden,), wd = refs.take(1), Separate(refs.take(2 * nh), nd)
    parts = refs.parts()
    width, depth = wd.shape
    for d in range(nd):
        total = dot(rows_of(hidden, slice(0, width)), wd.block(0, d))
        for jh in range(1, nh):
            total += dot(rows_of(hidden, slice(jh * width, (jh + 1) * width)), wd.block(jh, d))
        put_parts(total.astype(BF), slice(d * depth, (d + 1) * depth), parts)


def attention_back_kernel(nh, nd, *refs):
    refs = Pieces(refs)
    (a, o), tokens, (qkv, probs) = refs.take(2), refs.tokens(), refs.take(2)
    weights = Merged(refs.take(2 * nh))
    parts, (datt_out, dqkv_out, sent, all_datt, all_dqkv) = refs.parts(), refs.take(5)
    step = pl.program_id(0)
    datt, dqkv = (v.at[pl.ds(step, 1)] for v in (all_datt, all_dqkv))
    join_tokens(tokens, datt)
    nd = 2
    depth, block = weights.shape[0], weights.shape[1] // 4
    width = 3 * block
    inward = (slice(None), slice(0, width))
    outward = (slice(None), slice(width, width + block))
    kinds, length = datt.shape[1], datt.shape[2]
    for jh in range(nh):
        do_all = dot(rows_of(datt, slice(0, depth)), weights.block(jh, 0, *outward))
        for d in range(1, nd):
            do_all += dot(rows_of(datt, slice(d * depth, (d + 1) * depth)), weights.block(jh, d, *outward))
        do_all = do_all.astype(BF)
        for kind in range(kinds):
            for n in range(block // HD):
                q, k, v = (qkv[0, kind, :, head_columns(jh, i, n, block)] for i in range(3))
                do = do_all[kind * length : (kind + 1) * length, n * HD : (n + 1) * HD]
                rounded = probs[0, kind, jh * (block // HD) + n]
                dv = dot(rounded, do)
                dp = dot(v, do, (1, 1))
                p = rounded.astype(F32)
                ds = (p * (dp - jnp.sum(p * dp, axis=0, keepdims=True))).astype(BF)
                dq = dot(ds, k, (0, 0)) * HD ** (-0.5)
                dk = dot(ds, q) * HD ** (-0.5)
                for i, value in enumerate((dq, dk, dv)):
                    dqkv[0, kind, :, head_columns(jh, i, n, block)] = value.astype(BF)
    for d in range(nd):
        total = dot(rows_of(dqkv, slice(0, width)), weights.block(0, d, *inward), (1, 1))
        for jh in range(1, nh):
            total += dot(rows_of(dqkv, slice(jh * width, (jh + 1) * width)), weights.block(jh, d, *inward), (1, 1))
        put_parts(total.astype(BF), slice(d * depth, (d + 1) * depth), parts)
    datt_out[...] = datt[...]
    dqkv_out[...] = dqkv[...]
    across, both = nd // 2, width + block

    def every_row(ref, columns=slice(None)):
        value = ref[:, :, :, columns]
        return value.reshape(-1, value.shape[-1])

    @pl.when(step == pl.num_programs(0) - 1)
    def _():
        for jx in range(across):
            cols = slice((across + jx) * depth, (across + jx + 1) * depth)
            inward = dot(a[cols], every_row(all_dqkv)).astype(BF)
            outward = dot(every_row(all_datt, cols), every_row(o), (0, 0)).astype(BF)
            rows = slice(jx * depth, (jx + 1) * depth)
            for jh in range(nh):
                at = jh * both
                sent[rows, at : at + width] = inward[:, jh * width : (jh + 1) * width]
                sent[rows, at + width : at + both] = outward[:, jh * block : (jh + 1) * block]


def group_call(
    kernel, name, nh, nd, steps, blocked, whole, outs, resident=(), whole_outs=(), scratch=()
):
    def cut(shape):
        zeros = (0,) * (len(shape) - 1)
        return pl.BlockSpec((1,) + tuple(shape[1:]), lambda i: (i,) + zeros)

    def stay(shape):
        zeros = (0,) * len(shape)
        return pl.BlockSpec(tuple(shape), lambda i: zeros)

    return pl.pallas_call(
        lambda *refs: kernel(nh, nd, *refs),
        name=name,
        grid=(steps,),
        in_specs=[stay(v.shape) for v in resident]
        + [cut(v.shape) for v in blocked]
        + [pl.BlockSpec(memory_space=pltpu.VMEM)] * len(whole),
        out_specs=[cut(s) for s in outs] + [stay(s) for s in whole_outs],
        out_shape=[jax.ShapeDtypeStruct(s, BF) for s in (*outs, *whole_outs)],
        scratch_shapes=[pltpu.VMEM(shape, BF) for shape in scratch],
        compiler_params=pltpu.CompilerParams(vmem_limit_bytes=62 * 2**20),
        cost_estimate=pl.CostEstimate(flops=0, bytes_accessed=0, transcendentals=0),
    )(*resident, *blocked, *whole)


def image_call(kernel, name, steps, arrays, outs):
    def seen(shape):
        return (2, steps, *shape[1:]) if shape[0] == 2 * steps else tuple(shape)

    def cut(shape):
        zeros = (0,) * (len(shape) - 2)
        if shape[0] == 2 and len(shape) == 4:
            return pl.BlockSpec((2, 1, *shape[2:]), lambda i: (0, i, *zeros))
        return pl.BlockSpec((1, *shape[1:]), lambda i: (i, 0, *zeros))

    made = pl.pallas_call(
        kernel,
        name=name,
        grid=(steps,),
        in_specs=[cut(seen(v.shape)) for v in arrays],
        out_specs=[cut(seen(shape)) for shape, _ in outs],
        out_shape=[jax.ShapeDtypeStruct(seen(shape), dtype) for shape, dtype in outs],
        compiler_params=pltpu.CompilerParams(vmem_limit_bytes=32 * 2**20),
        cost_estimate=pl.CostEstimate(flops=0, bytes_accessed=0, transcendentals=0),
    )(*[v.reshape(seen(v.shape)) for v in arrays])
    return [v.reshape(shape) for v, (shape, _) in zip(made, outs)]


def move_call(kernel, name, table, arrays, outs):
    def whole(shape):
        zeros = (0,) * len(shape)
        return pl.BlockSpec(tuple(shape), lambda i, table: zeros)

    return pl.pallas_call(
        kernel,
        name=name,
        grid_spec=pltpu.PrefetchScalarGridSpec(
            num_scalar_prefetch=1,
            grid=(1,),
            in_specs=[whole(v.shape) for v in arrays],
            out_specs=[whole(shape) for shape, _ in outs],
        ),
        out_shape=[jax.ShapeDtypeStruct(shape, dtype) for shape, dtype in outs],
        compiler_params=pltpu.CompilerParams(vmem_limit_bytes=32 * 2**20),
        cost_estimate=pl.CostEstimate(flops=0, bytes_accessed=0, transcendentals=0),
    )(table, *arrays)


def leave_home(name, table, groups, v):
    slots, t, D = v.shape
    blocks, images = table.shape[0] - groups, slots // groups
    width = D // blocks

    def kernel(table, v, *outs):
        for jh in range(groups):
            picked = pl.ds(table[jh] * images, images)
            for e in range(blocks):
                columns = pl.ds(pl.multiple_of(table[groups + e] * width, width), width)
                outs[jh][:, :, e * width : (e + 1) * width] = v[picked, :, columns].astype(BF)

    return move_call(kernel, name, table, [v], [((images, t, D), BF)] * groups)


def come_home(name, table, groups, own, received, dtype):
    images, length, D = own.shape
    blocks, t = table.shape[0] - groups, length // groups
    width = D // blocks

    def kernel(table, own, *refs):
        *received, out = refs
        for jh in range(groups):
            picked = pl.ds(table[jh] * images, images)
            for e in range(blocks):
                columns = pl.ds(pl.multiple_of(table[groups + e] * width, width), width)
                part = received[jh - 1][:, :, columns] if jh else own[:, :t, columns]
                out[picked, :, e * width : (e + 1) * width] = part.astype(dtype)

    shape = (images * groups, t, D)
    return move_call(kernel, name, table, [own, *received], [(shape, dtype)])[0]


def row_parts(values):
    center = values - jnp.mean(values, axis=-1, keepdims=True)
    factor = lax.rsqrt(jnp.mean(center * center, axis=-1, keepdims=True) + 1e-06)
    return center * factor, factor


def norm_back(values, gradient):
    rows, factor = row_parts(values)
    return factor * (
        gradient
        - jnp.mean(gradient, axis=-1, keepdims=True)
        - rows * jnp.mean(gradient * rows, axis=-1, keepdims=True)
    )


def token_sum(sums, kind):
    keep, got, last = sums[kind], sums[2 + kind], sums[4 + kind]
    t = last.shape[1]
    return keep[0, :t].astype(F32) + got[0, :t].astype(F32) + last[0].astype(F32)


def first_norm_kernel(stream, mod, *a):
    for kind in range(2):
        rows, _ = row_parts(stream[kind, 0].astype(F32))
        a[kind][0] = (rows * mod[kind, 0, 1:2] + mod[kind, 0, 0:1]).astype(BF)


def loss_kernel(cot, weight, mod, *df):
    for kind in range(2):
        seed = cot[kind, 0].astype(F32) * weight[kind, 0]
        df[kind][0] = (mod[kind, 0, 5:6] * seed).astype(BF)


def second_norm_kernel(stream, mod, *refs):
    sums, residual, b = refs[:6], refs[6], refs[7:]
    for kind in range(2):
        r = stream[kind, 0].astype(F32) + mod[kind, 0, 2:3] * token_sum(sums, kind)
        residual[kind, 0] = r
        rows, _ = row_parts(r)
        b[kind][0] = (rows * mod[kind, 0, 4:5] + mod[kind, 0, 3:4]).astype(BF)


def second_norm_back_kernel(cot, weight, residual, mod, *refs):
    sums, dr, datt = refs[:6], refs[6], refs[7:]
    for kind in range(2):
        seed = cot[kind, 0].astype(F32) * weight[kind, 0]
        g = seed + norm_back(residual[kind, 0], token_sum(sums, kind) * mod[kind, 0, 4:5])
        dr[kind, 0] = g
        datt[kind][0] = (mod[kind, 0, 2:3] * g).astype(BF)


def first_norm_back_kernel(stream, dr, mod, *refs):
    sums, out = refs[:6], refs[6]
    for kind in range(2):
        g = norm_back(stream[kind, 0].astype(F32), token_sum(sums, kind) * mod[kind, 0, 1:2])
        out[kind, 0] = (dr[kind, 0] + g).astype(BF)


def output_kernel(residual, mod, *refs):
    sums, out = refs[:6], refs[6]
    for kind in range(2):
        out[kind, 0] = (residual[kind, 0] + mod[kind, 0, 5:6] * token_sum(sums, kind)).astype(BF)


def rounded(weights):
    def kernel(*refs):
        for source, copy in zip(refs[: len(weights)], refs[len(weights) :]):
            copy[...] = source[...].astype(BF)

    halves = [pl.BlockSpec((v.shape[0] // 2, v.shape[1]), lambda i: (i, 0)) for v in weights]
    return pl.pallas_call(
        kernel,
        name="rounded",
        grid=(2,),
        in_specs=halves,
        out_specs=halves,
        out_shape=[jax.ShapeDtypeStruct(v.shape, BF) for v in weights],
        compiler_params=pltpu.CompilerParams(vmem_limit_bytes=32 * 2**20),
        cost_estimate=pl.CostEstimate(flops=0, bytes_accessed=0, transcendentals=0),
    )(*weights)


def pack_attention_weights(w_qkv, w_out):
    depth, _, block = w_qkv.shape

    def kernel(inward, outward, packed):
        for i in range(3):
            packed[:, i * block : (i + 1) * block] = inward[i].astype(BF)
        packed[:, 3 * block :] = outward[...].T.astype(BF)

    return pl.pallas_call(
        kernel,
        name="pack",
        out_shape=jax.ShapeDtypeStruct((depth, 4 * block), BF),
        compiler_params=pltpu.CompilerParams(vmem_limit_bytes=32 * 2**20),
        cost_estimate=pl.CostEstimate(flops=0, bytes_accessed=0, transcendentals=0),
    )(w_qkv.transpose(1, 0, 2), w_out)


def gradient(name, nh, nd, left, right, left_is_hidden, core):
    rows = left.shape[0]
    hidden, features = (left, right) if left_is_hidden else (right, left)
    h_width, d_width, half = hidden.shape[1] // nh, features.shape[1] // nd, nd // 2

    def kernel(left, right, out):
        out[...] = dot(left[...], right[...], (0, 0)).astype(BF)

    h_spec = pl.BlockSpec((rows, h_width), lambda jh, d: (0, jh))
    d_spec = pl.BlockSpec((rows, d_width), lambda jh, d: (0, core * half + d))
    if left_is_hidden:
        in_specs, out_spec = [h_spec, d_spec], pl.BlockSpec((h_width, d_width), lambda jh, d: (jh, d))
        shape = (nh * h_width, half * d_width)
    else:
        in_specs, out_spec = [d_spec, h_spec], pl.BlockSpec((d_width, h_width), lambda jh, d: (d, jh))
        shape = (half * d_width, nh * h_width)
    return pl.pallas_call(
        kernel,
        name=name,
        grid=(nh, half),
        in_specs=in_specs,
        out_specs=out_spec,
        out_shape=jax.ShapeDtypeStruct(shape, BF),
        compiler_params=pltpu.CompilerParams(vmem_limit_bytes=48 * 2**20),
        cost_estimate=pl.CostEstimate(flops=0, bytes_accessed=0, transcendentals=0),
    )(left, right)


def one_step(kernel, name, arrays, columns, outs, dtype=BF):
    return pl.pallas_call(
        kernel,
        name=name,
        grid=(1,),
        in_specs=[
            pl.BlockSpec((v.shape[0], c or v.shape[1]), lambda i: (0, 0))
            for v, c in zip(arrays, columns)
        ],
        out_specs=[pl.BlockSpec(shape, lambda i: (0, 0)) for shape in outs],
        out_shape=[jax.ShapeDtypeStruct(shape, dtype) for shape in outs],
        compiler_params=pltpu.CompilerParams(vmem_limit_bytes=60 * 2**20),
        cost_estimate=pl.CostEstimate(flops=0, bytes_accessed=0, transcendentals=0),
    )(*arrays)


def down_kept(nh, nd, hidden, df, sent):
    half = nd // 2
    height, width = hidden.shape[1] // nh, df.shape[1] // nd
    cut = height // 2

    def kernel(hidden, df, sent, *outs):
        for jx in range(half):
            one, two, three = outs[3 * jx : 3 * jx + 3]
            cols = slice(jx * width, (jx + 1) * width)
            for jh in range(nh):
                rows = slice(jh * height, (jh + 1) * height)
                g = dot(hidden[:, rows], df[:, cols], (0, 0)) + sent[rows, cols].astype(F32)
                g = g.astype(BF)
                if jh:
                    one[(jh - 1) * cut : jh * cut] = g[:cut]
                    two[(jh - 1) * cut : jh * cut] = g[cut:]
                else:
                    two[(nh - 1) * cut :] = g[:cut]
                    three[...] = g[cut:]

    shapes = [((nh - 1) * cut, width), (nh * cut, width), (cut, width)] * half
    return one_step(kernel, "g_down_keep", (hidden, df, sent), (None, half * width, None), shapes)


def up_kept(nh, nd, b, du, sent):
    half = nd // 2
    height, width = b.shape[1] // nd, du.shape[1] // nh

    def kernel(b, du, sent, *outs):
        for jx in range(half):
            far, here = outs[2 * jx : 2 * jx + 2]
            rows = slice(jx * height, (jx + 1) * height)
            for jh in range(nh):
                cols = slice(jh * width, (jh + 1) * width)
                g = dot(b[:, rows], du[:, cols], (0, 0)) + sent[rows, cols].astype(F32)
                if jh:
                    far[:, (jh - 1) * width : jh * width] = g.astype(BF)
                else:
                    here[...] = g.astype(BF)

    shapes = [(height, (nh - 1) * width), (height, width)] * half
    return one_step(kernel, "g_up_keep", (b, du, sent), (half * height, None, None), shapes)


def attention_kept(nh, nd, a, dqkv, datt, o, sent):
    half = nd // 2
    height = a.shape[0] // nd
    width, block = dqkv.shape[1] // nh, o.shape[1] // nh
    both = width + block

    def kernel(a, dqkv, datt, o, sent, *outs):
        for jx in range(half):
            far, here = outs[2 * jx : 2 * jx + 2]
            rows = slice(jx * height, (jx + 1) * height)
            inward = dot(a[rows], dqkv[...])
            outward = dot(datt[:, rows], o[...], (0, 0))
            for jh in range(nh):
                out, at = (far, (jh - 1) * both) if jh else (here, 0)
                terms = sent[rows, jh * both : (jh + 1) * both].astype(F32)
                g = inward[:, jh * width : (jh + 1) * width] + terms[:, :width]
                out[:, at : at + width] = g.astype(BF)
                g = outward[:, jh * block : (jh + 1) * block] + terms[:, width:]
                out[:, at + width : at + both] = g.astype(BF)

    shapes = [(height, (nh - 1) * both), (height, both)] * half
    cols = half * height
    return one_step(
        kernel, "g_att_keep", (a, dqkv, datt, o, sent), (None, None, cols, None, None), shapes
    )


def add_terms(name, terms, cuts=1, rows=None):
    rows, width = rows or terms[0].shape[0], terms[0].shape[1]
    size = rows // cuts

    def kernel(*refs):
        terms, outs = refs[: len(refs) - cuts], refs[len(refs) - cuts :]
        for c, out in enumerate(outs):
            out[...] = sum(
                v[c * size : (c + 1) * size].astype(F32) for v in terms
            ).astype(BF)

    return one_step(kernel, name, terms, [None] * len(terms), [(size, width)] * cuts)


def onward_kernel(*refs):
    for kind in range(2):
        keep, got, out = refs[kind], refs[2 + kind], refs[4 + kind]
        t = out.shape[1]
        out[0] = (keep[0, t:].astype(F32) + got[0, t:].astype(F32)).astype(BF)


def unpack_attention_gradient(terms):
    depth, width = terms[0].shape
    block = width // 4

    def kernel(*refs):
        *terms, inward, outward, squares = refs
        total = sum(v[...].astype(F32) for v in terms)
        square = total * total
        squares[...] = sum(
            jnp.sum(square[:, c : c + 128].reshape(depth // 8, 8, 128), axis=0)
            for c in range(0, width, 128)
        )
        for i in range(3):
            inward[i] = total[:, i * block : (i + 1) * block]
        outward[...] = total[:, 3 * block :].T

    return pl.pallas_call(
        kernel,
        name="unpack",
        out_shape=[
            jax.ShapeDtypeStruct((3, depth, block), F32),
            jax.ShapeDtypeStruct((block, depth), F32),
            jax.ShapeDtypeStruct((8, 128), F32),
        ],
        compiler_params=pltpu.CompilerParams(vmem_limit_bytes=32 * 2**20),
        cost_estimate=pl.CostEstimate(flops=0, bytes_accessed=0, transcendentals=0),
    )(*terms)


class Links:
    axes = ("x", "core", "h", "p", "q")

    def __init__(self, n_dp, n_mp):
        self.X, self.H = n_dp // 2, n_mp // 4
        self.n_dp, self.n_mp = n_dp, n_mp

    def shifted(self, v, axis, size, offset, name):
        with jax.named_scope(f"{name}_{axis}"):
            return lax.ppermute(v, axis, [((dst + offset) % size, dst) for dst in range(size)])

    def from_core(self, v, name):
        return self.shifted(v, "core", 2, 1, name)

    def from_x(self, v, jx, name):
        return self.shifted(v, "x", self.X, jx, name)

    def from_h(self, v, jh, name):
        return self.shifted(v, "h", self.H, jh, name)

    def over_h(self, w, name):
        return [self.from_h(w, jh, name) for jh in range(1, self.H)]

    def over_x(self, w, name):
        return [self.from_x(w, jx, name) for jx in range(1, self.X)]

    def send_x(self, parts, name):
        return [self.from_x(parts[jx], -jx, name) for jx in range(1, self.X)]

    def send_h(self, g, h, name):
        width = g.shape[h] // (self.H - 1)
        return [
            self.from_h(lax.slice_in_dim(g, (jh - 1) * width, jh * width, axis=h), -jh, name)
            for jh in range(1, self.H)
        ]

    def tables(self):
        x, core, h = (lax.axis_index(axis) for axis in self.axes[:3])
        groups = [(h - jh) % self.H for jh in range(self.H)]
        here = [
            ((x + jx) % self.X) * 2 + (core ^ jc) for jc in range(2) for jx in range(self.X)
        ]
        home = [((e % 2) ^ core) * self.X + (e // 2 - x) % self.X for e in range(self.n_dp)]
        return [jnp.stack(groups + rest).astype(jnp.int32) for rest in (here, home)]

    def to_group(self, parts, name):
        return [self.from_h(parts[jh], jh, name) for jh in range(1, self.H)]

    def leave_group(self, v, name):
        tokens = v.shape[1] // self.H
        return [
            self.from_h(v[:, jh * tokens : (jh + 1) * tokens], -jh, name) for jh in range(1, self.H)
        ]

    def over(self, v, kind, late, name):
        return self.shifted(v, "p" if (kind == 0) != late else "q", 2, 1, f"{name}{kind}")

    def first_hop(self, own, name):
        return [(own[k], self.over(own[k], k, False, name)) for k in range(2)]

    def near(self, hops):
        return [jnp.concatenate(pair, axis=1) for pair in hops]

    def last_hop(self, near, name):
        return [self.over(near[k], k, True, name) for k in (1, 0)][::-1]

    def send_late(self, parts, name):
        return [self.over(parts[2 * k + 1], k, True, name) for k in (1, 0)][::-1]

    def send_on(self, onward, name):
        return [self.over(onward[k], k, False, name) for k in range(2)]

    def features_here(self, v):
        x, c = lax.axis_index("x"), lax.axis_index("core")
        width = v.shape[-1] // self.n_dp
        return jnp.concatenate(
            [
                lax.dynamic_slice_in_dim(
                    v, (((x + jx) % self.X) * 2 + (c ^ jc)) * width, width, axis=v.ndim - 1
                )
                for jc in range(2)
                for jx in range(self.X)
            ],
            axis=-1,
        )

    def total(self, v):
        for axis, size in (("p", 2), ("core", 2), ("q", 2), ("x", self.X), ("h", self.H)):
            step = 1
            while step < size:
                with jax.named_scope("norm"):
                    v = v + lax.ppermute(v, axis, [(i ^ step, i) for i in range(size)])
                step *= 2
        return v


def per_device(
    links,
    stream_in,
    cotangent,
    noise_table,
    timesteps,
    bins,
    counts,
    w_qkv,
    w_out,
    w_up,
    w_down,
    m_qkv,
    m_out,
    m_up,
    m_down,
    v_qkv,
    v_out,
    v_up,
    v_down,
):
    H = links.H
    slots, _, D = stream_in.shape
    images = slots // H
    here = lax.axis_index("h")

    steps_here = lax.dynamic_slice_in_dim(timesteps, here * images, images)
    table_rows = noise_table.shape[0]
    picks = (steps_here[:, None] == jnp.arange(table_rows)[None, :]).astype(F32)
    modulation = jnp.dot(
        picks, noise_table.reshape(table_rows, -1), precision=lax.Precision.HIGHEST
    ).reshape(images, 6, D)
    modulation = links.features_here(modulation)
    live = jnp.arange(slots) < counts[0]
    loss_scale = live.astype(F32) * (bins.astype(F32) + 1.0) / BINS
    loss_scale = lax.dynamic_slice_in_dim(loss_scale, here * images, images)
    loss_scale = jnp.broadcast_to(loss_scale[:, None, None], (images, 1, D))

    block = w_qkv.shape[2]
    length = stream_in.shape[1] * H * 4
    steps = images // 2
    rows = images * length
    nh, nd = H, 2 * links.X
    heads = H * block
    hidden_width = H * w_up.shape[1]
    whole = lambda width: (steps, 2, length, width)
    parts = [(steps, length // 2, D)] * 4

    tokens = length // 4
    every, kinds = (images, tokens, D), [((steps, tokens, D), BF)] * 2

    def over_images(kernel, name, arrays, outs):
        return image_call(kernel, name, steps, arrays, outs)

    def onward(parts, got, name):
        arrays = [parts[0], parts[2], *got]
        return over_images(onward_kernel, name, arrays, kinds)

    def sums(parts, got, last):
        return [parts[0], parts[2], *got, *last]

    def flat(v):
        return v.reshape(rows, v.shape[-1])

    def call(kernel, name, blocked, weights, outs, *staying):
        return list(group_call(kernel, name, nh, nd, steps, blocked, weights, outs, *staying))

    def halves(w):
        size = w.shape[0] // 2
        return w[:size], w[size:]

    def joined(pair):
        return [jnp.concatenate(two, axis=0) for two in zip(*pair)]

    def total(here, there):
        return here + sum(v.astype(F32) for v in there)

    leave, come = links.tables()
    stream_parts = leave_home("stream_leaves", leave, H, stream_in)
    packed = pack_attention_weights(w_qkv, w_out)
    stream_got = links.to_group(stream_parts, "stream")
    x_packed = links.over_x(packed, "wqo0")
    up, down = rounded([w_up, w_down])
    stream_parts, stream_got, x_packed, packed, up, down = sync(
        stream_parts, stream_got, x_packed, packed, up, down
    )

    stream = jnp.concatenate([stream_parts[0], *stream_got], axis=1)
    a_own = over_images(first_norm_kernel, "first_norm", [stream, modulation], kinds)
    a_hops = links.first_hop(a_own, "a")
    packed_one, packed_two = halves(packed)
    far_one = links.over_h(packed_one, "wqoA")
    x_up = links.over_x(up, "wu0")
    wqo = [jnp.stack([packed, *x_packed])]
    a_hops, far_one, x_up, wqo, packed_two = sync(a_hops, far_one, x_up, wqo, packed_two)
    a_near = links.near(a_hops)

    far_two = links.over_h(packed_two, "wqoB")
    a_far = links.last_hop(a_near, "a")
    x_one = [links.over_x(w, "wqoA1") for w in far_one]
    cot_parts = leave_home("cot_leaves", leave, H, cotangent)
    cot_one = [v[:steps] for v in cot_parts]
    cot_two = [v[steps:] for v in cot_parts]
    wu = [jnp.stack([up, *x_up])]
    a_far, far_two, x_one, cot_one, cot_two, wqo, wu = sync(
        a_far, far_two, x_one, cot_one, cot_two, wqo, wu
    )

    x_two = [links.over_x(w, "wqoB1") for w in far_two]
    cot_one = [cot_one[0], *links.to_group(cot_one, "cotA")]
    wqo.append(links.from_core(wqo[0], "wqo0"))
    wu.append(links.from_core(wu[0], "wu0"))
    packed_far = joined((far_one, far_two))
    packed_far, x_two, cot_one, cot_two, wqo, wu = sync(
        packed_far, x_two, cot_one, cot_two, wqo, wu
    )

    cot_two = [cot_two[0], *links.to_group(cot_two, "cotB")]
    for w, one, two in zip(packed_far, x_one, x_two):
        wqo.append(jnp.stack([w, *joined((one, two))]))
        wqo.append(links.from_core(wqo[-1], "wqo1"))
    up_one, up_two = halves(up)
    cot_one, cot_two, wqo, up_one, up_two, down = sync(cot_one, cot_two, wqo, up_one, up_two, down)

    cot = jnp.concatenate([jnp.concatenate(v, axis=1) for v in (cot_one, cot_two)], axis=0)
    df_own = over_images(loss_kernel, "loss", [cot, loss_scale, modulation], kinds)
    up_one = links.over_h(up_one, "wuA")
    df_hops = links.first_hop(df_own, "df")
    x_down = links.over_x(down, "wd0")
    a_rows, qkv, o, probs, *att = call(
        attention_kernel,
        "attention",
        [a_near[0], a_far[0], a_near[1], a_far[1]],
        wqo,
        [whole(D), whole(3 * heads), whole(heads), (steps, 2, heads // HD, length, length), *parts],
    )
    df_hops, att, up_one, up_two, x_down = sync(df_hops, att, up_one, up_two, x_down)

    up_two = links.over_h(up_two, "wuB")
    att_got = links.send_late(att, "att")
    wd = [jnp.stack([down, *x_down])]
    wd.append(links.from_core(wd[0], "wd0"))
    att_got, up_two, wd, down = sync(att_got, up_two, wd, down)

    down_one, down_two = halves(down)
    down_one = links.over_h(down_one, "wdA")
    att_last = links.send_on(onward(att, att_got, "att_onward"), "att")
    up_far = joined((up_one, up_two))
    x_up = [links.over_x(w, "wu1") for w in up_far]
    residual, *b = over_images(
        second_norm_kernel,
        "second_norm",
        [stream, modulation, *sums(att, att_got, att_last)],
        [(every, F32), *kinds],
    )
    b, down_one, up_far, x_up, down_two = sync(b, down_one, up_far, x_up, down_two)

    down_two = links.over_h(down_two, "wdB")
    b_hops = links.first_hop(b, "b")
    x_one = [links.over_x(w, "wdA1") for w in down_one]
    wu_far = [jnp.stack([w, *others]) for w, others in zip(up_far, x_up)]
    b_near, down_two, x_one, wu_far, df_hops = sync(
        links.near(b_hops), down_two, x_one, wu_far, df_hops
    )

    b_far = links.last_hop(b_near, "b")
    df_near = links.near(df_hops)
    x_two = [links.over_x(w, "wdB1") for w in down_two]
    for w in wu_far:
        wu += [w, links.from_core(w, "wu1")]
    b_far, x_two, wu, df_near = sync(b_far, x_two, wu, df_near)

    df_far = links.last_hop(df_near, "df")
    for w, one, two in zip(joined((down_one, down_two)), x_one, x_two):
        wd.append(jnp.stack([w, *joined((one, two))]))
        wd.append(links.from_core(wd[-1], "wd1"))
    b_rows, hidden, slope = call(
        up_kernel,
        "up",
        [b_near[0], b_far[0], b_near[1], b_far[1]],
        wu,
        [whole(D), whole(hidden_width), whole(hidden_width)],
    )
    df_far, wd, b_rows, hidden, slope = sync(df_far, wd, b_rows, hidden, slope)

    df_rows, du, *db = call(
        up_back_kernel,
        "up_back",
        [df_near[0], df_far[0], df_near[1], df_far[1], slope],
        wu + wd,
        [whole(D), whole(hidden_width), *parts],
    )
    b_rows, df_rows, hidden, du, db, a_rows = sync(b_rows, df_rows, hidden, du, db, a_rows)

    db_got = links.send_late(db, "db")
    down_send = gradient("g_down_send", nh, nd, flat(hidden), flat(df_rows), True, 1)
    up_send = gradient("g_up_send", nh, nd, flat(b_rows), flat(du), False, 1)
    a_columns = flat(a_rows).T
    db_got, down_send, up_send, b_rows, du, hidden, df_rows, a_columns = sync(
        db_got, down_send, up_send, b_rows, du, hidden, df_rows, a_columns
    )

    db_last = links.send_on(onward(db, db_got, "db_onward"), "db")
    down_sent = links.from_core(down_send, "g_down")
    g_down = down_kept(nh, nd, flat(hidden), flat(df_rows), down_sent)
    db_last, g_down, up_send, b_rows, du, hidden = sync(
        db_last, g_down, up_send, b_rows, du, hidden
    )

    dr, *datt_own = over_images(
        second_norm_back_kernel,
        "second_norm_back",
        [cot, loss_scale, residual, modulation, *sums(db, db_got, db_last)],
        [(every, F32), *kinds],
    )
    datt_hops = links.first_hop(datt_own, "datt")
    down_one = links.send_x(g_down[0::3], "g_downA")
    up_sent = links.from_core(up_send, "g_up")
    (down_one,) = add_terms("g_downA_sum", [g_down[0], *down_one])
    datt_hops, g_down, down_one, up_sent, b_rows, du, hidden = sync(
        datt_hops, g_down, down_one, up_sent, b_rows, du, hidden
    )
    datt_near = links.near(datt_hops)

    down_one = links.send_h(down_one, 0, "g_downA")
    datt_far = links.last_hop(datt_near, "datt")
    down_mid = links.send_x(g_down[1::3], "g_downB")
    ff = call(down_kernel, "down", [hidden], wd, parts)
    g_up = up_kept(nh, nd, flat(b_rows), flat(du), up_sent)
    far = (nh - 1) * (g_down[1].shape[0] // nh)
    (down_two,) = add_terms("g_downB_sum", [g_down[1], *down_mid], 1, far)
    datt_far, down_one, down_mid, down_two, g_down, g_up, ff = sync(
        datt_far, down_one, down_mid, down_two, g_down, g_up, ff
    )

    down_two = links.send_h(down_two, 0, "g_downB")
    up_far = links.send_x(g_up[0::2], "g_upA")
    ff_got = links.send_late(ff, "ff")
    *da, datt, dqkv, att_send = call(
        attention_back_kernel,
        "attention_back",
        [datt_near[0], datt_far[0], datt_near[1], datt_far[1], qkv, probs],
        wqo,
        [*parts, whole(D), whole(3 * heads)],
        (a_columns, o),
        [(D // 2, 4 * heads)],
        (whole(D), whole(3 * heads)),
    )
    down_two, up_far, ff_got, datt, dqkv, da, att_send, g_up, g_down = sync(
        down_two, up_far, ff_got, datt, dqkv, da, att_send, g_up, g_down
    )

    up_one, up_two = add_terms("g_upA_sum", [g_up[0], *up_far], 2)
    up_one = links.send_h(up_one, 1, "g_upA")
    da_got = links.send_late(da, "da")
    att_sent = links.from_core(att_send, "g_att")
    down_last = links.send_x(g_down[2::3], "g_downC")
    g_att = attention_kept(nh, nd, a_columns, flat(dqkv), flat(datt), flat(o), att_sent)
    da_got, g_att, g_up, up_one, up_two, da, ff_got, down_last = sync(
        da_got, g_att, g_up, up_one, up_two, da, ff_got, down_last
    )

    up_two = links.send_h(up_two, 1, "g_upB")
    att_far = links.send_x(g_att[0::2], "g_attA")
    da_last = links.send_on(onward(da, da_got, "da_onward"), "da")
    att_one, att_two = add_terms("g_attA_sum", [g_att[0], *att_far], 2)
    att_one, att_two, up_two, da_last, g_att, g_up, ff_got = sync(
        att_one, att_two, up_two, da_last, g_att, g_up, ff_got
    )

    att_one = links.send_h(att_one, 1, "g_attA")
    up_here = links.send_x(g_up[1::2], "g_upC")
    ff_last = links.send_on(onward(ff, ff_got, "ff_onward"), "ff")
    (input_grad,) = over_images(
        first_norm_back_kernel,
        "first_norm_back",
        [stream, dr, modulation, *sums(da, da_got, da_last)],
        [(every, BF)],
    )
    g_down = jnp.concatenate(
        [
            sum(v[far:].astype(F32) for v in (g_down[1], *down_mid)),
            sum(v.astype(F32) for v in (g_down[2], *down_last)),
        ],
        axis=0,
    )
    g_down = total(g_down, joined((down_one, down_two)))
    att_one, att_two, up_here, ff_last, g_att, g_up, input_grad = sync(
        att_one, att_two, up_here, ff_last, g_att, g_up, input_grad
    )

    att_two = links.send_h(att_two, 1, "g_attB")
    att_here = links.send_x(g_att[1::2], "g_attC")
    (output,) = over_images(
        output_kernel,
        "output",
        [residual, modulation, *sums(ff, ff_got, ff_last)],
        [(every, BF)],
    )
    g_up = total(
        g_up[1].astype(F32) + sum(v.astype(F32) for v in up_here), joined((up_one, up_two))
    )
    att_two, att_here, g_att, output, input_grad = sync(
        att_two, att_here, g_att, output, input_grad
    )

    input_grad_got = links.leave_group(input_grad, "input_grad")
    att_there = joined((att_one, att_two))
    g_qkv, g_out, squares = unpack_attention_gradient(
        [g_att[1], *att_here, *att_there]
    )
    squares = jnp.sum(squares) + jnp.sum(g_up * g_up) + jnp.sum(g_down * g_down)
    grad_norm = jnp.sqrt(links.total(squares))
    grad_norm, output = sync(grad_norm, output)
    output_got = links.leave_group(output, "output")
    input_grad = come_home("input_grad_home", come, H, input_grad, input_grad_got, F32)
    output = come_home("output_home", come, H, output, output_got, BF)
    factor = jnp.minimum(1.0, clip_limit / (grad_norm + 1e-06))
    one_qkv, two_qkv, new_qkv = (
        v.transpose(1, 0, 2)
        for v in adam_update(
            g_qkv, *(v.transpose(1, 0, 2) for v in (m_qkv, v_qkv, w_qkv)), factor, learn_rate
        )
    )
    one_out, two_out, new_out = adam_update(g_out, m_out, v_out, w_out, factor, output_rate)
    one_up, two_up, new_up = adam_update(g_up, m_up, v_up, w_up, factor, learn_rate)
    one_down, two_down, new_down = adam_update(g_down, m_down, v_down, w_down, factor, learn_rate)
    return (
        output,
        input_grad,
        grad_norm,
        one_qkv,
        one_out,
        one_up,
        one_down,
        two_qkv,
        two_out,
        two_up,
        two_down,
        new_qkv,
        new_out,
        new_up,
        new_down,
    )


def solution(mesh):
    n_dp, n_mp = mesh.shape["dp"], mesh.shape["mp"]
    links = Links(n_dp, n_mp)
    fine = Mesh(mesh.devices.reshape(links.X, 2, links.H, 2, 2), links.axes)
    dp, mp = ("x", "core"), ("h", "p", "q")
    tokens, qkv = P(dp, mp, None), P(dp, None, mp)
    rows, columns = P(mp, dp), P(dp, mp)
    weights = (qkv, rows, columns, rows)
    return jax.shard_map(
        lambda *args: per_device(links, *args),
        mesh=fine,
        in_specs=(tokens, tokens, P(), P(dp), P(dp), P(dp)) + 3 * weights,
        out_specs=(tokens, tokens, P()) + 3 * weights,
        check_vma=False,
    )
```
